32 devices in a mesh: dp: 16 (over z, x, core), mp: 2 (over y).
Axes of the slice: x: 2, y: 2, z: 4, core: 2. Of those that a mesh axis runs over, the one named last changes fastest.
Arguments:
- tokens: bfloat16 [32768, 1536], P('dp'), may hold values from -6 to 6
- token_seq: int32 [32768], P('dp'), may hold values from -1 to 31, as said below
- w_z: bfloat16 [1536, 3072], P('dp', 'mp'), may hold values from -0.15625 to 0.15625
- w_xbc: bfloat16 [1536, 3328], P('dp', 'mp'), may hold values from -0.15625 to 0.15625
- w_dt: bfloat16 [1536, 48], P('dp', 'mp'), may hold values from -0.078125 to 0.078125
- w_out: bfloat16 [3072, 1536], P('mp', 'dp'), may hold values from -0.109375 to 0.109375
- conv_w: bfloat16 [4, 3328], P(None, ('mp', 'dp')), may hold values from -3 to 3
- conv_b: bfloat16 [3328], P(('mp', 'dp')), may hold values from -3 to 3
- gate_gain: bfloat16 [3072], P(('mp', 'dp')), may hold values from 0.099609375 to 1.8984375
- norm_gain: bfloat16 [1536], P(('dp', 'mp')), may hold values from 0.099609375 to 1.8984375
- a_log: float32 [48], P('mp'), may hold values from -3 to 1.5
- d_skip: float32 [48], P('mp'), may hold values from 0.5 to 2
- dt_bias: float32 [48], P('mp'), may hold values from -6 to -2
- d_out: bfloat16 [32768, 1536], P('dp', 'mp'), may hold values from -6 to 6
Outputs:
- layer_out: bfloat16 [32768, 1536], P('dp', 'mp')
- d_tokens: float32 [32768, 1536], P('dp')
- grad_w_z: float32 [1536, 3072], P('dp', 'mp')
- grad_w_xbc: float32 [1536, 3328], P('dp', 'mp')
- grad_w_dt: float32 [1536, 48], P('dp', 'mp')
- grad_w_out: float32 [3072, 1536], P('mp', 'dp')
- grad_conv_w: float32 [4, 3328], P(None, ('mp', 'dp'))
- grad_conv_b: float32 [3328], P(('mp', 'dp'))
- grad_gate_gain: float32 [3072], P(('mp', 'dp'))
- grad_norm_gain: float32 [1536], P(('dp', 'mp'))
- grad_a_log: float32 [48], P('mp')
- grad_d_skip: float32 [48], P('mp')
- grad_dt_bias: float32 [48], P('mp')
The draws below stay inside these ranges and needn't reach their ends.
Inputs may be any that keep to these rules, and one draw needn't show every extreme that they name: `token_seq`: each block of 2048 rows holds one or two sequences, each on consecutive rows from the block's first row, followed by unused rows of id -1; ids are unique over all blocks; every block uses at least half of its rows, and in every draw some block holds a single sequence of 2048 rows.
All inputs are finite; a program needn't handle non-finite values.
Results may differ from the reference program's by a relative error of at most 0.012.
Values may be sent and summed in bfloat16 or wider, within the bound.
No kernel may reach another device: no remote copies, remote signals or barrier semaphores. Data moves between devices by JAX's collectives and lax.ppermute only.
A program may use at most 320 MiB of HBM per device.

```python
import jax
import jax.numpy as jnp
from jax import lax

D = 1536
HEADS = 48
STATE = 128
KERNEL = 4
SPAN = 256
TOK_DEV = 2048
INNER = 3072
TOKENS = 32768
N_DP = 16


def draw_token_seq(key, part):
    key = jax.random.fold_in(key, 7)
    first_key, second_key, third_key = jax.random.split(key, 3)
    device_count = TOKENS // TOK_DEV
    filled = jax.random.randint(first_key, (device_count,), TOK_DEV // 2, TOK_DEV + 1)
    fullest = jax.random.randint(third_key, (), 0, device_count)
    devices = jnp.arange(device_count)
    filled = jnp.where(devices == fullest, TOK_DEV, filled)
    offsets = jax.random.randint(second_key, (device_count,), 0, 1 << 20)
    cuts = filled // 4 + offsets % (filled - filled // 4 + 1)
    cuts = jnp.where(devices == fullest, TOK_DEV, cuts)
    position = jnp.arange(TOK_DEV)[None, :]
    labels = 2 * devices[:, None] + (position >= cuts[:, None]).astype(jnp.int32)
    return jnp.where(position >= filled[:, None], -1, labels).reshape(-1).astype(jnp.int32)


def with_spikes(values, key, source, target, blocks, factor):
    owner, partner = [(jnp.arange(values.shape[dim]) // (values.shape[dim] // blocks)).reshape([-1 if axis == dim else 1 for axis in range(values.ndim)]) for dim in (source, target)]
    chosen = jax.random.permutation(key, blocks)[partner]
    strong = (owner == chosen) | (owner == (partner + blocks // 2) % blocks)
    return jnp.where(strong, factor * values, values)


def steps_of(rng, shape, shards, least, largest):
    gain, own = 1.0, jax.random.fold_in(rng, 6)
    for dim, blocks in shards:
        steps = jnp.exp(jax.random.uniform(jax.random.fold_in(own, dim), (blocks,), jnp.float32, least / len(shards), largest / len(shards)))
        gain = gain * jnp.repeat(steps, shape[dim] // blocks).reshape([-1 if axis == dim else 1 for axis in range(len(shape))])
    return gain


def normal_values(key, shape, deviation, bound, cuts=(), kind=jnp.bfloat16):
    values = deviation * jax.random.normal(key, shape, jnp.float32)
    if cuts:
        values = values * steps_of(key, shape, cuts, -0.22, 0.18)
    return jnp.clip(values, -bound, bound).astype(kind)


def bell_draw_with(rng, shape, width, reach, cuts, heavy, held_as=jnp.bfloat16):
    values = width * jax.random.normal(rng, shape, jnp.float32)
    if cuts:
        values = values * steps_of(rng, shape, cuts, -0.22, 0.18)
    return jnp.clip(with_spikes(values, jax.random.fold_in(rng, 3), *heavy), -reach, reach).astype(held_as)


def setup_inputs(seed: int = 0) -> dict:
    streams_of = jax.random.split(jax.random.key(seed), 15)
    tokens = bell_draw_with(streams_of[0], (TOKENS, D), 1.0, 6.0, ((0, 16),), (0, 1, 16, 2.0))
    token_seq = draw_token_seq(jax.random.fold_in(streams_of[14], 71), 0)
    w_z = normal_values(streams_of[2], (D, INNER), D ** -0.5, 0.15625, ((0, 16), (1, 2)))
    w_xbc = normal_values(streams_of[3], (D, INNER + 2 * STATE), D ** -0.5, 0.15625, ((0, 16), (1, 2)))
    w_dt = normal_values(streams_of[4], (D, HEADS), (4 * D) ** -0.5, 0.078125, ((0, 16), (1, 2)))
    w_out = normal_values(streams_of[5], (INNER, D), INNER ** -0.5, 0.109375, ((0, 2), (1, 16)))
    conv_w = normal_values(streams_of[6], (KERNEL, INNER + 2 * STATE), KERNEL ** -0.5, 3.0, ((1, 32),))
    conv_b = normal_values(streams_of[7], (INNER + 2 * STATE,), 0.5, 3.0, ((0, 32),))
    gate_gain = jnp.clip(1.0 + 0.18 * jax.random.normal(streams_of[8], (INNER,), jnp.float32), 0.099609375, 1.8984375).astype(jnp.bfloat16)
    norm_gain = jnp.clip(1.0 + 0.18 * jax.random.normal(streams_of[9], (D,), jnp.float32), 0.099609375, 1.8984375).astype(jnp.bfloat16)
    a_log = jnp.clip(-3.0 + 4.5 * jax.random.uniform(streams_of[10], (HEADS,), jnp.float32) ** steps_of(streams_of[10], (HEADS,), ((0, 2),), -0.2, 0.2), -3.0, 1.5)
    d_skip = jnp.clip(0.5 + 1.5 * jax.random.uniform(streams_of[11], (HEADS,), jnp.float32) ** steps_of(streams_of[11], (HEADS,), ((0, 2),), -0.2, 0.2), 0.5, 2.0)
    dt_bias = jnp.clip(-6.0 + 4.0 * jax.random.uniform(streams_of[12], (HEADS,), jnp.float32) ** steps_of(streams_of[12], (HEADS,), ((0, 2),), -0.2, 0.2), -6.0, -2.0)
    d_out = bell_draw_with(streams_of[13], (TOKENS, D), 1.0, 6.0, ((0, 16), (1, 2)), (0, 1, 16, 2.0))
    return {"tokens": tokens, "token_seq": token_seq, "w_z": w_z, "w_xbc": w_xbc, "w_dt": w_dt, "w_out": w_out, "conv_w": conv_w, "conv_b": conv_b, "gate_gain": gate_gain, "norm_gain": norm_gain, "a_log": a_log, "d_skip": d_skip, "dt_bias": dt_bias, "d_out": d_out}


@jax.custom_vjp
def low(v):
    return lax.optimization_barrier(v.astype(jnp.bfloat16)).astype(jnp.float32)

@jax.custom_vjp
def low_back(v):
    return v

def low_keep(v):
    return (low(v), None)

def low_pass(kept, grad):
    return (grad,)

def back_keep(v):
    return (v, None)

def back_low(kept, grad):
    return (low(grad),)
low.defvjp(low_keep, low_pass)
low_back.defvjp(back_keep, back_low)
epsilon = 1e-05
highest = lax.Precision.HIGHEST

def matmul_high(left, right):
    return jnp.dot(left, right, precision=highest, preferred_element_type=jnp.float32)

def causal_conv(values, segment, kernel, bias_row):
    tap_count = kernel.shape[0]
    row_count = values.shape[0]
    padded = jnp.concatenate([jnp.zeros((tap_count - 1, values.shape[1]), values.dtype), values], 0)
    seg_padded = jnp.concatenate([jnp.full((tap_count - 1,), -3, jnp.int32), segment.astype(jnp.int32)], 0)
    summed = jnp.zeros_like(values) + bias_row[None, :]
    for offset in range(tap_count):
        matches = (seg_padded[offset:offset + row_count] == segment).astype(values.dtype)
        summed = summed + kernel[offset][None, :] * padded[offset:offset + row_count] * matches[:, None]
    return summed

def span_scan(x_heads, deltas, decay_rates, b_mat, c_mat, segment, span_len):
    token_count, head_count, head_dim = x_heads.shape
    block_count = token_count // span_len
    state_dim = b_mat.shape[1]
    causal_mask = jnp.arange(span_len)[:, None] >= jnp.arange(span_len)[None, :]

    def one_block(carried_value, pieces):
        state_now, prev_segment = carried_value
        x_block, dt_block, b_block, c_block, seg_block = pieces
        log_decay = jnp.cumsum(dt_block * decay_rates[None, :], axis=0)
        allowed = causal_mask & (seg_block[:, None] == seg_block[None, :])
        spread = log_decay[:, None, :] - log_decay[None, :, :]
        decays = jnp.exp(jnp.where(allowed[:, :, None], spread, -jnp.inf))
        scores = jnp.dot(c_block, b_block.T, precision=highest)
        mixing = decays * scores[:, :, None] * dt_block[None, :, :]
        within_block = jnp.einsum('ijh,jhp->ihp', mixing, x_block, precision=highest)
        carried_in = jnp.exp(log_decay) * (seg_block == prev_segment).astype(x_block.dtype)[:, None]
        from_state = jnp.einsum('in,hpn->ihp', c_block, state_now, precision=highest) * carried_in[:, :, None]
        last_segment = seg_block[-1]
        to_end = jnp.exp(log_decay[-1][None, :] - log_decay) * (seg_block == last_segment).astype(x_block.dtype)[:, None] * dt_block
        keep_factor = jnp.exp(log_decay[-1]) * (last_segment == prev_segment).astype(x_block.dtype)
        fresh_state = jnp.einsum('jh,jhp,jn->hpn', to_end, x_block, b_block, precision=highest)
        return ((state_now * keep_factor[:, None, None] + fresh_state, last_segment), within_block + from_state)
    initial = (jnp.zeros((head_count, head_dim, state_dim), x_heads.dtype), jnp.array(-2, jnp.int32))
    pieces = (x_heads.reshape(block_count, span_len, head_count, head_dim), deltas.reshape(block_count, span_len, head_count), b_mat.reshape(block_count, span_len, state_dim), c_mat.reshape(block_count, span_len, state_dim), segment.reshape(block_count, span_len))
    _, scanned = lax.scan(jax.checkpoint(one_block), initial, pieces)
    return scanned.reshape(token_count, head_count * head_dim)

def ssd_heads(x_flat, b_mat, c_mat, dt_raw, a_log, dt_bias, d_skip, segment, span_len):
    head_count = dt_raw.shape[1]
    x_heads = x_flat.reshape(x_flat.shape[0], head_count, -1)
    deltas = jax.nn.softplus(dt_raw + dt_bias[None, :])
    decay_rates = -jnp.exp(a_log)
    scanned = span_scan(x_heads, deltas, decay_rates, b_mat, c_mat, segment, span_len)
    return scanned + (d_skip[None, :, None] * x_heads).reshape(x_flat.shape)

def mixer_block(residual, segment, w_z, w_xbc, w_dt, w_out, conv_w, conv_b, gate_gain, norm_gain, a_log, d_skip, dt_bias):
    scaled_in = residual * lax.rsqrt(lax.optimization_barrier(jnp.mean(residual * residual, axis=1, keepdims=True)) + epsilon)
    normed = low(scaled_in * norm_gain[None, :])
    gate_in = low_back(matmul_high(normed, w_z))
    projected = low_back(matmul_high(normed, w_xbc))
    dt_raw = low_back(matmul_high(normed, w_dt))
    conved = low(jax.nn.silu(causal_conv(projected, segment, conv_w, conv_b)))
    inner_half = INNER // 2
    x_all = jnp.concatenate([conved[:, :inner_half], conved[:, inner_half + STATE:2 * inner_half + STATE]], 1)
    b_mat = conved[:, inner_half:inner_half + STATE]
    c_mat = conved[:, 2 * inner_half + STATE:]
    mixed_out = ssd_heads(x_all, b_mat, c_mat, dt_raw, a_log, dt_bias, d_skip, segment, SPAN)
    gated_out = mixed_out * jax.nn.silu(gate_in)
    gated_unit = gated_out * lax.rsqrt(lax.optimization_barrier(jnp.mean(gated_out * gated_out, axis=1, keepdims=True)) + epsilon)
    out_normed = low(gated_unit * gate_gain[None, :])
    branch = matmul_high(out_normed, w_out)
    live_rows = (segment >= 0).astype(residual.dtype)[:, None]
    return residual + live_rows * branch

def reference(tokens, token_seq, w_z, w_xbc, w_dt, w_out, conv_w, conv_b, gate_gain, norm_gain, a_log, d_skip, dt_bias, d_out):
    weights = tuple((weight_item.astype(jnp.float32) for weight_item in (w_z, w_xbc, w_dt, w_out, conv_w, conv_b, gate_gain, norm_gain, a_log, d_skip, dt_bias)))
    seg_blocks = token_seq.reshape(N_DP, TOK_DEV)

    def forward(residual, *params):

        def step_block(carried_value, pieces):
            return (carried_value, jax.checkpoint(mixer_block)(pieces[0], pieces[1], *params))
        _, outputs = lax.scan(step_block, jnp.zeros((), jnp.float32), (residual.reshape(N_DP, TOK_DEV, D), seg_blocks))
        return outputs.reshape(N_DP * TOK_DEV, D)
    result, pullback = jax.vjp(forward, tokens.astype(jnp.float32), *weights)
    gradients = pullback(d_out.astype(jnp.float32))
    return (result.astype(jnp.bfloat16), gradients[0], gradients[1], gradients[2], gradients[3], gradients[4], gradients[5], gradients[6], gradients[7], gradients[8], gradients[9], gradients[10], gradients[11])
```

```python
import functools

import jax
import jax.numpy as jnp
from jax import lax
from jax.experimental import pallas as pl
from jax.experimental.pallas import tpu as pltpu
from jax.sharding import PartitionSpec as P

F32 = jnp.float32
BF16 = jnp.bfloat16
EPS = 1e-05
LOG2E = 1.4426950408889634
CAP = 60.0
Q = 128
HALO = 128
VMEM = 60 * 1024 * 1024


def dot(a, b, ca, cb, precision=None):
    return lax.dot_general(
        a, b, (((ca,), (cb,)), ((), ())), precision=precision, preferred_element_type=F32
    )


def xor_perm(count, bits):
    return [(i, i ^ bits) for i in range(count)]


def line_perm(pairs):
    return [(a * 4 + r, b * 4 + r) for a, b in pairs for r in range(4)]


ENDS_IN = ((1, 0), (2, 3))
ENDS_OUT = ((0, 1), (3, 2))
MIDDLE = ((1, 2), (2, 1))
PAIRS = ((0, 1), (1, 0), (2, 3), (3, 2))
SWAP = [(0, 1), (1, 0)]


def send_line(a, pairs):
    return lax.ppermute(a, "dp", line_perm(pairs))


def send_x(a):
    return lax.ppermute(a, "dp", xor_perm(16, 2))


def send_core(a):
    return lax.ppermute(a, "dp", xor_perm(16, 1))


def send_y(a):
    return lax.ppermute(a, "mp", SWAP)


def place_kernel(where, me_ref, *refs):
    pieces, out_ref, held, arrived, left = refs[:-4], refs[-4], refs[-3], refs[-2], refs[-1]
    me, my = me_ref[0], me_ref[1]
    inward, outward = [], []
    for piece, parts in zip(pieces, where):
        for k, (ry, rest) in enumerate(parts):
            n = len(inward)
            slot = out_ref.at[jnp.bitwise_xor(my, ry), jnp.bitwise_xor(me, rest)]
            inward.append(pltpu.make_async_copy(piece.at[k], held.at[n], arrived.at[n]))
            outward.append(pltpu.make_async_copy(held.at[n], slot, left.at[n]))
    for copy in inward:
        copy.start()
    for copy, further in zip(inward, outward):
        copy.wait()
        further.start()
    for copy in outward:
        copy.wait()


def place(pieces, where, me, my):
    rows, width = pieces[0].shape[1:]
    return pl.pallas_call(
        functools.partial(place_kernel, where),
        out_shape=jax.ShapeDtypeStruct((2, 16, rows, width), pieces[0].dtype),
        in_specs=[pl.BlockSpec(memory_space=pltpu.SMEM)]
        + [pl.BlockSpec(memory_space=pl.ANY)] * len(pieces),
        out_specs=pl.BlockSpec(memory_space=pl.ANY),
        scratch_shapes=[
            pltpu.VMEM((32, rows, width), pieces[0].dtype),
            pltpu.SemaphoreType.DMA((32,)),
            pltpu.SemaphoreType.DMA((32,)),
        ],
        compiler_params=pltpu.CompilerParams(vmem_limit_bytes=VMEM),
    )(jnp.stack([me, my]).astype(jnp.int32), *pieces)


def tie(*values):
    return lax.optimization_barrier(values)


def gather_now(shard):
    me, my = lax.axis_index("dp"), lax.axis_index("mp")
    near = send_line(shard, PAIRS)
    far_mid = send_line(shard, MIDDLE)
    first = jnp.stack([shard, near])
    first_x, first_y = send_x(first), send_y(first)
    across_end = send_line(far_mid, ENDS_IN)
    across_mid = send_line(near, MIDDLE)
    far_end = send_line(across_mid, ENDS_IN)
    second = jnp.stack([across_end + across_mid, far_mid + far_end])
    second_x, second_y = send_x(second), send_y(second)
    first_xy = send_y(first_x)
    second_xy = send_x(second_y)
    pieces, where = [], []
    for k, part in enumerate((first, first_x, first_y, first_xy, second, second_x, second_y, second_xy)):
        for rc, piece in enumerate((part, send_core(part))):
            pieces.append(piece)
            side, pair = k % 4, k // 4
            where.append([(side // 2, (2 * pair + low) * 4 + (side % 2) * 2 + rc) for low in range(2)])
    return place(pieces, where, me, my), (first_xy, second_y)


def swap(a):
    return lax.ppermute(a, "mp", SWAP)


def gather_later(shard, marks):
    my = lax.axis_index("mp")
    if marks:
        shard = tie(shard, *marks)[0]
    other = swap(shard)
    pair = jnp.where(my == 0, jnp.stack([shard, other]), jnp.stack([other, shard]))
    return lax.all_gather(pair, "dp", axis=1, tiled=True)


class Flow:
    def __init__(self, steps=None, result=None):
        self.steps, self.result = steps, result
        self.sent, self.flying = [], []
        if steps is not None:
            self.sent, self.flying = next(steps)

    def move(self, got):
        try:
            self.sent, self.flying = self.steps.send(list(got))
        except StopIteration as stop:
            self.result = stop.value

    def finish(self):
        while self.result is None:
            self.move(self.flying)
        return self.result


def once(sent, send):
    def steps():
        (got,) = yield [sent], [send(sent)]
        return got

    return Flow(steps())


def ahead(value, *flows):
    sent = sum([f.sent for f in flows if f.result is None], [])
    return tie(value, *sent)[0] if sent else value


def after(value, *flows):
    live = [f for f in flows if f.result is None]
    if live:
        value, *got = tie(value, *sum([f.flying for f in live], []))
        for f in live:
            count = len(f.flying)
            part, got = got[:count], got[count:]
            f.move(part)
    return value


def add(a, b):
    return (a.astype(F32) + b.astype(F32)).astype(a.dtype)


def pick(a, index, axis):
    return lax.dynamic_index_in_dim(a, index, axis, keepdims=False)


def line_steps(a, z):
    block = [pick(a, jnp.bitwise_xor(z, r), 0) for r in range(4)]
    got, out = yield [block[3], block[2]], [send_line(block[3], ENDS_OUT), send_line(block[2], ENDS_OUT)]
    into_near, far = add(block[2], got), add(block[3], out)
    got, out = yield [into_near, far], [send_line(into_near, MIDDLE), send_line(far, MIDDLE)]
    near, mine = add(block[1], got), add(block[0], out)
    (got,) = yield [near], [send_line(near, PAIRS)]
    return add(mine, got)


def halve_step(a, axis, bit, send):
    sent = pick(a, 1 - bit, axis)
    return pick(a, bit, axis), sent, send(sent)


def both(first, second):
    flows = [first, second]
    state = [next(f) for f in flows]
    results = [None, None]
    while any(v is not None for v in state):
        live = [k for k in (0, 1) if state[k] is not None]
        got = yield sum([list(state[k][0]) for k in live], []), sum([list(state[k][1]) for k in live], [])
        at = 0
        for k in live:
            count = len(state[k][1])
            part, at = got[at : at + count], at + count
            try:
                state[k] = flows[k].send(part)
            except StopIteration as stop:
                results[k], state[k] = stop.value, None
    return results


def stages(a, order, my, z, x):
    names = ["y", "z", "x"]
    for name in order:
        axis = names.index(name)
        names.remove(name)
        if name == "z":
            a = yield from line_steps(jnp.moveaxis(a, axis, 0), z)
        else:
            bit, send = (my, send_y) if name == "y" else (x, send_x)
            keep, sent, flying = halve_step(a, axis, bit, send)
            (got,) = yield [sent], [flying]
            a = add(keep, got)
    return a


def scatter_steps(keep, sent, orders):
    rows, width = keep.shape[2:]
    me, my = lax.axis_index("dp"), lax.axis_index("mp")
    z, x = me // 4, (me // 2) % 2
    (got,) = yield [sent], [send_core(sent)]
    a = add(keep, got).reshape(2, 4, 2, rows, width)
    cut = width // 256 * 128
    first, second = yield from both(
        stages(a[..., :cut], orders[0], my, z, x), stages(a[..., cut:], orders[1], my, z, x)
    )
    return jnp.concatenate([first, second], 1)


def sum_to_owners(keep, sent, count, orders=("xyz", "yxz")):
    if count == 16:
        return Flow(scatter_steps(keep, sent, orders))
    core = lax.axis_index("dp") % 2
    pair = jnp.stack([keep, sent], 2)
    grad = jnp.where(core == 0, pair, pair[:, :, ::-1])
    mine = lax.psum_scatter(grad, "mp", scatter_dimension=0, tiled=False)
    mine = mine.reshape((-1,) + keep.shape[2:])
    return Flow(result=lax.psum_scatter(mine, "dp", scatter_dimension=0, tiled=False))


def total_steps(a):
    for send in (send_core, send_x, send_y, lambda v: send_line(v, PAIRS)):
        (got,) = yield [a], [send(a)]
        a = a + got
    (far,) = yield [a], [send_line(a, MIDDLE)]
    (further,) = yield [far], [send_line(far, ENDS_IN)]
    return a + far + further


def total(a, count):
    if count == 16:
        return Flow(total_steps(a))
    return Flow(result=lax.psum(a, ("dp", "mp")))


def sigmoid(v):
    return 0.5 * jnp.tanh(0.5 * v) + 0.5


def mask_kernel(place_ref, seg_ref, conv_ref, scan_ref, own_ref):
    seg = jnp.broadcast_to(seg_ref[...].astype(F32), (8, seg_ref.shape[1]))
    total = seg.shape[1]
    own = total // 2
    first = place_ref[0] == 0
    lane = lax.broadcasted_iota(jnp.int32, seg.shape, 1)
    conv_ref[...] = jnp.zeros_like(conv_ref)
    for k in (1, 2, 3):
        same = jnp.where((lane >= k) & (pltpu.roll(seg, k, 1) == seg), 1.0, 0.0)
        conv_ref[k - 1 : k, :own] = jnp.where(first, same[:1, :own], same[:1, own:])
        conv_ref[k - 1 : k, own:] = jnp.where(first, same[:1, own : own + HALO], 0.0)
    mine = jnp.where(first, seg[:1, :own], seg[:1, own:])
    own_ref[...] = mine
    outside = jnp.where(first, -2.0, seg[:1, own - 1 : own])
    scan_ref[...] = jnp.zeros_like(scan_ref)
    before, final = outside, mine[:, own - 1 :]
    for c in range(own // Q):
        span = slice(c * Q, (c + 1) * Q)
        here = mine[:, span]
        last = here[:, Q - 1 :]
        flags = (here == before, here == last, jnp.broadcast_to(last, here.shape) == before, here == final, here == outside)
        for k, flag in enumerate(flags):
            scan_ref[k : k + 1, span] = jnp.where(flag, 1.0, 0.0)
        before = last


def row_masks(place_id, token_seq):
    total = token_seq.shape[0]
    own = total // 2
    return pl.pallas_call(
        mask_kernel,
        in_specs=[pl.BlockSpec(memory_space=pltpu.SMEM), pl.BlockSpec(memory_space=pltpu.VMEM)],
        out_shape=[
            jax.ShapeDtypeStruct((8, own + HALO), F32),
            jax.ShapeDtypeStruct((8, own), F32),
            jax.ShapeDtypeStruct((1, own), F32),
        ],
    )(place_id, token_seq[None, :])


def param_kernel(sizes, got_ref, w_ref, gain_ref, norm_ref, tall_ref, head_ref):
    per, gains, norms, heads, stride, skip = sizes
    count = got_ref.shape[1]
    w_ref[...] = jnp.zeros_like(w_ref)
    head_ref[...] = jnp.zeros_like(head_ref)
    norm_ref[...] = jnp.zeros_like(norm_ref)
    for y in range(2):
        for group in range(count // 8):
            tiles = [got_ref[y, group * 8 + d].astype(F32) for d in range(8)]
            turned = jnp.concatenate(tiles, 0).T
            for d in range(8):
                device = group * 8 + d
                at = y * stride + device * per
                for k in range(5):
                    column = turned[skip : skip + per, d * 16 + k : d * 16 + k + 1]
                    w_ref[at : at + per, k * Q : (k + 1) * Q] = jnp.broadcast_to(column, (per, Q))
                column = turned[skip : skip + gains, d * 16 + 5 : d * 16 + 6]
                at = (y * count + device) * gains
                gain_ref[at : at + gains, :] = jnp.broadcast_to(column, (gains, Q))
                at = 2 * device + y
                norm_ref[at : at + 1, :] = tiles[d][6:7]
                column = turned[skip : skip + norms, d * 16 + 6 : d * 16 + 7]
                tall_ref[at * norms : (at + 1) * norms, :] = jnp.broadcast_to(column, (norms, Q))
            if group == 0:
                column = turned[:, 7:8] + turned[:, 8:9] + turned[:, 9:10]
                for j in range(3):
                    head_ref[y * heads : (y + 1) * heads, j : j + 1] = column[skip + j * heads : skip + (j + 1) * heads]


def parameters(full, sizes):
    per, gains, norms, heads, stride, skip = sizes
    count = full.shape[1]
    wide, gain, norm, tall, head = pl.pallas_call(
        functools.partial(param_kernel, sizes),
        grid=(1,),
        in_specs=[pl.BlockSpec((2, count, 16, Q), lambda i: (0, 0, 0, stride // Q - 1))],
        out_specs=[
            pl.BlockSpec((2 * stride, 5 * Q), lambda i: (0, 0)),
            pl.BlockSpec((2 * count * gains, Q), lambda i: (0, 0)),
            pl.BlockSpec((2 * count, Q), lambda i: (0, 0)),
            pl.BlockSpec((2 * count * norms, Q), lambda i: (0, 0)),
            pl.BlockSpec((2 * heads, 8), lambda i: (0, 0)),
        ],
        out_shape=[
            jax.ShapeDtypeStruct((2 * stride, 5 * Q), F32),
            jax.ShapeDtypeStruct((2 * count * gains, Q), F32),
            jax.ShapeDtypeStruct((2 * count, Q), F32),
            jax.ShapeDtypeStruct((2 * count * norms, Q), F32),
            jax.ShapeDtypeStruct((2 * heads, 8), F32),
        ],
        compiler_params=pltpu.CompilerParams(vmem_limit_bytes=VMEM),
    )(full)
    return wide, gain, norm[:, skip : skip + norms].reshape(1, -1), tall, head


def norm_kernel(place_ref, x_ref, gain_ref, window_ref, own_ref):
    mine = pl.program_id(0) - place_ref[0]
    x = x_ref[...].astype(F32)
    scaled = x * lax.rsqrt(jnp.mean(x * x, axis=1, keepdims=True) + EPS)
    normed = (scaled.T * gain_ref[...]).astype(BF16)
    window_ref[...] = normed

    @pl.when((mine >= 0) & (mine < pl.num_programs(0) - 1))
    def _():
        own_ref[...] = normed


def normalise(place_id, tokens, gain):
    total, width = tokens.shape
    own = total // 2
    blocks = own // Q
    return pl.pallas_call(
        norm_kernel,
        grid_spec=pltpu.PrefetchScalarGridSpec(
            num_scalar_prefetch=1,
            grid=(blocks + 1,),
            in_specs=[
                pl.BlockSpec((Q, width), lambda i, place: (i + place[0] * (blocks - 1), 0)),
                pl.BlockSpec((width, Q), lambda i, place: (0, 0)),
            ],
            out_specs=[
                pl.BlockSpec((width, Q), lambda i, place: (0, i)),
                pl.BlockSpec((width, Q), lambda i, place: (0, jnp.clip(i - place[0], 0, blocks - 1))),
            ],
        ),
        out_shape=[
            jax.ShapeDtypeStruct((width, own + HALO), BF16),
            jax.ShapeDtypeStruct((width, own), BF16),
        ],
        compiler_params=pltpu.CompilerParams(vmem_limit_bytes=VMEM),
    )(place_id, tokens, gain)


def cotangent_kernel(place_ref, mine_ref, other_ref, seg_ref, all_ref, turned_ref):
    first = place_ref[0] == 0
    mine, other = mine_ref[...].astype(F32), other_ref[...].astype(F32)
    whole = jnp.concatenate([jnp.where(first, mine, other), jnp.where(first, other, mine)], 1)
    all_ref[...] = whole.astype(BF16)
    turned_ref[...] = (whole.T * jnp.where(seg_ref[...] >= 0.0, 1.0, 0.0)).astype(BF16)


def cotangents(place_id, d_out, other, seg):
    own, half = other.shape
    blocks = own // Q
    return pl.pallas_call(
        cotangent_kernel,
        grid_spec=pltpu.PrefetchScalarGridSpec(
            num_scalar_prefetch=1,
            grid=(blocks,),
            in_specs=[
                pl.BlockSpec((Q, half), lambda i, place: (i + place[0] * blocks, 0)),
                pl.BlockSpec((Q, half), lambda i, place: (i, 0)),
                pl.BlockSpec((1, Q), lambda i, place: (0, i)),
            ],
            out_specs=[
                pl.BlockSpec((Q, 2 * half), lambda i, place: (i, 0)),
                pl.BlockSpec((2 * half, Q), lambda i, place: (0, i)),
            ],
        ),
        out_shape=[
            jax.ShapeDtypeStruct((own, 2 * half), BF16),
            jax.ShapeDtypeStruct((2 * half, own), BF16),
        ],
        compiler_params=pltpu.CompilerParams(vmem_limit_bytes=VMEM),
    )(place_id, d_out, other, seg)


def finish_kernel(sizes, xbc_ref, z_ref, w_xbc_ref, w_dt_ref, w_z_ref, own_xbc_ref, own_dt_ref, own_z_ref, small_ref, product_ref):
    conv = w_xbc_ref.shape[1]
    heads = w_dt_ref.shape[1]
    xbc, z = xbc_ref[:, :conv].astype(F32), z_ref[...].astype(F32)
    last = xbc_ref[:, conv:].astype(F32)
    dt = last[:, :heads]
    own_xbc_ref[...] = xbc
    own_dt_ref[...] = dt
    own_z_ref[...] = z
    small_ref[...] = last[:16]
    product = jnp.sum(xbc * w_xbc_ref[...].astype(F32), axis=1, keepdims=True)
    product += jnp.sum(z * w_z_ref[...].astype(F32), axis=1, keepdims=True)
    product += jnp.sum(dt * w_dt_ref[...].astype(F32), axis=1, keepdims=True)
    product_ref[...] = jnp.broadcast_to(product, product_ref.shape)


def finish(sizes, own_xbc, own_z, w_xbc, w_dt, w_z):
    rows = w_z.shape[0]
    return pl.pallas_call(
        functools.partial(finish_kernel, sizes),
        out_shape=[
            jax.ShapeDtypeStruct(w_xbc.shape, F32),
            jax.ShapeDtypeStruct(w_dt.shape, F32),
            jax.ShapeDtypeStruct(w_z.shape, F32),
            jax.ShapeDtypeStruct((16, own_xbc.shape[1] - w_xbc.shape[1]), F32),
            jax.ShapeDtypeStruct((rows, Q), F32),
        ],
        compiler_params=pltpu.CompilerParams(vmem_limit_bytes=VMEM),
    )(own_xbc, own_z, w_xbc, w_dt, w_z)


def spare_kernel(sizes, conv_ref, gain_ref, out_ref):
    per, gains, norms, heads, stride, skip = sizes
    count = out_ref.shape[1]
    lane = lax.broadcasted_iota(jnp.int32, (1, Q), 1)

    def turned(v):
        return jnp.concatenate([v, jnp.zeros((Q - v.shape[0], Q), F32)], 0).T

    def moved(row, size):
        return jnp.where((lane >= skip) & (lane < skip + size), pltpu.roll(row, skip, 1), 0.0)

    for y in range(2):
        for d in range(count):
            at = y * stride + d * per
            rows = [moved(turned(conv_ref[at : at + per, :])[k : k + 1], per) for k in range(5)]
            at = (y * count + d) * gains
            total = jnp.sum(turned(gain_ref[at : at + gains, :]), axis=0, keepdims=True)
            rows += [moved(total, gains), jnp.zeros((10, Q), F32)]
            out_ref[y, d] = jnp.concatenate(rows, 0)


def spare_block(sizes, count, conv_sums, gain_grad):
    return pl.pallas_call(
        functools.partial(spare_kernel, sizes),
        out_shape=jax.ShapeDtypeStruct((2, count, 16, Q), F32),
        compiler_params=pltpu.CompilerParams(vmem_limit_bytes=VMEM),
    )(conv_sums, gain_grad)


def grad_kernel(core_ref, left_ref, right_ref, *refs):
    spare_ref = refs[0] if len(refs) == 4 else None
    keep_ref, send_ref, scr = refs[-3:]
    parts, rows, tile = scr.shape
    scr[...] = dot(left_ref[...], right_ref[...], 1, 1).astype(BF16).reshape(scr.shape)
    if spare_ref is not None:

        @pl.when(pl.program_id(1) == pl.num_programs(1) - 1)
        def _():
            for p in range(parts):
                old = scr[p, :16, tile - Q :].astype(F32)
                scr[p, :16, tile - Q :] = (old + spare_ref[0, p]).astype(BF16)

    core = core_ref[0]
    for p in range(parts // 2):
        keep_ref[0, p] = scr[2 * p + core]
        send_ref[0, p] = scr[2 * p + 1 - core]


def grad_plain_kernel(left_ref, right_ref, out_ref):
    out_ref[...] = dot(left_ref[...], right_ref[...], 1, 1).astype(BF16).reshape(out_ref.shape)


def weight_grad_sum(left, right, count):
    width, rows = left.shape
    channels = right.shape[0] // 2
    tile = 256
    grad = pl.pallas_call(
        grad_plain_kernel,
        grid=(2, channels // tile),
        in_specs=[
            pl.BlockSpec((width, rows), lambda y, k: (0, 0)),
            pl.BlockSpec((tile, rows), lambda y, k: (y * (channels // tile) + k, 0)),
        ],
        out_specs=pl.BlockSpec((count, 1, width // count, tile), lambda y, k: (0, y, 0, k)),
        out_shape=jax.ShapeDtypeStruct((count, 2, width // count, channels), BF16),
        compiler_params=pltpu.CompilerParams(vmem_limit_bytes=VMEM),
    )(left, right)
    return grad, lax.psum_scatter(
        grad.reshape(-1, channels), ("dp", "mp"), scatter_dimension=0, tiled=True
    )


def weight_grad(left, right, count, spare=None):
    width, rows = left.shape
    channels = right.shape[0] // 2
    tile = 256
    shape = (2, count // 2, width // count, channels)
    block = pl.BlockSpec((1, count // 2, width // count, tile), lambda y, k: (y, 0, 0, k))
    core = (lax.axis_index("dp") % 2).reshape(1).astype(jnp.int32)
    more = [] if spare is None else [pl.BlockSpec((1,) + spare.shape[1:], lambda y, k: (y, 0, 0, 0))]
    return pl.pallas_call(
        grad_kernel,
        grid=(2, channels // tile),
        in_specs=[
            pl.BlockSpec(memory_space=pltpu.SMEM),
            pl.BlockSpec((width, rows), lambda y, k: (0, 0)),
            pl.BlockSpec((tile, rows), lambda y, k: (y * (channels // tile) + k, 0)),
        ]
        + more,
        out_specs=[block, block],
        out_shape=[jax.ShapeDtypeStruct(shape, BF16)] * 2,
        scratch_shapes=[pltpu.VMEM((count, width // count, tile), BF16)],
        compiler_params=pltpu.CompilerParams(vmem_limit_bytes=VMEM),
    )(core, left, right, *([] if spare is None else [spare]))


def rows_kernel(raw_ref, head_ref, mask_ref, *outs):
    cum_ref, shift_ref, into_ref, onto_ref, keep_ref, step_ref, slope_ref, ratio_ref, start_ref, end_ref = outs
    chunks = raw_ref.shape[1] // Q
    rate = -jnp.exp(head_ref[:, 0:1])
    bias = head_ref[:, 1:2]
    source = lax.broadcasted_iota(jnp.int32, (Q, Q), 0)
    target = lax.broadcasted_iota(jnp.int32, (Q, Q), 1)
    upto = (source <= target).astype(F32)
    totals, sums, log_steps, steps = [], [], [], []
    for c in range(chunks):
        span = slice(c * Q, (c + 1) * Q)
        v = raw_ref[:, span] + bias
        tail = jnp.log1p(jnp.exp(-jnp.abs(v)))
        step = jnp.maximum(v, 0.0) + tail
        low = v < -20.0
        log_step = jnp.where(low, v, jnp.log(jnp.where(low, 1.0, step)))
        slope = 1.0 / (1.0 + jnp.exp(-v))
        decay = step * rate * LOG2E
        cum = dot(decay, upto, 1, 0, lax.Precision.HIGHEST)
        total = cum[:, Q - 1 : Q]
        shift = cum - log_step * LOG2E
        cum_ref[:, span] = cum
        shift_ref[:, span] = shift
        step_ref[:, span] = step
        slope_ref[:, span] = slope
        ratio_ref[:, span] = jnp.where(low, 1.0, slope / jnp.where(low, 1.0, step))
        into_ref[:, span] = jnp.exp2(cum) * mask_ref[0:1, span]
        onto_ref[:, span] = jnp.exp2(total - cum) * step * mask_ref[1:2, span]
        keep_ref[:, span] = jnp.exp2(total) * mask_ref[2:3, span]
        totals.append(total)
        sums.append(cum)
        steps.append(step)
    before = jnp.zeros_like(totals[0])
    for c in range(chunks):
        span = slice(c * Q, (c + 1) * Q)
        start_ref[:, span] = jnp.exp2(before + sums[c]) * mask_ref[4:5, span]
        before = before + totals[c]
    after = jnp.zeros_like(totals[0])
    for c in reversed(range(chunks)):
        span = slice(c * Q, (c + 1) * Q)
        end_ref[:, span] = jnp.exp2(after + totals[c] - sums[c]) * steps[c] * mask_ref[3:4, span]
        after = after + totals[c]


def head_rows(raw, heads, masks):
    shape = jax.ShapeDtypeStruct(raw.shape, F32)
    return pl.pallas_call(
        rows_kernel,
        out_shape=[shape] * 10,
        compiler_params=pltpu.CompilerParams(vmem_limit_bytes=VMEM),
    )(raw, heads, masks)


def wide_columns(w_ref, rows):
    return [w_ref[rows, k * Q : (k + 1) * Q] for k in range(5)]


def conv_kernel(place_ref, proj_ref, w_ref, mask_ref, end_ref, out_ref, pre_ref, state_ref, b_scr, x_scr):
    s = pl.program_id(0)
    channels, own = out_ref.shape
    at = pl.multiple_of(place_ref[0] * HALO, HALO)
    size = 64

    def strip(i, carry):
        rows = pl.ds(pl.multiple_of(i * size, size), size)
        wide = wide_columns(w_ref, rows)
        before = proj_ref[rows, pl.ds(pl.multiple_of(jnp.maximum(at - Q, 0), Q), Q)].astype(F32)
        lane = lax.broadcasted_iota(jnp.int32, (size, Q), 1)
        last = [pltpu.roll(before, k, 1) for k in (1, 2, 3)]
        weight = end_ref[pl.ds(jnp.maximum(s - 1, 0) * 4 + i, 1), :]
        for j in range(own // Q):
            now = proj_ref[rows, pl.ds(pl.multiple_of(at + j * Q, Q), Q)].astype(F32)
            span = slice(j * Q, (j + 1) * Q)
            pre = wide[4] + wide[3] * now
            for k in (1, 2, 3):
                rolled = pltpu.roll(now, k, 1)
                pre = pre + wide[3 - k] * (jnp.where(lane < k, last[k - 1], rolled) * mask_ref[k - 1 : k, span])
                last[k - 1] = rolled
            act = pre * sigmoid(pre)
            pre_ref[rows, span] = pre.astype(BF16)
            out_ref[rows, span] = act.astype(BF16)
            x_scr[rows, span] = (act * weight[:, span]).astype(BF16)
        return carry

    lax.fori_loop(0, channels // size, strip, 0)

    @pl.when(s == 0)
    def _():
        b_scr[...] = out_ref[:Q, :].astype(F32).T.astype(BF16)

    @pl.when((s > 0) & (s < pl.num_programs(0) - 1))
    def _():
        state_ref[...] = dot(x_scr[...], b_scr[...], 1, 0).astype(state_ref.dtype)


def conv_forward(place_id, proj, w_wide, masks, end_rows):
    channels, window = proj.shape
    own = window - HALO
    blocks = channels // 256
    half = blocks // 2

    def order(s):
        return jnp.where(s == 0, half - 1, jnp.where(s < half, s - 1, s))

    end_rows = jnp.pad(end_rows, ((0, 8), (0, 0)))
    return pl.pallas_call(
        conv_kernel,
        grid=(blocks,),
        in_specs=[
            pl.BlockSpec(memory_space=pltpu.SMEM),
            pl.BlockSpec((256, window), lambda s: (order(s), 0)),
            pl.BlockSpec((256, 5 * Q), lambda s: (order(s), 0)),
            pl.BlockSpec(masks.shape, lambda s: (0, 0)),
            pl.BlockSpec(end_rows.shape, lambda s: (0, 0)),
        ],
        out_specs=[
            pl.BlockSpec((256, own), lambda s: (order(s), 0)),
            pl.BlockSpec((256, own), lambda s: (order(s), 0)),
            pl.BlockSpec((256, Q), lambda s: (jnp.clip(s - 1, 0, blocks - 3), 0)),
        ],
        out_shape=[
            jax.ShapeDtypeStruct((channels, own), BF16),
            jax.ShapeDtypeStruct((channels, own), BF16),
            jax.ShapeDtypeStruct(((blocks - 2) * 256, Q), BF16),
        ],
        scratch_shapes=[pltpu.VMEM((own, Q), BF16), pltpu.VMEM((256, own), BF16)],
        compiler_params=pltpu.CompilerParams(vmem_limit_bytes=VMEM),
    )(place_id, proj, w_wide, masks, end_rows)


def chunk_scores(conv_ref, bc, seg_ref):
    inner_half, stride = bc
    b_t = conv_ref[inner_half : inner_half + Q, :]
    c_t = conv_ref[stride + inner_half : stride + inner_half + Q, :]
    b_m = b_t.astype(F32).T.astype(BF16)
    scores = dot(b_m, c_t, 1, 0)
    source = lax.broadcasted_iota(jnp.int32, (Q, Q), 0)
    target = lax.broadcasted_iota(jnp.int32, (Q, Q), 1)
    seg = jnp.broadcast_to(seg_ref[...], (Q, Q))
    allowed = (source <= target) & (seg.T == seg)
    return b_t, c_t, b_m, jnp.where(allowed, scores, 0.0), allowed


def columns_of(shift_ref, col_scr):
    heads = shift_ref.shape[0]
    padded = jnp.concatenate([shift_ref[...], jnp.zeros((Q - heads, Q), F32)], 0).T
    for g in range(heads // 8):
        col_scr[g] = padded[:, g * 8 : (g + 1) * 8]


def scan_kernel(
    bc, skip_ref, conv_ref, z_ref, cum_ref, shift_ref, into_ref, onto_ref, keep_ref, seg_ref,
    gain_ref, first_ref, out_ref, ssd_ref, scale_ref, states_ref, state, gated, col_scr,
):
    inner_half, stride = bc
    groups = 2 * inner_half // 512

    @pl.when(pl.program_id(0) == 0)
    def _():
        state[...] = first_ref[...].astype(F32)

    _, c_t, b_m, scores, _ = chunk_scores(conv_ref, bc, seg_ref)
    columns_of(shift_ref, col_scr)

    def group(g, squares):
        at = pl.multiple_of(g * 512, 512)
        x_at = pl.multiple_of(g * 512 + jnp.where(g >= groups // 2, stride - inner_half, 0), 256)
        held = state[pl.ds(at, 512), :].astype(BF16)
        states_ref[0, pl.ds(at, 512), :] = held
        from_state = dot(held, c_t, 1, 0)
        cols = col_scr[g]
        parts = []
        for k in range(8):
            h = g * 8 + k
            x = conv_ref[pl.ds(x_at + k * 64, 64), :]
            spread = jnp.minimum(cum_ref[pl.ds(h, 1), :] - cols[:, k : k + 1], CAP)
            mixing = (jnp.exp2(spread) * scores).astype(BF16)
            xf = x.astype(F32)
            y = dot(x, mixing, 1, 0) + from_state[k * 64 : (k + 1) * 64] * into_ref[pl.ds(h, 1), :] + skip_ref[h] * xf
            z = z_ref[pl.ds(at + k * 64, 64), :].astype(F32)
            g_out = y * (z * sigmoid(z))
            squares = squares + g_out * g_out
            ssd_ref[pl.ds(at + k * 64, 64), :] = y.astype(BF16)
            gated[pl.ds(at + k * 64, 64), :] = g_out
            parts.append((xf * onto_ref[pl.ds(h, 1), :]).astype(BF16))
        fresh = dot(jnp.concatenate(parts, 0), b_m, 1, 0)
        for k in range(8):
            rows = pl.ds(at + k * 64, 64)
            state[rows, :] = state[rows, :] * keep_ref[pl.ds(g * 8 + k, 1), :] + fresh[k * 64 : (k + 1) * 64]
        return squares

    squares = lax.fori_loop(0, groups, group, jnp.zeros((64, Q), F32))
    scale = lax.rsqrt(jnp.sum(squares, axis=0, keepdims=True) / (2 * inner_half) + EPS)
    scale_ref[...] = scale

    def finish(g, carry):
        rows = pl.ds(pl.multiple_of(g * 512, 512), 512)
        out_ref[rows, :] = (gated[rows, :] * scale * gain_ref[rows, :]).astype(BF16)
        return carry

    lax.fori_loop(0, groups, finish, 0)


def scan_forward(bc, skip, conv, z, rows, seg, gain, first):
    inner = 2 * bc[0]
    channels, own = conv.shape
    chunks = own // Q
    heads = inner // 64
    row_spec = pl.BlockSpec((heads, Q), lambda c: (0, c))
    whole = pl.BlockSpec((inner, Q), lambda c: (0, 0))
    tile = pl.BlockSpec((inner, Q), lambda c: (0, c))
    cum, shift, into, onto, keep = rows[:5]
    return pl.pallas_call(
        functools.partial(scan_kernel, bc),
        grid=(chunks,),
        in_specs=[
            pl.BlockSpec(memory_space=pltpu.SMEM),
            pl.BlockSpec((channels, Q), lambda c: (0, c)),
            tile,
            row_spec, row_spec, row_spec, row_spec, row_spec,
            pl.BlockSpec((1, Q), lambda c: (0, c)),
            whole, whole,
        ],
        out_specs=[tile, tile, pl.BlockSpec((1, Q), lambda c: (0, c)), pl.BlockSpec((1, inner, Q), lambda c: (c, 0, 0))],
        out_shape=[
            jax.ShapeDtypeStruct((inner, own), BF16),
            jax.ShapeDtypeStruct((inner, own), BF16),
            jax.ShapeDtypeStruct((1, own), F32),
            jax.ShapeDtypeStruct((chunks, inner, Q), BF16),
        ],
        scratch_shapes=[pltpu.VMEM((inner, Q), F32), pltpu.VMEM((inner, Q), F32), pltpu.VMEM((heads // 8, Q, 8), F32)],
        compiler_params=pltpu.CompilerParams(vmem_limit_bytes=VMEM),
    )(skip, conv, z, cum, shift, into, onto, keep, seg, gain, first)


def gate_back_kernel(
    d_unit_ref, ssd_ref, z_ref, scale_ref, gain_ref, start_ref, c_ref, d_ssd_ref, d_gate_ref, gain_grad_ref, first_grad_ref, into
):
    inner, width = ssd_ref.shape
    size = 64

    @pl.when(pl.program_id(0) == 0)
    def _():
        gain_grad_ref[...] = jnp.zeros_like(gain_grad_ref)
        first_grad_ref[...] = jnp.zeros_like(first_grad_ref)

    scale = scale_ref[...]

    def gain_of(rows):
        return jnp.concatenate([gain_ref[rows, :]] * (width // Q), 1)

    def look(g, cross):
        rows = pl.ds(pl.multiple_of(g * size, size), size)
        z = z_ref[rows, :].astype(F32)
        unit = ssd_ref[rows, :].astype(F32) * (z * sigmoid(z)) * scale
        product = d_unit_ref[rows, :].astype(F32) * unit
        gain_grad_ref[rows, :] += sum(product[:, k * Q : (k + 1) * Q] for k in range(width // Q))
        product = product * gain_of(rows)
        return cross + jnp.sum(product.reshape(size // 8, 8, width), axis=0)

    cross = lax.fori_loop(0, inner // size, look, jnp.zeros((8, width), F32))
    cross = jnp.sum(cross, axis=0, keepdims=True) / inner

    def head(h, carry):
        rows = pl.ds(pl.multiple_of(h * size, size), size)
        z = z_ref[rows, :].astype(F32)
        ssd = ssd_ref[rows, :].astype(F32)
        sig = sigmoid(z)
        act = z * sig
        unit = ssd * act * scale
        d_gated = scale * (d_unit_ref[rows, :].astype(F32) * gain_of(rows) - unit * cross)
        d_ssd = d_gated * act
        d_ssd_ref[rows, :] = d_ssd.astype(BF16)
        d_gate_ref[rows, :] = (d_gated * ssd * (sig + act * (1.0 - sig))).astype(BF16)
        into[rows, :] = (d_ssd * start_ref[pl.ds(h, 1), :]).astype(BF16)
        return carry

    lax.fori_loop(0, inner // size, head, 0)
    c_m = c_ref[...].astype(F32).T.astype(BF16)

    def sums(g, carry):
        rows = pl.ds(pl.multiple_of(g * 512, 512), 512)
        first_grad_ref[rows, :] += dot(into[rows, :], c_m, 1, 0)
        return carry

    lax.fori_loop(0, inner // 512, sums, 0)


def gate_backward(bc, d_unit, ssd, z, scale, gain, start, conv):
    inner, own = ssd.shape
    heads = inner // 64
    width = 2 * Q
    tile = pl.BlockSpec((inner, width), lambda c: (0, c))
    whole = pl.BlockSpec((inner, Q), lambda c: (0, 0))
    c_block = (bc[0] + bc[1]) // Q
    return pl.pallas_call(
        gate_back_kernel,
        grid=(own // width,),
        in_specs=[
            tile, tile, tile,
            pl.BlockSpec((1, width), lambda c: (0, c)),
            whole,
            pl.BlockSpec((heads, width), lambda c: (0, c)),
            pl.BlockSpec((Q, width), lambda c: (c_block, c)),
        ],
        out_specs=[tile, tile, whole, whole],
        out_shape=[
            jax.ShapeDtypeStruct((inner, own), BF16),
            jax.ShapeDtypeStruct((inner, own), BF16),
            jax.ShapeDtypeStruct((inner, Q), F32),
            jax.ShapeDtypeStruct((inner, Q), F32),
        ],
        scratch_shapes=[pltpu.VMEM((inner, width), BF16)],
        compiler_params=pltpu.CompilerParams(vmem_limit_bytes=VMEM),
    )(d_unit, ssd, z, scale, gain, start, conv)


def scan_back_kernel(
    bc, skip_ref, conv_ref, d_ssd_ref, states_ref, last_ref, cum_ref, shift_ref, into_ref, onto_ref, keep_ref,
    step_ref, slope_ref, ratio_ref, seg_ref, head_ref,
    d_conv_ref, d_raw_ref, bias_grad_ref, rate_grad_ref, skip_grad_ref,
    grad, col_scr, row_scr, diag_scr, state_scr, hold_scr, y_scr, x_scr, dst_scr, dc_scr, db_scr,
):
    inner_half, stride = bc
    groups = 2 * inner_half // 512
    heads = 2 * inner_half // 64

    @pl.when(pl.program_id(0) == 0)
    def _():
        grad[...] = last_ref[...].astype(F32)
        bias_grad_ref[...] = jnp.zeros_like(bias_grad_ref)
        rate_grad_ref[...] = jnp.zeros_like(rate_grad_ref)
        skip_grad_ref[...] = jnp.zeros_like(skip_grad_ref)

    b_t, c_t, b_m, scores, allowed = chunk_scores(conv_ref, bc, seg_ref)
    c_m = c_t.astype(F32).T.astype(BF16)
    columns_of(shift_ref, col_scr)
    dst_scr[...] = jnp.zeros_like(dst_scr)
    dc_scr[...] = jnp.zeros_like(dc_scr)
    db_scr[...] = jnp.zeros_like(db_scr)

    def group(g, carry):
        at = pl.multiple_of(g * 512, 512)
        x_at = pl.multiple_of(g * 512 + jnp.where(g >= groups // 2, stride - inner_half, 0), 256)
        held = states_ref[0, pl.ds(at, 512), :]
        g_low = grad[pl.ds(at, 512), :].astype(BF16)
        from_state = dot(held, c_t, 1, 0)
        onto_state = dot(g_low, b_t, 1, 0)
        cols = col_scr[g]
        d_scores = jnp.zeros((Q, Q), F32)
        for k in range(8):
            h = g * 8 + k
            row = pl.ds(h, 1)
            span = slice(k * 64, (k + 1) * 64)
            x = conv_ref[pl.ds(x_at + k * 64, 64), :]
            dy = d_ssd_ref[pl.ds(at + k * 64, 64), :]
            xf, dyf = x.astype(F32), dy.astype(F32)
            decays = jnp.exp2(jnp.minimum(cum_ref[row, :] - cols[:, k : k + 1], CAP))
            mixing = (decays * scores).astype(BF16)
            d_scores = d_scores + decays * dot(x, dy, 0, 0)
            y = dot(x, mixing, 1, 0) + from_state[span] * into_ref[row, :]
            dx = dot(dy, mixing, 1, 1)
            dx_state = onto_state[span] * onto_ref[row, :]
            row_scr[row, :] = jnp.sum(dyf * y, axis=0, keepdims=True)
            diag_scr[row, :] = jnp.sum(xf * dx, axis=0, keepdims=True)
            state_scr[row, :] = jnp.sum(xf * dx_state, axis=0, keepdims=True)
            skip_grad_ref[row, :] += jnp.sum(xf * dyf, axis=0, keepdims=True)
            hold_scr[row, :] = jnp.sum(grad[pl.ds(at + k * 64, 64), :] * held[span].astype(F32), axis=0, keepdims=True)
            d_conv_ref[pl.ds(x_at + k * 64, 64), :] = (dx + dx_state + skip_ref[h] * dyf).astype(BF16)
            y_scr[span, :] = (dyf * into_ref[row, :]).astype(BF16)
            x_scr[span, :] = (xf * onto_ref[row, :]).astype(BF16)
        dst_scr[...] += d_scores
        fresh = dot(y_scr[...], c_m, 1, 0)
        dc_scr[...] += dot(held, y_scr[...], 0, 0)
        db_scr[...] += dot(g_low, x_scr[...], 0, 0)
        for k in range(8):
            rows = pl.ds(at + k * 64, 64)
            grad[rows, :] = grad[rows, :] * keep_ref[pl.ds(g * 8 + k, 1), :] + fresh[k * 64 : (k + 1) * 64]
        return carry

    lax.fori_loop(0, groups, group, 0)
    d_scores = jnp.where(allowed, dst_scr[...], 0.0).astype(BF16)
    zeros = jnp.zeros((stride - inner_half - Q, Q), BF16)
    d_conv_ref[inner_half : inner_half + Q, :] = (db_scr[...] + dot(c_t, d_scores, 1, 1)).astype(BF16)
    d_conv_ref[inner_half + Q : stride, :] = zeros
    d_conv_ref[stride + inner_half : stride + inner_half + Q, :] = (dc_scr[...] + dot(b_t, d_scores, 1, 0)).astype(BF16)
    d_conv_ref[stride + inner_half + Q :, :] = zeros

    source = lax.broadcasted_iota(jnp.int32, (Q, Q), 0)
    target = lax.broadcasted_iota(jnp.int32, (Q, Q), 1)
    since = (source >= target).astype(F32)
    columns = diag_scr[...] + state_scr[...]
    d_decay = dot(row_scr[...] - columns, since, 1, 0, lax.Precision.HIGHEST)
    d_decay = d_decay + jnp.sum(state_scr[...] + hold_scr[...] * keep_ref[...], axis=1, keepdims=True)
    rate = -jnp.exp(head_ref[:, 0:1])
    slope = slope_ref[...]
    d_raw = columns * ratio_ref[...] + rate * d_decay * slope
    bias_grad_ref[...] += d_raw
    rate_grad_ref[...] += step_ref[...] * d_decay * rate
    d_raw_ref[...] = jnp.zeros_like(d_raw_ref)
    d_raw_ref[0 : heads // 2, :] = d_raw[: heads // 2].astype(BF16)
    d_raw_ref[Q : Q + heads // 2, :] = d_raw[heads // 2 :].astype(BF16)


def scan_backward(bc, skip, conv, d_ssd, states, last, rows, seg, head_cols):
    inner = 2 * bc[0]
    channels, own = conv.shape
    chunks = own // Q
    heads = inner // 64
    end = chunks - 1
    row_spec = pl.BlockSpec((heads, Q), lambda c: (0, end - c))
    whole = pl.BlockSpec((inner, Q), lambda c: (0, 0))
    sums = pl.BlockSpec((heads, Q), lambda c: (0, 0))
    cum, shift, into, onto, keep, step, slope, ratio = rows[:8]
    small = jax.ShapeDtypeStruct((heads, Q), F32)
    row_buf = pltpu.VMEM((heads, Q), F32)
    square = pltpu.VMEM((Q, Q), F32)
    return pl.pallas_call(
        functools.partial(scan_back_kernel, bc),
        grid=(chunks,),
        in_specs=[
            pl.BlockSpec(memory_space=pltpu.SMEM),
            pl.BlockSpec((channels, Q), lambda c: (0, end - c)),
            pl.BlockSpec((inner, Q), lambda c: (0, end - c)),
            pl.BlockSpec((1, inner, Q), lambda c: (end - c, 0, 0)),
            whole,
        ]
        + [row_spec] * 8
        + [
            pl.BlockSpec((1, Q), lambda c: (0, end - c)),
            pl.BlockSpec(head_cols.shape, lambda c: (0, 0)),
        ],
        out_specs=[
            pl.BlockSpec((channels, Q), lambda c: (0, end - c)),
            pl.BlockSpec((2 * Q, Q), lambda c: (0, end - c)),
            sums, sums, sums,
        ],
        out_shape=[
            jax.ShapeDtypeStruct((channels, own), BF16),
            jax.ShapeDtypeStruct((2 * Q, own), BF16),
            small, small, small,
        ],
        scratch_shapes=[
            pltpu.VMEM((inner, Q), F32), pltpu.VMEM((heads // 8, Q, 8), F32),
            row_buf, row_buf, row_buf, row_buf,
            pltpu.VMEM((512, Q), BF16), pltpu.VMEM((512, Q), BF16),
            square, square, square,
        ],
        compiler_params=pltpu.CompilerParams(vmem_limit_bytes=VMEM),
    )(skip, conv, d_ssd, states, last, cum, shift, into, onto, keep, step, slope, ratio, seg, head_cols)


def conv_back_kernel(half, place_ref, proj_ref, pre_ref, d_ref, beyond_ref, raw_ref, w_ref, mask_ref, out_ref, sums_ref, acc):
    s = pl.program_id(0)
    channels, own = out_ref.shape
    tiles = own // Q
    at = pl.multiple_of(place_ref[0] * HALO, HALO)
    size = 32

    def strip(i, carry):
        rows = pl.ds(pl.multiple_of(i * size, size), size)
        wide = wide_columns(w_ref, rows)
        lane = lax.broadcasted_iota(jnp.int32, (size, Q), 1)
        sums = [jnp.zeros((size, Q), F32)] * 5
        kept, moved = None, None
        for j in range(tiles + 1):
            span = slice(j * Q, (j + 1) * Q)
            if j < tiles:
                pre = pre_ref[rows, span].astype(F32)
                sig = sigmoid(pre)
                d_pre = d_ref[rows, span].astype(F32) * (sig + pre * sig * (1.0 - sig))
            else:
                d_pre = beyond_ref[rows, :].astype(F32)
            back = [pltpu.roll(d_pre * mask_ref[k - 1 : k, span], Q - k, 1) for k in (1, 2, 3)]
            if j > 0:
                now = proj_ref[rows, pl.ds(pl.multiple_of(at + (j - 1) * Q, Q), Q)].astype(F32)
                shifted = [kept] + [jnp.where(lane < Q - k, moved[k - 1], back[k - 1]) for k in (1, 2, 3)]
                d_proj = wide[3] * kept
                for k in (1, 2, 3):
                    d_proj = d_proj + wide[3 - k] * shifted[k]
                for k in range(4):
                    sums[3 - k] = sums[3 - k] + now * shifted[k]
                out_ref[rows, (j - 1) * Q : j * Q] = d_proj.astype(BF16)
            if j < tiles:
                sums[4] = sums[4] + d_pre
            kept, moved = d_pre, back
        for k in range(5):
            acc[rows, k * Q : (k + 1) * Q] = sums[k]
        return carry

    lax.fori_loop(0, channels // size, strip, 0)
    rows_of = lax.broadcasted_iota(jnp.int32, (5 * Q, Q), 0) // Q
    column = lax.broadcasted_iota(jnp.int32, (5 * Q, Q), 1)
    ones = jnp.where(rows_of == column, 1.0, 0.0).astype(BF16)
    high = acc[...].astype(BF16)
    low = (acc[...] - high.astype(F32)).astype(BF16)
    sums_ref[...] = dot(high, ones, 1, 0) + dot(low, ones, 1, 0)

    @pl.when(lax.rem(s, half) == half - 1)
    def _():
        out_ref[Q:, :] = raw_ref[...]


def conv_backward(place_id, proj, pre, d_conv, beyond, d_raw, w_wide, masks):
    channels, window = proj.shape
    own = window - HALO
    blocks = channels // 256
    half = blocks // 2
    return pl.pallas_call(
        functools.partial(conv_back_kernel, half),
        grid=(blocks,),
        in_specs=[
            pl.BlockSpec(memory_space=pltpu.SMEM),
            pl.BlockSpec((256, window), lambda s: (s, 0)),
            pl.BlockSpec((256, own), lambda s: (s, 0)),
            pl.BlockSpec((256, own), lambda s: (s, 0)),
            pl.BlockSpec((256, HALO), lambda s: (s, 0)),
            pl.BlockSpec((Q, own), lambda s: (s // half, 0)),
            pl.BlockSpec((256, 5 * Q), lambda s: (s, 0)),
            pl.BlockSpec(masks.shape, lambda s: (0, 0)),
        ],
        out_specs=[pl.BlockSpec((256, own), lambda s: (s, 0)), pl.BlockSpec((256, Q), lambda s: (s, 0))],
        out_shape=[jax.ShapeDtypeStruct((channels, own), BF16), jax.ShapeDtypeStruct((channels, Q), F32)],
        scratch_shapes=[pltpu.VMEM((256, 5 * Q), F32)],
        compiler_params=pltpu.CompilerParams(vmem_limit_bytes=VMEM),
    )(place_id, proj, pre, d_conv, beyond, d_raw, w_wide, masks)


def shards(
    tokens, token_seq, w_z, w_xbc, w_dt, w_out, conv_w, conv_b, gate_gain, norm_gain, a_log, d_skip, dt_bias, d_out, *, count
):
    my = lax.axis_index("mp")
    all_rows, width = tokens.shape
    own = all_rows // 2
    window = own + HALO
    inner_half = w_z.shape[1]
    inner = 2 * inner_half
    conv_half = w_xbc.shape[1]
    state_dim = conv_half - inner_half
    heads_half = w_dt.shape[1]
    stride = -(-(conv_half + heads_half) // 256) * 256
    bc = (inner_half, stride)
    place_id = my.reshape(1).astype(jnp.int32)

    per, taps = conv_w.shape[1], conv_w.shape[0]
    shard_rows = w_dt.shape[0]
    spare = stride - conv_half - heads_half
    head_params = jnp.concatenate([a_log, dt_bias, d_skip])
    high = head_params.astype(BF16)
    middle = (head_params - high.astype(F32)).astype(BF16)
    low = (head_params - high.astype(F32) - middle.astype(F32)).astype(BF16)
    vectors = [*conv_w, conv_b, gate_gain, norm_gain, high, middle, low]
    block = jnp.stack([jnp.pad(v, (0, spare - v.shape[0])) for v in vectors])
    block = jnp.pad(block, ((0, shard_rows - len(vectors)), (0, 0)))
    shard_xbc = jnp.concatenate([w_xbc, w_dt, block], 1)
    sizes = (per, gate_gain.shape[0], norm_gain.shape[0], heads_half, stride, Q - spare)
    conv_masks, scan_masks, seg_row = row_masks(place_id, token_seq)

    if count == 16:
        full_xbc, marks = gather_now(shard_xbc)
    else:
        marks = ()
        full_xbc = gather_later(shard_xbc, marks).reshape(2, count, shard_rows, stride)
    full_z = gather_later(w_z, marks)
    full_out = gather_later(w_out.T, marks)
    w_wide, gain_wide, gain_in, gain_tall, head_cols = parameters(full_xbc, sizes)
    skip_all = head_cols[:, 2]
    full_xbc = full_xbc.reshape(2, width, stride)

    window_t, normed_t = normalise(place_id, tokens, gain_tall)
    proj = jnp.einsum("ydc,dt->yct", full_xbc, window_t, preferred_element_type=F32).astype(BF16)
    proj = proj.reshape(2 * stride, window)
    full_dt = full_xbc[:, :, conv_half : conv_half + heads_half]
    dt_raw = jnp.einsum("ydh,dt->yht", full_dt, normed_t, preferred_element_type=F32).reshape(2 * heads_half, own)
    rows = head_rows(dt_raw, head_cols, scan_masks)
    start_rows, end_rows = rows[8], rows[9]
    conved, pre, end_state = conv_forward(place_id, proj, w_wide, conv_masks, end_rows)
    state_flow = once(end_state, lambda a: lax.ppermute(a, "mp", [(0, 1)]))
    z = jnp.einsum("ydk,dt->ykt", full_z, ahead(normed_t, state_flow), preferred_element_type=F32).astype(BF16).reshape(inner, own)
    z = after(z, state_flow)
    d_flow = once(lax.dynamic_slice_in_dim(tie(d_out, proj)[0], (1 - my) * own, own, 0), swap)
    z = ahead(z, d_flow)
    out_normed, ssd, scale, states = scan_forward(
        bc, skip_all, conved, z, rows, seg_row, gain_wide, state_flow.result
    )
    out_normed = after(out_normed, d_flow)
    cotangent, cot_t = cotangents(place_id, d_out, d_flow.result, seg_row)
    grad_out, own_out = weight_grad_sum(cot_t, out_normed, count)
    out_ready = tie(out_normed, grad_out)[0]
    branch = jnp.einsum(
        "ykt,ydk->td", out_ready.reshape(2, inner_half, own), full_out, preferred_element_type=F32
    )
    first_half = my == 0
    live_rows = (lax.dynamic_slice_in_dim(token_seq, my * own, own, 0) >= 0)[:, None]
    tokens_own = lax.dynamic_slice_in_dim(tokens, my * own, own, 0).astype(F32)
    layer_rows = (tokens_own + jnp.where(live_rows, branch, 0.0)).astype(BF16)
    half_width = width // 2
    layer_mine = lax.dynamic_slice_in_dim(layer_rows, my * half_width, half_width, 1)
    layer_flow = once(lax.dynamic_slice_in_dim(layer_rows, (1 - my) * half_width, half_width, 1), swap)

    d_unit = jnp.einsum("ydk,dt->ykt", full_out, ahead(cot_t, layer_flow), preferred_element_type=F32).astype(BF16).reshape(inner, own)
    d_ssd, d_gate, gain_grad, first_grad = gate_backward(bc, d_unit, ssd, z, scale, gain_wide, start_rows, conved)
    d_gate = after(d_gate, layer_flow)
    layer_recv = layer_flow.result
    layer_out = jnp.where(
        first_half, jnp.concatenate([layer_mine, layer_recv], 0), jnp.concatenate([layer_recv, layer_mine], 0)
    )
    grad_flow = once(first_grad.astype(BF16), lambda a: lax.ppermute(a, "mp", [(1, 0)]))
    grad_z, own_z = weight_grad_sum(normed_t, ahead(d_gate, grad_flow), count)
    grad_z = after(grad_z, grad_flow)
    d_conv, d_raw, bias_grad, rate_grad, skip_grad = scan_backward(
        bc, skip_all, conved, tie(d_ssd, grad_z)[0], states, grad_flow.result, rows, seg_row, head_cols
    )
    head_grads = jnp.stack([jnp.sum(v, 1) for v in (rate_grad, skip_grad, bias_grad)])
    head_grads = jnp.pad(head_grads.reshape(1, -1), ((0, 7), (0, -head_grads.size % Q)))
    heads_flow = total(head_grads, count)
    first_pre = pre[:, :HALO].astype(F32)
    first_sig = sigmoid(first_pre)
    d_first = d_conv[:, :HALO].astype(F32) * (first_sig + first_pre * first_sig * (1.0 - first_sig))
    d_first = d_first.astype(BF16)
    beyond_flow = once(d_first, lambda a: lax.ppermute(a, "mp", [(1, 0)]))
    d_gate = ahead(d_gate, beyond_flow, heads_flow)
    d_normed_z = jnp.einsum("ykt,ydk->td", d_gate.reshape(2, inner_half, own), full_z, preferred_element_type=F32)
    d_normed_z = after(d_normed_z, beyond_flow, heads_flow)
    d_conv = ahead(tie(d_conv, d_normed_z, own_out)[0], heads_flow)
    d_proj, conv_sums = conv_backward(
        place_id, proj, pre, d_conv, beyond_flow.result, d_raw, w_wide, conv_masks
    )
    d_proj = after(d_proj, heads_flow)
    small = spare_block(sizes, count, conv_sums, gain_grad)
    keep_xbc, sent_xbc = weight_grad(ahead(normed_t, heads_flow), d_proj, count, small)
    keep_xbc = after(keep_xbc, heads_flow)
    sum_xbc = sum_to_owners(keep_xbc, sent_xbc, count, ("xzy", "zxy"))
    full_back = ahead(full_xbc, sum_xbc, heads_flow)
    d_normed = d_normed_z + jnp.einsum(
        "yct,ydc->td", d_proj.reshape(2, stride, own), full_back, preferred_element_type=F32
    )
    d_normed = after(d_normed, sum_xbc, heads_flow)
    inv_rms = lax.rsqrt(jnp.mean(tokens_own * tokens_own, 1, keepdims=True) + EPS)
    scaled_in = tokens_own * inv_rms
    d_scaled = d_normed * gain_in
    d_rows = cotangent.astype(F32) + inv_rms * (
        d_scaled - scaled_in * jnp.mean(d_scaled * scaled_in, 1, keepdims=True)
    )
    rows_flow = once(ahead(d_rows, sum_xbc).astype(BF16), swap)
    own_xbc = sum_xbc.finish()
    head_grads = heads_flow.finish().reshape(-1)[: 6 * heads_half]
    d_recv_rows = rows_flow.finish().astype(F32)
    d_tokens = jnp.where(
        first_half, jnp.concatenate([d_rows, d_recv_rows], 0), jnp.concatenate([d_recv_rows, d_rows], 0)
    )

    own_xbc, own_dt, own_z, own_small, product = finish(sizes, own_xbc, own_z, w_xbc, w_dt, w_z)
    own_out = own_out.astype(F32).T
    own_small = own_small[:, heads_half:]
    norms = norm_gain.shape[0]
    product = lax.dynamic_slice_in_dim(product[:, 0] + swap(product)[:, 0], my * norms, norms, 0)
    norm_mine = product / norm_gain.astype(F32)
    heads_mine = pick(head_grads.reshape(3, 2, heads_half), my, 1)
    return (
        layer_out,
        d_tokens,
        own_z,
        own_xbc,
        own_dt,
        own_out,
        own_small[:taps, :per],
        own_small[taps, :per],
        own_small[taps + 1, : gate_gain.shape[0]],
        norm_mine,
        heads_mine[0],
        heads_mine[1],
        heads_mine[2],
    )


def solution(mesh):
    placed = (
        P("dp", None),
        P("dp"),
        P("dp", "mp"),
        P("dp", "mp"),
        P("dp", "mp"),
        P("mp", "dp"),
        P(None, ("mp", "dp")),
        P(("mp", "dp")),
        P(("mp", "dp")),
        P(("dp", "mp")),
        P("mp"),
        P("mp"),
        P("mp"),
        P("dp", "mp"),
    )
    return jax.shard_map(
        functools.partial(shards, count=mesh.shape["dp"]),
        mesh=mesh,
        in_specs=placed,
        out_specs=(
            P("dp", "mp"),
            P("dp", None),
            P("dp", "mp"),
            P("dp", "mp"),
            P("dp", "mp"),
            P("mp", "dp"),
            P(None, ("mp", "dp")),
            P(("mp", "dp")),
            P(("mp", "dp")),
            P(("dp", "mp")),
            P("mp"),
            P("mp"),
            P("mp"),
        ),
        check_vma=False,
    )
```

```python
import functools

import jax
import jax.numpy as jnp
from jax import lax
from jax.experimental import pallas as pl
from jax.experimental.pallas import tpu as pltpu
from jax.sharding import PartitionSpec as P

F32 = jnp.float32
BF16 = jnp.bfloat16
EPS = 1e-05
LOG2E = 1.4426950408889634
CAP = 60.0
Q = 128
HALO = 128
VMEM = 60 * 1024 * 1024


def dot(a, b, ca, cb, precision=None):
    return lax.dot_general(
        a, b, (((ca,), (cb,)), ((), ())), precision=precision, preferred_element_type=F32
    )


def takes(micros):
    return pl.CostEstimate(flops=0, transcendentals=0, bytes_accessed=int(micros * 3.0e6))


def xor_perm(count, bits):
    return [(i, i ^ bits) for i in range(count)]


def line_perm(pairs):
    return [(a * 4 + r, b * 4 + r) for a, b in pairs for r in range(4)]


ENDS_IN = ((1, 0), (2, 3))
ENDS_OUT = ((0, 1), (3, 2))
MIDDLE = ((1, 2), (2, 1))
PAIRS = ((0, 1), (1, 0), (2, 3), (3, 2))
SWAP = [(0, 1), (1, 0)]


def send_line(a, pairs):
    return lax.ppermute(a, "dp", line_perm(pairs))


def send_x(a):
    return lax.ppermute(a, "dp", xor_perm(16, 2))


def send_core(a):
    return lax.ppermute(a, "dp", xor_perm(16, 1))


def send_y(a):
    return lax.ppermute(a, "mp", SWAP)


def place_kernel(where, me_ref, *refs):
    pieces, out_ref, held, arrived, left = refs[:-4], refs[-4], refs[-3], refs[-2], refs[-1]
    me, my = me_ref[0], me_ref[1]
    inward, outward = [], []
    for piece, parts in zip(pieces, where):
        for k, (ry, rest) in enumerate(parts):
            n = len(inward)
            slot = out_ref.at[jnp.bitwise_xor(my, ry), jnp.bitwise_xor(me, rest)]
            inward.append(pltpu.make_async_copy(piece.at[k], held.at[n], arrived.at[n]))
            outward.append(pltpu.make_async_copy(held.at[n], slot, left.at[n]))
    for copy in inward:
        copy.start()
    for copy, further in zip(inward, outward):
        copy.wait()
        further.start()
    for copy in outward:
        copy.wait()


def place(pieces, where, me, my):
    rows, width = pieces[0].shape[1:]
    return pl.pallas_call(
        functools.partial(place_kernel, where),
        cost_estimate=takes(9),
        out_shape=jax.ShapeDtypeStruct((2, 16, rows, width), pieces[0].dtype),
        in_specs=[pl.BlockSpec(memory_space=pltpu.SMEM)]
        + [pl.BlockSpec(memory_space=pl.ANY)] * len(pieces),
        out_specs=pl.BlockSpec(memory_space=pl.ANY),
        scratch_shapes=[
            pltpu.VMEM((32, rows, width), pieces[0].dtype),
            pltpu.SemaphoreType.DMA((32,)),
            pltpu.SemaphoreType.DMA((32,)),
        ],
        compiler_params=pltpu.CompilerParams(vmem_limit_bytes=VMEM),
    )(jnp.stack([me, my]).astype(jnp.int32), *pieces)


def tie(*values):
    return lax.optimization_barrier(values)


def gather_now(shard, small, prepare, normalised):
    me, my = lax.axis_index("dp"), lax.axis_index("mp")
    near = send_line(shard, PAIRS)
    far_mid = send_line(shard, MIDDLE)
    small = small[None]
    for send in (send_x, send_core, send_y):
        small = jnp.concatenate([small, send(small)], 0)
    first = jnp.stack([shard, near])
    first_x, first_y = send_x(first), send_y(first)
    small, far_mid, near = tie(small, far_mid, near)
    across_end = send_line(far_mid, ENDS_IN)
    across_mid = send_line(near, MIDDLE)
    small_near, small_far = send_line(small, PAIRS), send_line(small, MIDDLE)
    across_end, across_mid, small_near, small_far = tie(across_end, across_mid, small_near, small_far)
    far_end = send_line(across_mid, ENDS_IN)
    small_across_end, small_across = send_line(small_far, ENDS_IN), send_line(small_near, MIDDLE)
    second = jnp.stack([across_end + across_mid, far_mid + far_end])
    second, first_x, first_y, small_across_end, small_across = tie(
        second, first_x, first_y, small_across_end, small_across
    )
    second_x, second_y = send_x(second), send_y(second)
    small_far_end = send_line(small_across, ENDS_IN)
    early = [first, first_x, first_y]
    early_core = [send_core(a) for a in early]
    small = jnp.concatenate([small, small_near, small_across_end + small_across, small_far + small_far_end], 0)
    prepared = prepare(small)
    second_x, second_y, first_x, second, *rest = tie(second_x, second_y, first_x, second, *early_core, *prepared)
    early_core, prepared = rest[:3], rest[3:]
    first_xy, second_xy = send_y(first_x), send_x(second_y)
    late = [second, second_x, second_y]
    late_core = [send_core(a) for a in late]
    rows = normalised(prepared)
    first_xy, second_xy, *rest = tie(first_xy, second_xy, *late_core, *rows)
    late_core, rows = rest[:3], rest[3:]
    last_core = [send_core(first_xy), send_core(second_xy)]
    pieces, where = [], []
    for own, other, pair, sides in (
        (early, early_core, 0, (0, 1, 2)),
        (late, late_core, 1, (0, 1, 2)),
        ([first_xy], last_core[:1], 0, (3,)),
        ([second_xy], last_core[1:], 1, (3,)),
    ):
        for rc, parts in enumerate((own, other)):
            pieces += parts
            where += [[(side // 2, (2 * pair + low) * 4 + (side % 2) * 2 + rc) for low in range(2)] for side in sides]
    return place(pieces, where, me, my), prepared, rows, (second_x, second_y)


def swap(a):
    return lax.ppermute(a, "mp", SWAP)


def gather_later(shard, marks):
    my = lax.axis_index("mp")
    other = swap(shard)
    pair = jnp.where(my == 0, jnp.stack([shard, other]), jnp.stack([other, shard]))
    if marks:
        pair = tie(pair, *marks)[0]
    return lax.all_gather(pair, "dp", axis=1, tiled=True)


class Flow:
    def __init__(self, steps=None, result=None):
        self.steps, self.result = steps, result
        self.sent, self.flying = [], []
        if steps is not None:
            self.sent, self.flying = next(steps)

    def move(self, got):
        try:
            self.sent, self.flying = self.steps.send(list(got))
        except StopIteration as stop:
            self.result = stop.value

    def finish(self):
        while self.result is None:
            self.move(self.flying)
        return self.result


def once(sent, send):
    def steps():
        (got,) = yield [sent], [send(sent)]
        return got

    return Flow(steps())


def ahead(value, *flows):
    sent = sum([f.sent for f in flows if f.result is None], [])
    return tie(value, *sent)[0] if sent else value


def after(value, *flows, also=()):
    live = [f for f in flows if f.result is None]
    if live:
        value, *got = tie(value, *sum([f.flying for f in live], []), *also)
        for f in live:
            count = len(f.flying)
            part, got = got[:count], got[count:]
            f.move(part)
    return value


def add(a, b):
    return (a.astype(F32) + b.astype(F32)).astype(a.dtype)


def pick(a, index, axis):
    return lax.dynamic_index_in_dim(a, index, axis, keepdims=False)


def line_steps(a, z):
    block = [pick(a, jnp.bitwise_xor(z, r), 0) for r in range(4)]
    got, out = yield [block[3], block[2]], [send_line(block[3], ENDS_OUT), send_line(block[2], ENDS_OUT)]
    into_near, far = add(block[2], got), add(block[3], out)
    got, out = yield [into_near, far], [send_line(into_near, MIDDLE), send_line(far, MIDDLE)]
    near, mine = add(block[1], got), add(block[0], out)
    (got,) = yield [near], [send_line(near, PAIRS)]
    return add(mine, got)


def halve_step(a, axis, bit, send):
    sent = pick(a, 1 - bit, axis)
    return pick(a, bit, axis), sent, send(sent)


def stages(a, order, my, z, x):
    names = ["y", "z", "x"]
    for name in order:
        axis = names.index(name)
        names.remove(name)
        if name == "z":
            a = yield from line_steps(jnp.moveaxis(a, axis, 0), z)
        else:
            bit, send = (my, send_y) if name == "y" else (x, send_x)
            keep, sent, flying = halve_step(a, axis, bit, send)
            (got,) = yield [sent], [flying]
            a = add(keep, got)
    return a


def scatter_steps(keep, sent, order):
    rows, width = keep.shape[2:]
    me, my = lax.axis_index("dp"), lax.axis_index("mp")
    z, x = me // 4, (me // 2) % 2
    (got,) = yield [sent], [send_core(sent)]
    a = add(keep, got).reshape(2, 4, 2, rows, width)
    return (yield from stages(a, order, my, z, x))


def sum_to_owners(keep, sent, count, order):
    if count == 16:
        return Flow(scatter_steps(keep, sent, order))
    core = lax.axis_index("dp") % 2
    pair = jnp.stack([keep, sent], 2)
    grad = jnp.where(core == 0, pair, pair[:, :, ::-1])
    mine = lax.psum_scatter(grad, "mp", scatter_dimension=0, tiled=False)
    mine = mine.reshape((-1,) + keep.shape[2:])
    return Flow(result=lax.psum_scatter(mine, "dp", scatter_dimension=0, tiled=False))


def total_steps(a):
    for send in (send_core, send_x, send_y, lambda v: send_line(v, PAIRS)):
        (got,) = yield [a], [send(a)]
        a = a + got
    (far,) = yield [a], [send_line(a, MIDDLE)]
    (further,) = yield [far], [send_line(far, ENDS_IN)]
    return a + far + further


def total(a, count):
    if count == 16:
        return Flow(total_steps(a))
    return Flow(result=lax.psum(a, ("dp", "mp")))


def sigmoid(v):
    return 0.5 * jnp.tanh(0.5 * v) + 0.5


def mask_kernel(place_ref, seg_ref, conv_ref, scan_ref, own_ref):
    seg = jnp.broadcast_to(seg_ref[...].astype(F32), (8, seg_ref.shape[1]))
    total = seg.shape[1]
    own = total // 2
    first = place_ref[0] == 0
    lane = lax.broadcasted_iota(jnp.int32, seg.shape, 1)
    conv_ref[...] = jnp.zeros_like(conv_ref)
    for k in (1, 2, 3):
        same = jnp.where((lane >= k) & (pltpu.roll(seg, k, 1) == seg), 1.0, 0.0)
        conv_ref[k - 1 : k, :own] = jnp.where(first, same[:1, :own], same[:1, own:])
        conv_ref[k - 1 : k, own:] = jnp.where(first, same[:1, own : own + HALO], 0.0)
    mine = jnp.where(first, seg[:1, :own], seg[:1, own:])
    own_ref[...] = mine
    outside = jnp.where(first, -2.0, seg[:1, own - 1 : own])
    scan_ref[...] = jnp.zeros_like(scan_ref)
    before, final = outside, mine[:, own - 1 :]
    for c in range(own // Q):
        span = slice(c * Q, (c + 1) * Q)
        here = mine[:, span]
        last = here[:, Q - 1 :]
        flags = (here == before, here == last, jnp.broadcast_to(last, here.shape) == before, here == final, here == outside)
        for k, flag in enumerate(flags):
            scan_ref[k : k + 1, span] = jnp.where(flag, 1.0, 0.0)
        before = last


def row_masks(place_id, token_seq):
    total = token_seq.shape[0]
    own = total // 2
    return pl.pallas_call(
        mask_kernel,
        cost_estimate=takes(2),
        in_specs=[pl.BlockSpec(memory_space=pltpu.SMEM), pl.BlockSpec(memory_space=pltpu.VMEM)],
        out_shape=[
            jax.ShapeDtypeStruct((8, own + HALO), F32),
            jax.ShapeDtypeStruct((8, own), F32),
            jax.ShapeDtypeStruct((1, own), F32),
        ],
    )(place_id, token_seq[None, :])


def param_kernel(sizes, by_distance, me_ref, got_ref, w_ref, gain_ref, norm_ref, tall_ref, head_ref, scr):
    per, gains, norms, heads, stride = sizes
    count = got_ref.shape[0] // 2
    me, my = me_ref[0], me_ref[1]
    for r in range(2 * count):
        if by_distance:
            rz, ry, rest = r // 8, (r // 4) % 2, (r // 2) % 2 + (r % 2) * 2
            at = jnp.bitwise_xor(my, ry) * count + jnp.bitwise_xor(me, rz * 4 + rest)
        else:
            at = r
        scr[at] = got_ref[r].astype(F32)
    w_ref[...] = jnp.zeros_like(w_ref)
    head_ref[...] = jnp.zeros_like(head_ref)
    for y in range(2):
        for group in range(count // 8):
            tiles = [scr[y * count + group * 8 + d] for d in range(8)]
            turned = jnp.concatenate(tiles, 0).T
            for d in range(8):
                device = group * 8 + d
                at = y * stride + device * per
                for k in range(5):
                    column = turned[:per, d * 16 + k : d * 16 + k + 1]
                    w_ref[at : at + per, k * Q : (k + 1) * Q] = jnp.broadcast_to(column, (per, Q))
                column = turned[:gains, d * 16 + 5 : d * 16 + 6]
                at = (y * count + device) * gains
                gain_ref[at : at + gains, :] = jnp.broadcast_to(column, (gains, Q))
                at = 2 * device + y
                norm_ref[at : at + 1, :] = tiles[d][6:7]
                column = turned[:norms, d * 16 + 6 : d * 16 + 7]
                tall_ref[at * norms : (at + 1) * norms, :] = jnp.broadcast_to(column, (norms, Q))
            if group == 0:
                column = turned[:, 7:8] + turned[:, 8:9] + turned[:, 9:10]
                for j in range(3):
                    head_ref[y * heads : (y + 1) * heads, j : j + 1] = column[j * heads : (j + 1) * heads]


def parameters(got, sizes, by_distance):
    per, gains, norms, heads, stride = sizes
    count = got.shape[0] // 2
    me, my = lax.axis_index("dp"), lax.axis_index("mp")
    wide, gain, norm, tall, head = pl.pallas_call(
        functools.partial(param_kernel, sizes, by_distance),
        cost_estimate=takes(10),
        in_specs=[pl.BlockSpec(memory_space=pltpu.SMEM), pl.BlockSpec(memory_space=pltpu.VMEM)],
        out_shape=[
            jax.ShapeDtypeStruct((2 * stride, 5 * Q), F32),
            jax.ShapeDtypeStruct((2 * count * gains, Q), F32),
            jax.ShapeDtypeStruct((2 * count, Q), F32),
            jax.ShapeDtypeStruct((2 * count * norms, Q), F32),
            jax.ShapeDtypeStruct((2 * heads, 8), F32),
        ],
        scratch_shapes=[pltpu.VMEM((2 * count, 16, Q), F32)],
        compiler_params=pltpu.CompilerParams(vmem_limit_bytes=VMEM),
    )(jnp.stack([me, my]).astype(jnp.int32), got)
    return wide, gain, norm[:, :norms].reshape(1, -1), tall, head


def norm_kernel(place_ref, x_ref, gain_ref, window_ref, own_ref):
    mine = pl.program_id(0) - place_ref[0]
    x = x_ref[...].astype(F32)
    scaled = x * lax.rsqrt(jnp.mean(x * x, axis=1, keepdims=True) + EPS)
    normed = (scaled.T * gain_ref[...]).astype(BF16)
    window_ref[...] = normed

    @pl.when((mine >= 0) & (mine < pl.num_programs(0) - 1))
    def _():
        own_ref[...] = normed


def normalise(place_id, tokens, gain):
    total, width = tokens.shape
    own = total // 2
    blocks = own // Q
    return pl.pallas_call(
        norm_kernel,
        cost_estimate=takes(10),
        grid_spec=pltpu.PrefetchScalarGridSpec(
            num_scalar_prefetch=1,
            grid=(blocks + 1,),
            in_specs=[
                pl.BlockSpec((Q, width), lambda i, place: (i + place[0] * (blocks - 1), 0)),
                pl.BlockSpec((width, Q), lambda i, place: (0, 0)),
            ],
            out_specs=[
                pl.BlockSpec((width, Q), lambda i, place: (0, i)),
                pl.BlockSpec((width, Q), lambda i, place: (0, jnp.clip(i - place[0], 0, blocks - 1))),
            ],
        ),
        out_shape=[
            jax.ShapeDtypeStruct((width, own + HALO), BF16),
            jax.ShapeDtypeStruct((width, own), BF16),
        ],
        compiler_params=pltpu.CompilerParams(vmem_limit_bytes=VMEM),
    )(place_id, tokens, gain)


def cotangent_kernel(place_ref, mine_ref, other_ref, seg_ref, all_ref, turned_ref):
    first = place_ref[0] == 0
    mine, other = mine_ref[...].astype(F32), other_ref[...].astype(F32)
    whole = jnp.concatenate([jnp.where(first, mine, other), jnp.where(first, other, mine)], 1)
    all_ref[...] = whole.astype(BF16)
    turned_ref[...] = (whole.T * jnp.where(seg_ref[...] >= 0.0, 1.0, 0.0)).astype(BF16)


def cotangents(place_id, d_out, other, seg):
    own, half = other.shape
    blocks = own // Q
    return pl.pallas_call(
        cotangent_kernel,
        cost_estimate=takes(8),
        grid_spec=pltpu.PrefetchScalarGridSpec(
            num_scalar_prefetch=1,
            grid=(blocks,),
            in_specs=[
                pl.BlockSpec((Q, half), lambda i, place: (i + place[0] * blocks, 0)),
                pl.BlockSpec((Q, half), lambda i, place: (i, 0)),
                pl.BlockSpec((1, Q), lambda i, place: (0, i)),
            ],
            out_specs=[
                pl.BlockSpec((Q, 2 * half), lambda i, place: (i, 0)),
                pl.BlockSpec((2 * half, Q), lambda i, place: (0, i)),
            ],
        ),
        out_shape=[
            jax.ShapeDtypeStruct((own, 2 * half), BF16),
            jax.ShapeDtypeStruct((2 * half, own), BF16),
        ],
        compiler_params=pltpu.CompilerParams(vmem_limit_bytes=VMEM),
    )(place_id, d_out, other, seg)


def norm_back_kernel(place_ref, d_ref, x_ref, cot_ref, gain_ref, out_ref, low_ref):
    x = x_ref[...].astype(F32)
    inverse = lax.rsqrt(jnp.mean(x * x, axis=1, keepdims=True) + EPS)
    scaled = x * inverse
    d_scaled = d_ref[...] * gain_ref[...]
    inner = jnp.mean(d_scaled * scaled, axis=1, keepdims=True)
    rows = cot_ref[...].astype(F32) + inverse * (d_scaled - scaled * inner)
    out_ref[...] = rows
    low_ref[...] = rows.astype(BF16)


def norm_backward(place_id, d_normed, tokens, cotangent, gain):
    total, width = tokens.shape
    own = total // 2
    blocks = own // Q
    here = pl.BlockSpec((Q, width), lambda i, place: (i, 0))
    among = pl.BlockSpec((Q, width), lambda i, place: (i + place[0] * blocks, 0))
    return pl.pallas_call(
        norm_back_kernel,
        cost_estimate=takes(11),
        grid_spec=pltpu.PrefetchScalarGridSpec(
            num_scalar_prefetch=1,
            grid=(blocks,),
            in_specs=[here, among, here, pl.BlockSpec((1, width), lambda i, place: (0, 0))],
            out_specs=[among, here],
        ),
        out_shape=[jax.ShapeDtypeStruct((total, width), F32), jax.ShapeDtypeStruct((own, width), BF16)],
        compiler_params=pltpu.CompilerParams(vmem_limit_bytes=VMEM),
    )(place_id, d_normed, tokens, cotangent, gain)


def fill_kernel(place_ref, *refs):
    out_ref = refs[-1]
    at = pl.program_id(0)
    for k, part in enumerate(refs[:-2]):

        @pl.when(at == k)
        def _(part=part):
            out_ref[...] = part[...].astype(F32)


def fill_rows(place_id, whole, parts):
    blocks = len(parts)
    rows, width = parts[0].shape
    return pl.pallas_call(
        fill_kernel,
        cost_estimate=takes(5),
        grid_spec=pltpu.PrefetchScalarGridSpec(
            num_scalar_prefetch=1,
            grid=(blocks,),
            in_specs=[pl.BlockSpec((rows, width), lambda i, place: (0, 0))] * blocks
            + [pl.BlockSpec(memory_space=pl.ANY)],
            out_specs=pl.BlockSpec((rows, width), lambda i, place: (i + (1 - place[0]) * blocks, 0)),
        ),
        out_shape=jax.ShapeDtypeStruct(whole.shape, F32),
        input_output_aliases={1 + blocks: 0},
        compiler_params=pltpu.CompilerParams(vmem_limit_bytes=VMEM),
    )(place_id, *parts, whole)


def finish_kernel(sizes, xbc_ref, z_ref, w_xbc_ref, w_dt_ref, w_z_ref, own_xbc_ref, own_dt_ref, own_z_ref, taps_ref, bias_ref, gain_ref, product_ref):
    conv = w_xbc_ref.shape[1]
    heads = w_dt_ref.shape[1]
    xbc, z = xbc_ref[:, :conv].astype(F32), z_ref[...].astype(F32)
    last = xbc_ref[:, conv:].astype(F32)
    dt = last[:, :heads]
    own_xbc_ref[...] = xbc
    own_dt_ref[...] = dt
    own_z_ref[...] = z
    taps, per = taps_ref.shape
    taps_ref[...] = last[:taps, heads : heads + per]
    bias_ref[...] = last[taps : taps + 1, heads : heads + per]
    gain_ref[...] = last[taps + 1 : taps + 2, heads : heads + gain_ref.shape[1]]
    product = jnp.sum(xbc * w_xbc_ref[...].astype(F32), axis=1, keepdims=True)
    product += jnp.sum(z * w_z_ref[...].astype(F32), axis=1, keepdims=True)
    product += jnp.sum(dt * w_dt_ref[...].astype(F32), axis=1, keepdims=True)
    product_ref[...] = jnp.broadcast_to(product, product_ref.shape)


def finish(sizes, own_xbc, own_z, w_xbc, w_dt, w_z):
    rows = w_z.shape[0]
    return pl.pallas_call(
        functools.partial(finish_kernel, sizes),
        cost_estimate=takes(3),
        out_shape=[
            jax.ShapeDtypeStruct(w_xbc.shape, F32),
            jax.ShapeDtypeStruct(w_dt.shape, F32),
            jax.ShapeDtypeStruct(w_z.shape, F32),
            jax.ShapeDtypeStruct((4, sizes[0]), F32),
            jax.ShapeDtypeStruct((1, sizes[0]), F32),
            jax.ShapeDtypeStruct((1, sizes[1]), F32),
            jax.ShapeDtypeStruct((rows, Q), F32),
        ],
        compiler_params=pltpu.CompilerParams(vmem_limit_bytes=VMEM),
    )(own_xbc, own_z, w_xbc, w_dt, w_z)


def spare_kernel(sizes, conv_ref, gain_ref, out_ref):
    per, gains, norms, heads, stride, skip = sizes
    count = out_ref.shape[1]
    lane = lax.broadcasted_iota(jnp.int32, (1, Q), 1)

    def turned(v):
        return jnp.concatenate([v, jnp.zeros((Q - v.shape[0], Q), F32)], 0).T

    def moved(row, size):
        return jnp.where((lane >= skip) & (lane < skip + size), pltpu.roll(row, skip, 1), 0.0)

    for y in range(2):
        for d in range(count):
            at = y * stride + d * per
            rows = [moved(turned(conv_ref[at : at + per, :])[k : k + 1], per) for k in range(5)]
            at = (y * count + d) * gains
            total = jnp.sum(turned(gain_ref[at : at + gains, :]), axis=0, keepdims=True)
            rows += [moved(total, gains), jnp.zeros((10, Q), F32)]
            out_ref[y, d] = jnp.concatenate(rows, 0)


def spare_block(sizes, count, conv_sums, gain_grad):
    return pl.pallas_call(
        functools.partial(spare_kernel, sizes),
        cost_estimate=takes(4),
        out_shape=jax.ShapeDtypeStruct((2, count, 16, Q), F32),
        compiler_params=pltpu.CompilerParams(vmem_limit_bytes=VMEM),
    )(conv_sums, gain_grad)


def grad_kernel(core_ref, left_ref, right_ref, *refs):
    spare_ref = refs[0] if len(refs) == 4 else None
    keep_ref, send_ref, scr = refs[-3:]
    parts, rows, tile = scr.shape
    scr[...] = dot(left_ref[...], right_ref[...], 1, 1).astype(BF16).reshape(scr.shape)
    if spare_ref is not None:

        @pl.when(pl.program_id(1) == pl.num_programs(1) - 1)
        def _():
            for p in range(parts):
                old = scr[p, :16, tile - Q :].astype(F32)
                scr[p, :16, tile - Q :] = (old + spare_ref[0, p]).astype(BF16)

    core = core_ref[0]
    for p in range(parts // 2):
        keep_ref[0, p] = scr[2 * p + core]
        send_ref[0, p] = scr[2 * p + 1 - core]


def grad_plain_kernel(left_ref, right_ref, out_ref):
    out_ref[...] = dot(left_ref[...], right_ref[...], 1, 1).astype(BF16).reshape(out_ref.shape)


def weight_grad_sum(left, right, count):
    width, rows = left.shape
    channels = right.shape[0] // 2
    tile = 256
    grad = pl.pallas_call(
        grad_plain_kernel,
        cost_estimate=takes(17),
        grid=(2, channels // tile),
        in_specs=[
            pl.BlockSpec((width, rows), lambda y, k: (0, 0)),
            pl.BlockSpec((tile, rows), lambda y, k: (y * (channels // tile) + k, 0)),
        ],
        out_specs=pl.BlockSpec((count, 1, width // count, tile), lambda y, k: (0, y, 0, k)),
        out_shape=jax.ShapeDtypeStruct((count, 2, width // count, channels), BF16),
        compiler_params=pltpu.CompilerParams(vmem_limit_bytes=VMEM),
    )(left, right)
    return grad, lax.psum_scatter(
        grad.reshape(-1, channels), ("dp", "mp"), scatter_dimension=0, tiled=True
    )


def weight_grad(left, right, count, tiles, spare=None):
    width, rows = left.shape
    tile = 256
    per_half = right.shape[0] // 2 // tile
    begin, end = tiles
    shape = (2, count // 2, width // count, (end - begin) * tile)
    block = pl.BlockSpec((1, count // 2, width // count, tile), lambda y, k: (y, 0, 0, k))
    core = (lax.axis_index("dp") % 2).reshape(1).astype(jnp.int32)
    more = [] if spare is None else [pl.BlockSpec((1,) + spare.shape[1:], lambda y, k: (y, 0, 0, 0))]
    return pl.pallas_call(
        grad_kernel,
        cost_estimate=takes(12),
        grid=(2, end - begin),
        in_specs=[
            pl.BlockSpec(memory_space=pltpu.SMEM),
            pl.BlockSpec((width, rows), lambda y, k: (0, 0)),
            pl.BlockSpec((tile, rows), lambda y, k: (y * per_half + begin + k, 0)),
        ]
        + more,
        out_specs=[block, block],
        out_shape=[jax.ShapeDtypeStruct(shape, BF16)] * 2,
        scratch_shapes=[pltpu.VMEM((count, width // count, tile), BF16)],
        compiler_params=pltpu.CompilerParams(vmem_limit_bytes=VMEM),
    )(core, left, right, *([] if spare is None else [spare]))


def rows_kernel(raw_ref, head_ref, mask_ref, *outs):
    cum_ref, shift_ref, into_ref, onto_ref, keep_ref, step_ref, slope_ref, ratio_ref, start_ref, end_ref = outs
    chunks = raw_ref.shape[1] // Q
    rate = -jnp.exp(head_ref[:, 0:1])
    bias = head_ref[:, 1:2]
    source = lax.broadcasted_iota(jnp.int32, (Q, Q), 0)
    target = lax.broadcasted_iota(jnp.int32, (Q, Q), 1)
    upto = (source <= target).astype(F32)
    totals, sums, log_steps, steps = [], [], [], []
    for c in range(chunks):
        span = slice(c * Q, (c + 1) * Q)
        v = raw_ref[:, span] + bias
        tail = jnp.log1p(jnp.exp(-jnp.abs(v)))
        step = jnp.maximum(v, 0.0) + tail
        low = v < -20.0
        log_step = jnp.where(low, v, jnp.log(jnp.where(low, 1.0, step)))
        slope = 1.0 / (1.0 + jnp.exp(-v))
        decay = step * rate * LOG2E
        cum = dot(decay, upto, 1, 0, lax.Precision.HIGHEST)
        total = cum[:, Q - 1 : Q]
        shift = cum - log_step * LOG2E
        cum_ref[:, span] = cum
        shift_ref[:, span] = shift
        step_ref[:, span] = step
        slope_ref[:, span] = slope
        ratio_ref[:, span] = jnp.where(low, 1.0, slope / jnp.where(low, 1.0, step))
        into_ref[:, span] = jnp.exp2(cum) * mask_ref[0:1, span]
        onto_ref[:, span] = jnp.exp2(total - cum) * step * mask_ref[1:2, span]
        keep_ref[:, span] = jnp.exp2(total) * mask_ref[2:3, span]
        totals.append(total)
        sums.append(cum)
        steps.append(step)
    before = jnp.zeros_like(totals[0])
    for c in range(chunks):
        span = slice(c * Q, (c + 1) * Q)
        start_ref[:, span] = jnp.exp2(before + sums[c]) * mask_ref[4:5, span]
        before = before + totals[c]
    after = jnp.zeros_like(totals[0])
    for c in reversed(range(chunks)):
        span = slice(c * Q, (c + 1) * Q)
        end_ref[:, span] = jnp.exp2(after + totals[c] - sums[c]) * steps[c] * mask_ref[3:4, span]
        after = after + totals[c]


def head_rows(raw, heads, masks):
    shape = jax.ShapeDtypeStruct(raw.shape, F32)
    return pl.pallas_call(
        rows_kernel,
        cost_estimate=takes(3),
        out_shape=[shape] * 10,
        compiler_params=pltpu.CompilerParams(vmem_limit_bytes=VMEM),
    )(raw, heads, masks)


def wide_columns(w_ref, rows):
    return [w_ref[rows, k * Q : (k + 1) * Q] for k in range(5)]


def conv_kernel(place_ref, proj_ref, w_ref, mask_ref, end_ref, out_ref, pre_ref, state_ref, b_scr, x_scr):
    s = pl.program_id(0)
    channels, own = out_ref.shape
    at = pl.multiple_of(place_ref[0] * HALO, HALO)
    size = 64

    def strip(i, carry):
        rows = pl.ds(pl.multiple_of(i * size, size), size)
        wide = wide_columns(w_ref, rows)
        before = proj_ref[rows, pl.ds(pl.multiple_of(jnp.maximum(at - Q, 0), Q), Q)].astype(F32)
        lane = lax.broadcasted_iota(jnp.int32, (size, Q), 1)
        last = [pltpu.roll(before, k, 1) for k in (1, 2, 3)]
        weight = end_ref[pl.ds(jnp.clip((s - 1) * 4 + i, 0, end_ref.shape[0] - 1), 1), :]
        for j in range(own // Q):
            now = proj_ref[rows, pl.ds(pl.multiple_of(at + j * Q, Q), Q)].astype(F32)
            span = slice(j * Q, (j + 1) * Q)
            pre = wide[4] + wide[3] * now
            for k in (1, 2, 3):
                rolled = pltpu.roll(now, k, 1)
                pre = pre + wide[3 - k] * (jnp.where(lane < k, last[k - 1], rolled) * mask_ref[k - 1 : k, span])
                last[k - 1] = rolled
            act = pre * sigmoid(pre)
            pre_ref[rows, span] = pre.astype(BF16)
            out_ref[rows, span] = act.astype(BF16)
            x_scr[rows, span] = (act * weight[:, span]).astype(BF16)
        return carry

    lax.fori_loop(0, channels // size, strip, 0)

    @pl.when(s == 0)
    def _():
        b_scr[...] = out_ref[:Q, :].astype(F32).T.astype(BF16)

    @pl.when((s > 0) & (s < pl.num_programs(0) - 1))
    def _():
        state_ref[...] = dot(x_scr[...], b_scr[...], 1, 0).astype(state_ref.dtype)


def conv_forward(place_id, proj, w_wide, masks, end_rows):
    channels, window = proj.shape
    own = window - HALO
    blocks = channels // 256
    half = blocks // 2

    def order(s):
        return jnp.where(s == 0, half - 1, jnp.where(s < half, s - 1, s))

    return pl.pallas_call(
        conv_kernel,
        cost_estimate=takes(25),
        grid=(blocks,),
        in_specs=[
            pl.BlockSpec(memory_space=pltpu.SMEM),
            pl.BlockSpec((256, window), lambda s: (order(s), 0)),
            pl.BlockSpec((256, 5 * Q), lambda s: (order(s), 0)),
            pl.BlockSpec(masks.shape, lambda s: (0, 0)),
            pl.BlockSpec(end_rows.shape, lambda s: (0, 0)),
        ],
        out_specs=[
            pl.BlockSpec((256, own), lambda s: (order(s), 0)),
            pl.BlockSpec((256, own), lambda s: (order(s), 0)),
            pl.BlockSpec((256, Q), lambda s: (jnp.clip(s - 1, 0, blocks - 3), 0)),
        ],
        out_shape=[
            jax.ShapeDtypeStruct((channels, own), BF16),
            jax.ShapeDtypeStruct((channels, own), BF16),
            jax.ShapeDtypeStruct(((blocks - 2) * 256, Q), BF16),
        ],
        scratch_shapes=[pltpu.VMEM((own, Q), BF16), pltpu.VMEM((256, own), BF16)],
        compiler_params=pltpu.CompilerParams(vmem_limit_bytes=VMEM),
    )(place_id, proj, w_wide, masks, end_rows)


def chunk_scores(conv_ref, bc, seg_ref):
    inner_half, stride = bc
    b_t = conv_ref[inner_half : inner_half + Q, :]
    c_t = conv_ref[stride + inner_half : stride + inner_half + Q, :]
    b_m = b_t.astype(F32).T.astype(BF16)
    scores = dot(b_m, c_t, 1, 0)
    source = lax.broadcasted_iota(jnp.int32, (Q, Q), 0)
    target = lax.broadcasted_iota(jnp.int32, (Q, Q), 1)
    seg = jnp.broadcast_to(seg_ref[...], (Q, Q))
    allowed = (source <= target) & (seg.T == seg)
    return b_t, c_t, b_m, jnp.where(allowed, scores, 0.0), allowed


def columns_of(shift_ref, col_scr):
    heads = shift_ref.shape[0]
    padded = jnp.concatenate([shift_ref[...], jnp.zeros((Q - heads, Q), F32)], 0).T
    for g in range(heads // 8):
        col_scr[g] = padded[:, g * 8 : (g + 1) * 8]


def scan_kernel(
    bc, skip_ref, conv_ref, z_ref, cum_ref, shift_ref, into_ref, onto_ref, keep_ref, seg_ref,
    gain_ref, first_ref, out_ref, ssd_ref, scale_ref, states_ref, state, gated, col_scr,
):
    inner_half, stride = bc
    groups = 2 * inner_half // 512

    @pl.when(pl.program_id(0) == 0)
    def _():
        state[...] = first_ref[...].astype(F32)

    _, c_t, b_m, scores, _ = chunk_scores(conv_ref, bc, seg_ref)
    columns_of(shift_ref, col_scr)

    def group(g, squares):
        at = pl.multiple_of(g * 512, 512)
        x_at = pl.multiple_of(g * 512 + jnp.where(g >= groups // 2, stride - inner_half, 0), 256)
        held = state[pl.ds(at, 512), :].astype(BF16)
        states_ref[0, pl.ds(at, 512), :] = held
        from_state = dot(held, c_t, 1, 0)
        cols = col_scr[g]
        parts = []
        for k in range(8):
            h = g * 8 + k
            x = conv_ref[pl.ds(x_at + k * 64, 64), :]
            spread = jnp.minimum(cum_ref[pl.ds(h, 1), :] - cols[:, k : k + 1], CAP)
            mixing = (jnp.exp2(spread) * scores).astype(BF16)
            xf = x.astype(F32)
            y = dot(x, mixing, 1, 0) + from_state[k * 64 : (k + 1) * 64] * into_ref[pl.ds(h, 1), :] + skip_ref[h] * xf
            z = z_ref[pl.ds(at + k * 64, 64), :].astype(F32)
            g_out = y * (z * sigmoid(z))
            squares = squares + g_out * g_out
            ssd_ref[pl.ds(at + k * 64, 64), :] = y.astype(BF16)
            gated[pl.ds(at + k * 64, 64), :] = g_out
            parts.append((xf * onto_ref[pl.ds(h, 1), :]).astype(BF16))
        fresh = dot(jnp.concatenate(parts, 0), b_m, 1, 0)
        for k in range(8):
            rows = pl.ds(at + k * 64, 64)
            state[rows, :] = state[rows, :] * keep_ref[pl.ds(g * 8 + k, 1), :] + fresh[k * 64 : (k + 1) * 64]
        return squares

    squares = lax.fori_loop(0, groups, group, jnp.zeros((64, Q), F32))
    scale = lax.rsqrt(jnp.sum(squares, axis=0, keepdims=True) / (2 * inner_half) + EPS)
    scale_ref[...] = scale

    def finish(g, carry):
        rows = pl.ds(pl.multiple_of(g * 512, 512), 512)
        out_ref[rows, :] = (gated[rows, :] * scale * gain_ref[rows, :]).astype(BF16)
        return carry

    lax.fori_loop(0, groups, finish, 0)


def scan_forward(bc, skip, conv, z, rows, seg, gain, first):
    inner = 2 * bc[0]
    channels, own = conv.shape
    chunks = own // Q
    heads = inner // 64
    row_spec = pl.BlockSpec((heads, Q), lambda c: (0, c))
    whole = pl.BlockSpec((inner, Q), lambda c: (0, 0))
    tile = pl.BlockSpec((inner, Q), lambda c: (0, c))
    cum, shift, into, onto, keep = rows[:5]
    return pl.pallas_call(
        functools.partial(scan_kernel, bc),
        cost_estimate=takes(29),
        grid=(chunks,),
        in_specs=[
            pl.BlockSpec(memory_space=pltpu.SMEM),
            pl.BlockSpec((channels, Q), lambda c: (0, c)),
            tile,
            row_spec, row_spec, row_spec, row_spec, row_spec,
            pl.BlockSpec((1, Q), lambda c: (0, c)),
            whole, whole,
        ],
        out_specs=[tile, tile, pl.BlockSpec((1, Q), lambda c: (0, c)), pl.BlockSpec((1, inner, Q), lambda c: (c, 0, 0))],
        out_shape=[
            jax.ShapeDtypeStruct((inner, own), BF16),
            jax.ShapeDtypeStruct((inner, own), BF16),
            jax.ShapeDtypeStruct((1, own), F32),
            jax.ShapeDtypeStruct((chunks, inner, Q), BF16),
        ],
        scratch_shapes=[pltpu.VMEM((inner, Q), F32), pltpu.VMEM((inner, Q), F32), pltpu.VMEM((heads // 8, Q, 8), F32)],
        compiler_params=pltpu.CompilerParams(vmem_limit_bytes=VMEM),
    )(skip, conv, z, cum, shift, into, onto, keep, seg, gain, first)


def gate_back_kernel(
    d_unit_ref, ssd_ref, z_ref, scale_ref, gain_ref, start_ref, c_ref, d_ssd_ref, d_gate_ref, gain_grad_ref, first_grad_ref, into, first_scr
):
    inner, width = ssd_ref.shape
    size = 64

    @pl.when(pl.program_id(0) == 0)
    def _():
        gain_grad_ref[...] = jnp.zeros_like(gain_grad_ref)
        first_scr[...] = jnp.zeros_like(first_scr)

    scale = scale_ref[...]

    def gain_of(rows):
        return jnp.concatenate([gain_ref[rows, :]] * (width // Q), 1)

    def look(g, cross):
        rows = pl.ds(pl.multiple_of(g * size, size), size)
        z = z_ref[rows, :].astype(F32)
        unit = ssd_ref[rows, :].astype(F32) * (z * sigmoid(z)) * scale
        product = d_unit_ref[rows, :].astype(F32) * unit
        gain_grad_ref[rows, :] += sum(product[:, k * Q : (k + 1) * Q] for k in range(width // Q))
        product = product * gain_of(rows)
        return cross + jnp.sum(product.reshape(size // 8, 8, width), axis=0)

    cross = lax.fori_loop(0, inner // size, look, jnp.zeros((8, width), F32))
    cross = jnp.sum(cross, axis=0, keepdims=True) / inner

    def head(h, carry):
        rows = pl.ds(pl.multiple_of(h * size, size), size)
        z = z_ref[rows, :].astype(F32)
        ssd = ssd_ref[rows, :].astype(F32)
        sig = sigmoid(z)
        act = z * sig
        unit = ssd * act * scale
        d_gated = scale * (d_unit_ref[rows, :].astype(F32) * gain_of(rows) - unit * cross)
        d_ssd = d_gated * act
        d_ssd_ref[rows, :] = d_ssd.astype(BF16)
        d_gate_ref[rows, :] = (d_gated * ssd * (sig + act * (1.0 - sig))).astype(BF16)
        into[rows, :] = (d_ssd * start_ref[pl.ds(h, 1), :]).astype(BF16)
        return carry

    lax.fori_loop(0, inner // size, head, 0)
    c_m = c_ref[...].astype(F32).T.astype(BF16)

    def sums(g, carry):
        rows = pl.ds(pl.multiple_of(g * 512, 512), 512)
        first_scr[rows, :] += dot(into[rows, :], c_m, 1, 0)
        return carry

    lax.fori_loop(0, inner // 512, sums, 0)

    @pl.when(pl.program_id(0) == pl.num_programs(0) - 1)
    def _():
        first_grad_ref[...] = first_scr[...].astype(BF16)


def gate_backward(bc, d_unit, ssd, z, scale, gain, start, conv):
    inner, own = ssd.shape
    heads = inner // 64
    width = 2 * Q
    tile = pl.BlockSpec((inner, width), lambda c: (0, c))
    whole = pl.BlockSpec((inner, Q), lambda c: (0, 0))
    c_block = (bc[0] + bc[1]) // Q
    return pl.pallas_call(
        gate_back_kernel,
        cost_estimate=takes(32),
        grid=(own // width,),
        in_specs=[
            tile, tile, tile,
            pl.BlockSpec((1, width), lambda c: (0, c)),
            whole,
            pl.BlockSpec((heads, width), lambda c: (0, c)),
            pl.BlockSpec((Q, width), lambda c: (c_block, c)),
        ],
        out_specs=[tile, tile, whole, whole],
        out_shape=[
            jax.ShapeDtypeStruct((inner, own), BF16),
            jax.ShapeDtypeStruct((inner, own), BF16),
            jax.ShapeDtypeStruct((inner, Q), F32),
            jax.ShapeDtypeStruct((inner, Q), BF16),
        ],
        scratch_shapes=[pltpu.VMEM((inner, width), BF16), pltpu.VMEM((inner, Q), F32)],
        compiler_params=pltpu.CompilerParams(vmem_limit_bytes=VMEM),
    )(d_unit, ssd, z, scale, gain, start, conv)


def scan_back_kernel(
    bc, skip_ref, conv_ref, d_ssd_ref, states_ref, last_ref, cum_ref, shift_ref, into_ref, onto_ref, keep_ref,
    step_ref, slope_ref, ratio_ref, seg_ref, head_ref,
    d_conv_ref, d_raw_ref, bias_grad_ref, rate_grad_ref, skip_grad_ref,
    grad, col_scr, row_scr, diag_scr, state_scr, hold_scr, y_scr, x_scr, dst_scr, dc_scr, db_scr,
):
    inner_half, stride = bc
    groups = 2 * inner_half // 512
    heads = 2 * inner_half // 64

    @pl.when(pl.program_id(0) == 0)
    def _():
        grad[...] = last_ref[...].astype(F32)
        bias_grad_ref[...] = jnp.zeros_like(bias_grad_ref)
        rate_grad_ref[...] = jnp.zeros_like(rate_grad_ref)
        skip_grad_ref[...] = jnp.zeros_like(skip_grad_ref)

    b_t, c_t, b_m, scores, allowed = chunk_scores(conv_ref, bc, seg_ref)
    c_m = c_t.astype(F32).T.astype(BF16)
    columns_of(shift_ref, col_scr)
    dst_scr[...] = jnp.zeros_like(dst_scr)
    dc_scr[...] = jnp.zeros_like(dc_scr)
    db_scr[...] = jnp.zeros_like(db_scr)

    def group(g, carry):
        at = pl.multiple_of(g * 512, 512)
        x_at = pl.multiple_of(g * 512 + jnp.where(g >= groups // 2, stride - inner_half, 0), 256)
        held = states_ref[0, pl.ds(at, 512), :]
        g_low = grad[pl.ds(at, 512), :].astype(BF16)
        from_state = dot(held, c_t, 1, 0)
        onto_state = dot(g_low, b_t, 1, 0)
        cols = col_scr[g]
        d_scores = jnp.zeros((Q, Q), F32)
        for k in range(8):
            h = g * 8 + k
            row = pl.ds(h, 1)
            span = slice(k * 64, (k + 1) * 64)
            x = conv_ref[pl.ds(x_at + k * 64, 64), :]
            dy = d_ssd_ref[pl.ds(at + k * 64, 64), :]
            xf, dyf = x.astype(F32), dy.astype(F32)
            decays = jnp.exp2(jnp.minimum(cum_ref[row, :] - cols[:, k : k + 1], CAP))
            mixing = (decays * scores).astype(BF16)
            d_scores = d_scores + decays * dot(x, dy, 0, 0)
            y = dot(x, mixing, 1, 0) + from_state[span] * into_ref[row, :]
            dx = dot(dy, mixing, 1, 1)
            dx_state = onto_state[span] * onto_ref[row, :]
            row_scr[row, :] = jnp.sum(dyf * y, axis=0, keepdims=True)
            diag_scr[row, :] = jnp.sum(xf * dx, axis=0, keepdims=True)
            state_scr[row, :] = jnp.sum(xf * dx_state, axis=0, keepdims=True)
            skip_grad_ref[row, :] += jnp.sum(xf * dyf, axis=0, keepdims=True)
            hold_scr[row, :] = jnp.sum(grad[pl.ds(at + k * 64, 64), :] * held[span].astype(F32), axis=0, keepdims=True)
            d_conv_ref[pl.ds(x_at + k * 64, 64), :] = (dx + dx_state + skip_ref[h] * dyf).astype(BF16)
            y_scr[span, :] = (dyf * into_ref[row, :]).astype(BF16)
            x_scr[span, :] = (xf * onto_ref[row, :]).astype(BF16)
        dst_scr[...] += d_scores
        fresh = dot(y_scr[...], c_m, 1, 0)
        dc_scr[...] += dot(held, y_scr[...], 0, 0)
        db_scr[...] += dot(g_low, x_scr[...], 0, 0)
        for k in range(8):
            rows = pl.ds(at + k * 64, 64)
            grad[rows, :] = grad[rows, :] * keep_ref[pl.ds(g * 8 + k, 1), :] + fresh[k * 64 : (k + 1) * 64]
        return carry

    lax.fori_loop(0, groups, group, 0)
    d_scores = jnp.where(allowed, dst_scr[...], 0.0).astype(BF16)
    zeros = jnp.zeros((stride - inner_half - Q, Q), BF16)
    d_conv_ref[inner_half : inner_half + Q, :] = (db_scr[...] + dot(c_t, d_scores, 1, 1)).astype(BF16)
    d_conv_ref[inner_half + Q : stride, :] = zeros
    d_conv_ref[stride + inner_half : stride + inner_half + Q, :] = (dc_scr[...] + dot(b_t, d_scores, 1, 0)).astype(BF16)
    d_conv_ref[stride + inner_half + Q :, :] = zeros

    source = lax.broadcasted_iota(jnp.int32, (Q, Q), 0)
    target = lax.broadcasted_iota(jnp.int32, (Q, Q), 1)
    since = (source >= target).astype(F32)
    columns = diag_scr[...] + state_scr[...]
    d_decay = dot(row_scr[...] - columns, since, 1, 0, lax.Precision.HIGHEST)
    d_decay = d_decay + jnp.sum(state_scr[...] + hold_scr[...] * keep_ref[...], axis=1, keepdims=True)
    rate = -jnp.exp(head_ref[:, 0:1])
    slope = slope_ref[...]
    d_raw = columns * ratio_ref[...] + rate * d_decay * slope
    bias_grad_ref[...] += d_raw
    rate_grad_ref[...] += step_ref[...] * d_decay * rate
    d_raw_ref[...] = jnp.zeros_like(d_raw_ref)
    d_raw_ref[0 : heads // 2, :] = d_raw[: heads // 2].astype(BF16)
    d_raw_ref[Q : Q + heads // 2, :] = d_raw[heads // 2 :].astype(BF16)


def scan_backward(bc, skip, conv, d_ssd, states, last, rows, seg, head_cols):
    inner = 2 * bc[0]
    channels, own = conv.shape
    chunks = own // Q
    heads = inner // 64
    end = chunks - 1
    row_spec = pl.BlockSpec((heads, Q), lambda c: (0, end - c))
    whole = pl.BlockSpec((inner, Q), lambda c: (0, 0))
    sums = pl.BlockSpec((heads, Q), lambda c: (0, 0))
    cum, shift, into, onto, keep, step, slope, ratio = rows[:8]
    small = jax.ShapeDtypeStruct((heads, Q), F32)
    row_buf = pltpu.VMEM((heads, Q), F32)
    square = pltpu.VMEM((Q, Q), F32)
    return pl.pallas_call(
        functools.partial(scan_back_kernel, bc),
        cost_estimate=takes(44),
        grid=(chunks,),
        in_specs=[
            pl.BlockSpec(memory_space=pltpu.SMEM),
            pl.BlockSpec((channels, Q), lambda c: (0, end - c)),
            pl.BlockSpec((inner, Q), lambda c: (0, end - c)),
            pl.BlockSpec((1, inner, Q), lambda c: (end - c, 0, 0)),
            whole,
        ]
        + [row_spec] * 8
        + [
            pl.BlockSpec((1, Q), lambda c: (0, end - c)),
            pl.BlockSpec(head_cols.shape, lambda c: (0, 0)),
        ],
        out_specs=[
            pl.BlockSpec((channels, Q), lambda c: (0, end - c)),
            pl.BlockSpec((2 * Q, Q), lambda c: (0, end - c)),
            sums, sums, sums,
        ],
        out_shape=[
            jax.ShapeDtypeStruct((channels, own), BF16),
            jax.ShapeDtypeStruct((2 * Q, own), BF16),
            small, small, small,
        ],
        scratch_shapes=[
            pltpu.VMEM((inner, Q), F32), pltpu.VMEM((heads // 8, Q, 8), F32),
            row_buf, row_buf, row_buf, row_buf,
            pltpu.VMEM((512, Q), BF16), pltpu.VMEM((512, Q), BF16),
            square, square, square,
        ],
        compiler_params=pltpu.CompilerParams(vmem_limit_bytes=VMEM),
    )(skip, conv, d_ssd, states, last, cum, shift, into, onto, keep, step, slope, ratio, seg, head_cols)


def conv_back_kernel(half, place_ref, proj_ref, pre_ref, d_ref, beyond_ref, raw_ref, w_ref, mask_ref, out_ref, sums_ref, acc):
    s = pl.program_id(0)
    channels, own = out_ref.shape
    tiles = own // Q
    at = pl.multiple_of(place_ref[0] * HALO, HALO)
    size = 32

    def strip(i, carry):
        rows = pl.ds(pl.multiple_of(i * size, size), size)
        wide = wide_columns(w_ref, rows)
        lane = lax.broadcasted_iota(jnp.int32, (size, Q), 1)
        sums = [jnp.zeros((size, Q), F32)] * 5
        kept, moved = None, None
        for j in range(tiles + 1):
            span = slice(j * Q, (j + 1) * Q)
            if j < tiles:
                pre = pre_ref[rows, span].astype(F32)
                sig = sigmoid(pre)
                d_pre = d_ref[rows, span].astype(F32) * (sig + pre * sig * (1.0 - sig))
            else:
                d_pre = beyond_ref[rows, :].astype(F32)
            back = [pltpu.roll(d_pre * mask_ref[k - 1 : k, span], Q - k, 1) for k in (1, 2, 3)]
            if j > 0:
                now = proj_ref[rows, pl.ds(pl.multiple_of(at + (j - 1) * Q, Q), Q)].astype(F32)
                shifted = [kept] + [jnp.where(lane < Q - k, moved[k - 1], back[k - 1]) for k in (1, 2, 3)]
                d_proj = wide[3] * kept
                for k in (1, 2, 3):
                    d_proj = d_proj + wide[3 - k] * shifted[k]
                for k in range(4):
                    sums[3 - k] = sums[3 - k] + now * shifted[k]
                out_ref[rows, (j - 1) * Q : j * Q] = d_proj.astype(BF16)
            if j < tiles:
                sums[4] = sums[4] + d_pre
            kept, moved = d_pre, back
        for k in range(5):
            acc[rows, k * Q : (k + 1) * Q] = sums[k]
        return carry

    lax.fori_loop(0, channels // size, strip, 0)
    rows_of = lax.broadcasted_iota(jnp.int32, (5 * Q, Q), 0) // Q
    column = lax.broadcasted_iota(jnp.int32, (5 * Q, Q), 1)
    ones = jnp.where(rows_of == column, 1.0, 0.0).astype(BF16)
    high = acc[...].astype(BF16)
    low = (acc[...] - high.astype(F32)).astype(BF16)
    sums_ref[...] = dot(high, ones, 1, 0) + dot(low, ones, 1, 0)

    @pl.when(lax.rem(s, half) == half - 1)
    def _():
        out_ref[Q:, :] = raw_ref[...]


def conv_backward(place_id, proj, pre, d_conv, beyond, d_raw, w_wide, masks):
    channels, window = proj.shape
    own = window - HALO
    blocks = channels // 256
    half = blocks // 2
    return pl.pallas_call(
        functools.partial(conv_back_kernel, half),
        cost_estimate=takes(31),
        grid=(blocks,),
        in_specs=[
            pl.BlockSpec(memory_space=pltpu.SMEM),
            pl.BlockSpec((256, window), lambda s: (s, 0)),
            pl.BlockSpec((256, own), lambda s: (s, 0)),
            pl.BlockSpec((256, own), lambda s: (s, 0)),
            pl.BlockSpec((256, HALO), lambda s: (s, 0)),
            pl.BlockSpec((Q, own), lambda s: (s // half, 0)),
            pl.BlockSpec((256, 5 * Q), lambda s: (s, 0)),
            pl.BlockSpec(masks.shape, lambda s: (0, 0)),
        ],
        out_specs=[pl.BlockSpec((256, own), lambda s: (s, 0)), pl.BlockSpec((256, Q), lambda s: (s, 0))],
        out_shape=[jax.ShapeDtypeStruct((channels, own), BF16), jax.ShapeDtypeStruct((channels, Q), F32)],
        scratch_shapes=[pltpu.VMEM((256, 5 * Q), F32)],
        compiler_params=pltpu.CompilerParams(vmem_limit_bytes=VMEM),
    )(place_id, proj, pre, d_conv, beyond, d_raw, w_wide, masks)


def shards(
    tokens, token_seq, w_z, w_xbc, w_dt, w_out, conv_w, conv_b, gate_gain, norm_gain, a_log, d_skip, dt_bias, d_out, *, count
):
    my = lax.axis_index("mp")
    all_rows, width = tokens.shape
    own = all_rows // 2
    window = own + HALO
    inner_half = w_z.shape[1]
    inner = 2 * inner_half
    conv_half = w_xbc.shape[1]
    state_dim = conv_half - inner_half
    heads_half = w_dt.shape[1]
    stride = -(-(conv_half + heads_half) // 256) * 256
    bc = (inner_half, stride)
    place_id = my.reshape(1).astype(jnp.int32)

    per, taps = conv_w.shape[1], conv_w.shape[0]
    shard_rows = w_dt.shape[0]
    spare = stride - conv_half - heads_half
    head_params = jnp.concatenate([a_log, dt_bias, d_skip])
    high = head_params.astype(BF16)
    middle = (head_params - high.astype(F32)).astype(BF16)
    low = (head_params - high.astype(F32) - middle.astype(F32)).astype(BF16)
    vectors = [*conv_w, conv_b, gate_gain, norm_gain, high, middle, low]
    small = jnp.stack([jnp.pad(v, (0, Q - v.shape[0])) for v in vectors])
    small = jnp.pad(small, ((0, 16 - len(vectors)), (0, 0)))
    shard_xbc = jnp.concatenate([w_xbc, w_dt, jnp.zeros((shard_rows, spare), BF16)], 1)
    sizes = (per, gate_gain.shape[0], norm_gain.shape[0], heads_half, stride)
    spare_sizes = (*sizes, Q - spare)
    conv_masks, scan_masks, seg_row = row_masks(place_id, token_seq)

    if count == 16:
        full_xbc, prepared, normed_rows, marks = gather_now(
            shard_xbc,
            small,
            lambda got: parameters(got, sizes, True),
            lambda got: normalise(place_id, tokens, got[3]),
        )
    else:
        marks = ()
        full_xbc = gather_later(shard_xbc, marks)
        small = lax.all_gather(lax.all_gather(small, "dp", axis=0, tiled=False), "mp", axis=0, tiled=False)
        prepared = parameters(small.reshape(2 * count, 16, Q), sizes, False)
        normed_rows = normalise(place_id, tokens, prepared[3])
    full_z = gather_later(w_z, marks)
    full_out = gather_later(w_out.T, marks)
    w_wide, gain_wide, gain_in, gain_tall, head_cols = prepared
    window_t, normed_t = normed_rows
    skip_all = head_cols[:, 2]
    full_xbc = full_xbc.reshape(2, width, stride)

    proj = jnp.einsum("ydc,dt->yct", full_xbc, window_t, preferred_element_type=F32).astype(BF16)
    proj = proj.reshape(2 * stride, window)
    full_dt = full_xbc[:, :, conv_half : conv_half + heads_half]
    dt_raw = jnp.einsum("ydh,dt->yht", full_dt, normed_t, preferred_element_type=F32).reshape(2 * heads_half, own)
    rows = head_rows(dt_raw, head_cols, scan_masks)
    start_rows, end_rows = rows[8], rows[9]
    conved, pre, end_state = conv_forward(place_id, proj, w_wide, conv_masks, end_rows)
    state_flow = once(end_state, lambda a: lax.ppermute(a, "mp", [(0, 1)]))
    z = jnp.einsum("ydk,dt->ykt", full_z, ahead(normed_t, state_flow), preferred_element_type=F32).astype(BF16).reshape(inner, own)
    z = after(z, state_flow)
    d_flow = once(lax.dynamic_slice_in_dim(tie(d_out, proj)[0], (1 - my) * own, own, 0), swap)
    z = ahead(z, d_flow)
    out_normed, ssd, scale, states = scan_forward(
        bc, skip_all, conved, z, rows, seg_row, gain_wide, state_flow.result
    )
    out_normed = after(out_normed, d_flow)
    cotangent, cot_t = cotangents(place_id, d_out, d_flow.result, seg_row)
    grad_out, own_out = weight_grad_sum(cot_t, out_normed, count)
    out_ready = tie(out_normed, grad_out)[0]
    branch = jnp.einsum(
        "ykt,ydk->td", out_ready.reshape(2, inner_half, own), full_out, preferred_element_type=F32
    )
    first_half = my == 0
    live_rows = (lax.dynamic_slice_in_dim(token_seq, my * own, own, 0) >= 0)[:, None]
    tokens_own = lax.dynamic_slice_in_dim(tokens, my * own, own, 0).astype(F32)
    layer_rows = (tokens_own + jnp.where(live_rows, branch, 0.0)).astype(BF16)
    half_width = width // 2
    layer_mine = lax.dynamic_slice_in_dim(layer_rows, my * half_width, half_width, 1)
    layer_flow = once(lax.dynamic_slice_in_dim(layer_rows, (1 - my) * half_width, half_width, 1), swap)

    d_unit = jnp.einsum("ydk,dt->ykt", full_out, ahead(cot_t, layer_flow), preferred_element_type=F32).astype(BF16).reshape(inner, own)
    d_ssd, d_gate, gain_grad, first_grad = gate_backward(bc, d_unit, ssd, z, scale, gain_wide, start_rows, conved)
    d_gate = after(d_gate, layer_flow)
    grad_flow = once(first_grad, lambda a: lax.ppermute(a, "mp", [(1, 0)]))
    grad_z, own_z = weight_grad_sum(normed_t, ahead(d_gate, grad_flow), count)
    d_gate = tie(d_gate, grad_z)[0]
    d_normed_z = jnp.einsum("ykt,ydk->td", d_gate.reshape(2, inner_half, own), full_z, preferred_element_type=F32)
    d_normed_z = after(d_normed_z, grad_flow)
    d_conv, d_raw, bias_grad, rate_grad, skip_grad = scan_backward(
        bc, skip_all, conved, tie(d_ssd, d_normed_z)[0], states, grad_flow.result, rows, seg_row, head_cols
    )
    head_grads = jnp.stack([jnp.sum(v, 1) for v in (rate_grad, skip_grad, bias_grad)])
    head_grads = jnp.pad(head_grads.reshape(1, -1), ((0, 7), (0, -head_grads.size % Q)))
    heads_flow = total(head_grads, count)
    first_pre = pre[:, :HALO].astype(F32)
    first_sig = sigmoid(first_pre)
    d_first = d_conv[:, :HALO].astype(F32) * (first_sig + first_pre * first_sig * (1.0 - first_sig))
    d_first = d_first[:, :16].astype(BF16).T
    beyond_flow = once(d_first, lambda a: lax.ppermute(a, "mp", [(1, 0)]))
    layer_recv = ahead(layer_flow.result, beyond_flow, heads_flow)
    layer_out = jnp.where(
        first_half, jnp.concatenate([layer_mine, layer_recv], 0), jnp.concatenate([layer_recv, layer_mine], 0)
    )
    layer_out = after(layer_out, beyond_flow, heads_flow)
    beyond = jnp.pad(beyond_flow.result.T, ((0, 0), (0, HALO - 16)))
    d_conv = ahead(tie(d_conv, own_out, layer_out)[0], heads_flow)
    d_proj, conv_sums = conv_backward(
        place_id, proj, pre, d_conv, beyond, d_raw, w_wide, conv_masks
    )
    d_proj = after(d_proj, heads_flow)
    small = spare_block(spare_sizes, count, conv_sums, gain_grad)
    tiles = stride // 256
    keep_a, sent_a = weight_grad(ahead(normed_t, heads_flow), d_proj, count, (0, tiles - 3))
    keep_a = after(keep_a, heads_flow)
    flow_a = sum_to_owners(keep_a, sent_a, count, "yxz")
    keep_b, sent_b = weight_grad(ahead(normed_t, flow_a, heads_flow), d_proj, count, (tiles - 3, tiles), small)
    keep_b = after(keep_b, flow_a, heads_flow)
    flow_b = sum_to_owners(keep_b, sent_b, count, "zxy")
    full_back = ahead(full_xbc, flow_a, flow_b, heads_flow)
    d_normed = d_normed_z + jnp.einsum(
        "yct,ydc->td", d_proj.reshape(2, stride, own), full_back, preferred_element_type=F32
    )
    d_normed = after(d_normed, flow_b, heads_flow)
    d_tokens, low_rows = norm_backward(place_id, d_normed, tokens, cotangent, gain_in)
    parts = [low_rows[k * 256 : (k + 1) * 256] for k in range(own // 256)]
    low_flows = [once(parts[0], swap)]
    mark = after(norm_gain, flow_a, flow_b, heads_flow, low_flows[0], also=(own_z,))
    for k in range(1, len(parts)):
        low_flows.append(once(tie(parts[k], mark)[0], swap))
        mark = after(mark, flow_a, flow_b, heads_flow, low_flows[k])
    own_xbc = jnp.concatenate([flow_a.finish(), flow_b.finish()], 1)
    head_grads = heads_flow.finish().reshape(-1)[: 6 * heads_half]
    d_tokens = fill_rows(place_id, d_tokens, [f.finish() for f in low_flows])

    own_xbc, own_dt, own_z, own_taps, own_bias, own_gain, product = finish(sizes, own_xbc, own_z, w_xbc, w_dt, w_z)
    own_out = own_out.astype(F32).T
    norms = norm_gain.shape[0]
    product = lax.dynamic_slice_in_dim(product[:, 0] + swap(product)[:, 0], my * norms, norms, 0)
    norm_mine = product / norm_gain.astype(F32)
    heads_mine = pick(head_grads.reshape(3, 2, heads_half), my, 1)
    return (
        layer_out,
        d_tokens,
        own_z,
        own_xbc,
        own_dt,
        own_out,
        own_taps,
        own_bias[0],
        own_gain[0],
        norm_mine,
        heads_mine[0],
        heads_mine[1],
        heads_mine[2],
    )


def solution(mesh):
    placed = (
        P("dp", None),
        P("dp"),
        P("dp", "mp"),
        P("dp", "mp"),
        P("dp", "mp"),
        P("mp", "dp"),
        P(None, ("mp", "dp")),
        P(("mp", "dp")),
        P(("mp", "dp")),
        P(("dp", "mp")),
        P("mp"),
        P("mp"),
        P("mp"),
        P("dp", "mp"),
    )
    return jax.shard_map(
        functools.partial(shards, count=mesh.shape["dp"]),
        mesh=mesh,
        in_specs=placed,
        out_specs=(
            P("dp", "mp"),
            P("dp", None),
            P("dp", "mp"),
            P("dp", "mp"),
            P("dp", "mp"),
            P("mp", "dp"),
            P(None, ("mp", "dp")),
            P(("mp", "dp")),
            P(("mp", "dp")),
            P(("dp", "mp")),
            P("mp"),
            P("mp"),
            P("mp"),
        ),
        check_vma=False,
    )
```

```python
import functools

import jax
import jax.numpy as jnp
from jax import lax
from jax.experimental import pallas as pl
from jax.experimental.pallas import tpu as pltpu
from jax.sharding import PartitionSpec as P

F32 = jnp.float32
BF16 = jnp.bfloat16
EPS = 1e-05
LOG2E = 1.4426950408889634
CAP = 60.0
Q = 128
HALO = 128
VMEM = 60 * 1024 * 1024


def dot(a, b, ca, cb, precision=None):
    return lax.dot_general(
        a, b, (((ca,), (cb,)), ((), ())), precision=precision, preferred_element_type=F32
    )


def takes(micros):
    return pl.CostEstimate(flops=0, transcendentals=0, bytes_accessed=int(micros * 3.0e6))


def xor_perm(count, bits):
    return [(i, i ^ bits) for i in range(count)]


def line_perm(pairs):
    return [(a * 4 + r, b * 4 + r) for a, b in pairs for r in range(4)]


ENDS_IN = ((1, 0), (2, 3))
ENDS_OUT = ((0, 1), (3, 2))
MIDDLE = ((1, 2), (2, 1))
PAIRS = ((0, 1), (1, 0), (2, 3), (3, 2))
SWAP = [(0, 1), (1, 0)]


def send_line(a, pairs):
    return lax.ppermute(a, "dp", line_perm(pairs))


def send_x(a):
    return lax.ppermute(a, "dp", xor_perm(16, 2))


def send_core(a):
    return lax.ppermute(a, "dp", xor_perm(16, 1))


def send_y(a):
    return lax.ppermute(a, "mp", SWAP)


def place_kernel(where, me_ref, *refs):
    pieces, out_ref, held, arrived, left = refs[:-4], refs[-4], refs[-3], refs[-2], refs[-1]
    me, my = me_ref[0], me_ref[1]
    inward, outward = [], []
    for piece, parts in zip(pieces, where):
        for k, (ry, rest) in enumerate(parts):
            n = len(inward)
            slot = out_ref.at[jnp.bitwise_xor(my, ry), jnp.bitwise_xor(me, rest)]
            inward.append(pltpu.make_async_copy(piece.at[k], held.at[n], arrived.at[n]))
            outward.append(pltpu.make_async_copy(held.at[n], slot, left.at[n]))
    for copy in inward:
        copy.start()
    for copy, further in zip(inward, outward):
        copy.wait()
        further.start()
    for copy in outward:
        copy.wait()


def place(pieces, where, me, my):
    rows, width = pieces[0].shape[1:]
    return pl.pallas_call(
        functools.partial(place_kernel, where),
        cost_estimate=takes(9),
        out_shape=jax.ShapeDtypeStruct((2, 16, rows, width), pieces[0].dtype),
        in_specs=[pl.BlockSpec(memory_space=pltpu.SMEM)]
        + [pl.BlockSpec(memory_space=pl.ANY)] * len(pieces),
        out_specs=pl.BlockSpec(memory_space=pl.ANY),
        scratch_shapes=[
            pltpu.VMEM((32, rows, width), pieces[0].dtype),
            pltpu.SemaphoreType.DMA((32,)),
            pltpu.SemaphoreType.DMA((32,)),
        ],
        compiler_params=pltpu.CompilerParams(vmem_limit_bytes=VMEM),
    )(jnp.stack([me, my]).astype(jnp.int32), *pieces)


def tie(*values):
    return lax.optimization_barrier(values)


def gather_now(shard, small, prepare, normalised, swapped):
    me, my = lax.axis_index("dp"), lax.axis_index("mp")
    near = send_line(shard, PAIRS)
    far_mid = send_line(shard, MIDDLE)
    small = small[None]
    for send in (send_x, send_core, send_y):
        small = jnp.concatenate([small, send(small)], 0)
    first = jnp.stack([shard, near])
    first_x, first_y = send_x(first), send_y(first)
    small, far_mid, near = tie(small, far_mid, near)
    across_end = send_line(far_mid, ENDS_IN)
    across_mid = send_line(near, MIDDLE)
    small_near, small_far = send_line(small, PAIRS), send_line(small, MIDDLE)
    across_end, across_mid, small_near, small_far = tie(across_end, across_mid, small_near, small_far)
    far_end = send_line(across_mid, ENDS_IN)
    small_across_end, small_across = send_line(small_far, ENDS_IN), send_line(small_near, MIDDLE)
    second = jnp.stack([across_end + across_mid, far_mid + far_end])
    second, first_x, first_y, small_across_end, small_across = tie(
        second, first_x, first_y, small_across_end, small_across
    )
    second_x, second_y = send_x(second), send_y(second)
    small_far_end = send_line(small_across, ENDS_IN)
    early = [first, first_x, first_y]
    early_core = [send_core(a) for a in early]
    small = jnp.concatenate([small, small_near, small_across_end + small_across, small_far + small_far_end], 0)
    prepared = prepare(small)
    second_x, second_y, first_x, second, *rest = tie(second_x, second_y, first_x, second, *early_core, *prepared)
    early_core, prepared = rest[:3], rest[3:]
    first_xy, second_xy = send_y(first_x), send_x(second_y)
    late = [second, second_x, second_y]
    late_core = [send_core(a) for a in late]
    rows = normalised(prepared)
    first_xy, second_xy, *rest = tie(first_xy, second_xy, *late_core, *rows)
    late_core, rows = rest[:3], rest[3:]
    last_core = [send_core(first_xy), send_core(second_xy)]
    pieces, where = [], []
    for own, other, pair, sides in (
        (early, early_core, 0, (0, 1, 2)),
        (late, late_core, 1, (0, 1, 2)),
        ([first_xy], last_core[:1], 0, (3,)),
        ([second_xy], last_core[1:], 1, (3,)),
    ):
        for rc, parts in enumerate((own, other)):
            pieces += parts
            where += [[(side // 2, (2 * pair + low) * 4 + (side % 2) * 2 + rc) for low in range(2)] for side in sides]
    return place(pieces, where, me, my), prepared, rows, swapped, (second_x, second_y)


def swap(a):
    return lax.ppermute(a, "mp", SWAP)


def gather_later(shard, other, marks):
    my = lax.axis_index("mp")
    pair = jnp.where(my == 0, jnp.stack([shard, other]), jnp.stack([other, shard]))
    if marks:
        pair = tie(pair, *marks)[0]
    return lax.all_gather(pair, "dp", axis=1, tiled=True)


class Flow:
    def __init__(self, steps=None, result=None):
        self.steps, self.result = steps, result
        self.sent, self.flying = [], []
        if steps is not None:
            self.sent, self.flying = next(steps)

    def move(self, got):
        try:
            self.sent, self.flying = self.steps.send(list(got))
        except StopIteration as stop:
            self.result = stop.value

    def finish(self):
        while self.result is None:
            self.move(self.flying)
        return self.result


def once(sent, send):
    def steps():
        (got,) = yield [sent], [send(sent)]
        return got

    return Flow(steps())


def ahead(value, *flows):
    sent = sum([f.sent for f in flows if f.result is None], [])
    return tie(value, *sent)[0] if sent else value


def after(value, *flows, also=()):
    live = [f for f in flows if f.result is None]
    if live:
        value, *got = tie(value, *sum([f.flying for f in live], []), *also)
        for f in live:
            count = len(f.flying)
            part, got = got[:count], got[count:]
            f.move(part)
    return value


def add(a, b):
    return (a.astype(F32) + b.astype(F32)).astype(a.dtype)


def pick(a, index, axis):
    return lax.dynamic_index_in_dim(a, index, axis, keepdims=False)


def line_steps(a, z):
    block = [pick(a, jnp.bitwise_xor(z, r), 0) for r in range(4)]
    (got,) = yield [block[3]], [send_line(block[3], ENDS_OUT)]
    into_near = add(block[2], got)
    out, got = yield [block[2], into_near], [send_line(block[2], ENDS_OUT), send_line(into_near, MIDDLE)]
    far, near = add(block[3], out), add(block[1], got)
    got, out = yield [far, near], [send_line(far, MIDDLE), send_line(near, PAIRS)]
    return (block[0].astype(F32) + got.astype(F32) + out.astype(F32)).astype(a.dtype)


def halve_step(a, axis, bit, send):
    sent = pick(a, 1 - bit, axis)
    return pick(a, bit, axis), sent, send(sent)


def stages(a, order, my, z, x):
    names = ["y", "z", "x"]
    for name in order:
        axis = names.index(name)
        names.remove(name)
        if name == "z":
            a = yield from line_steps(jnp.moveaxis(a, axis, 0), z)
        else:
            bit, send = (my, send_y) if name == "y" else (x, send_x)
            keep, sent, flying = halve_step(a, axis, bit, send)
            (got,) = yield [sent], [flying]
            a = add(keep, got)
    return a


def scatter_steps(keep, sent, order):
    rows, width = keep.shape[2:]
    me, my = lax.axis_index("dp"), lax.axis_index("mp")
    z, x = me // 4, (me // 2) % 2
    (got,) = yield [sent], [send_core(sent)]
    a = add(keep, got).reshape(2, 4, 2, rows, width)
    return (yield from stages(a, order, my, z, x))


def sum_to_owners(keep, sent, count, order):
    if count == 16:
        return Flow(scatter_steps(keep, sent, order))
    core = lax.axis_index("dp") % 2
    pair = jnp.stack([keep, sent], 2)
    grad = jnp.where(core == 0, pair, pair[:, :, ::-1])
    mine = lax.psum_scatter(grad, "mp", scatter_dimension=0, tiled=False)
    mine = mine.reshape((-1,) + keep.shape[2:])
    return Flow(result=lax.psum_scatter(mine, "dp", scatter_dimension=0, tiled=False))


def total_steps(a):
    for send in (send_core, send_x, send_y, lambda v: send_line(v, PAIRS)):
        (got,) = yield [a], [send(a)]
        a = a + got
    (far,) = yield [a], [send_line(a, MIDDLE)]
    (further,) = yield [far], [send_line(far, ENDS_IN)]
    return a + far + further


def total(a, count):
    if count == 16:
        return Flow(total_steps(a))
    return Flow(result=lax.psum(a, ("dp", "mp")))


def sigmoid(v):
    return 0.5 * jnp.tanh(0.5 * v) + 0.5


def mask_kernel(place_ref, seg_ref, conv_ref, scan_ref, own_ref):
    seg = jnp.broadcast_to(seg_ref[...].astype(F32), (8, seg_ref.shape[1]))
    total = seg.shape[1]
    own = total // 2
    first = place_ref[0] == 0
    lane = lax.broadcasted_iota(jnp.int32, seg.shape, 1)
    conv_ref[...] = jnp.zeros_like(conv_ref)
    for k in (1, 2, 3):
        same = jnp.where((lane >= k) & (pltpu.roll(seg, k, 1) == seg), 1.0, 0.0)
        conv_ref[k - 1 : k, :own] = jnp.where(first, same[:1, :own], same[:1, own:])
        conv_ref[k - 1 : k, own:] = jnp.where(first, same[:1, own : own + HALO], 0.0)
    mine = jnp.where(first, seg[:1, :own], seg[:1, own:])
    own_ref[...] = mine
    outside = jnp.where(first, -2.0, seg[:1, own - 1 : own])
    scan_ref[...] = jnp.zeros_like(scan_ref)
    before, final = outside, mine[:, own - 1 :]
    for c in range(own // Q):
        span = slice(c * Q, (c + 1) * Q)
        here = mine[:, span]
        last = here[:, Q - 1 :]
        flags = (here == before, here == last, jnp.broadcast_to(last, here.shape) == before, here == final, here == outside)
        for k, flag in enumerate(flags):
            scan_ref[k : k + 1, span] = jnp.where(flag, 1.0, 0.0)
        before = last


def row_masks(place_id, token_seq):
    total = token_seq.shape[0]
    own = total // 2
    return pl.pallas_call(
        mask_kernel,
        cost_estimate=takes(2),
        in_specs=[pl.BlockSpec(memory_space=pltpu.SMEM), pl.BlockSpec(memory_space=pltpu.VMEM)],
        out_shape=[
            jax.ShapeDtypeStruct((8, own + HALO), F32),
            jax.ShapeDtypeStruct((8, own), F32),
            jax.ShapeDtypeStruct((1, own), F32),
        ],
    )(place_id, token_seq[None, :])


def param_kernel(sizes, by_distance, me_ref, got_ref, w_ref, gain_ref, norm_ref, tall_ref, head_ref, scr):
    per, gains, norms, heads, stride = sizes
    count = got_ref.shape[0] // 2
    me, my = me_ref[0], me_ref[1]
    for r in range(2 * count):
        if by_distance:
            rz, ry, rest = r // 8, (r // 4) % 2, (r // 2) % 2 + (r % 2) * 2
            at = jnp.bitwise_xor(my, ry) * count + jnp.bitwise_xor(me, rz * 4 + rest)
        else:
            at = r
        scr[at] = got_ref[r].astype(F32)
    w_ref[...] = jnp.zeros_like(w_ref)
    head_ref[...] = jnp.zeros_like(head_ref)
    for y in range(2):
        for group in range(count // 8):
            tiles = [scr[y * count + group * 8 + d] for d in range(8)]
            turned = jnp.concatenate(tiles, 0).T
            for d in range(8):
                device = group * 8 + d
                at = y * stride + device * per
                for k in range(5):
                    column = turned[:per, d * 16 + k : d * 16 + k + 1]
                    w_ref[at : at + per, k * Q : (k + 1) * Q] = jnp.broadcast_to(column, (per, Q))
                column = turned[:gains, d * 16 + 5 : d * 16 + 6]
                at = (y * count + device) * gains
                gain_ref[at : at + gains, :] = jnp.broadcast_to(column, (gains, Q))
                at = 2 * device + y
                norm_ref[at : at + 1, :] = tiles[d][6:7]
                column = turned[:norms, d * 16 + 6 : d * 16 + 7]
                tall_ref[at * norms : (at + 1) * norms, :] = jnp.broadcast_to(column, (norms, Q))
            if group == 0:
                column = turned[:, 7:8] + turned[:, 8:9] + turned[:, 9:10]
                for j in range(3):
                    head_ref[y * heads : (y + 1) * heads, j : j + 1] = column[j * heads : (j + 1) * heads]


def parameters(got, sizes, by_distance):
    per, gains, norms, heads, stride = sizes
    count = got.shape[0] // 2
    me, my = lax.axis_index("dp"), lax.axis_index("mp")
    wide, gain, norm, tall, head = pl.pallas_call(
        functools.partial(param_kernel, sizes, by_distance),
        cost_estimate=takes(10),
        in_specs=[pl.BlockSpec(memory_space=pltpu.SMEM), pl.BlockSpec(memory_space=pltpu.VMEM)],
        out_shape=[
            jax.ShapeDtypeStruct((2 * stride, 5 * Q), F32),
            jax.ShapeDtypeStruct((2 * count * gains, Q), F32),
            jax.ShapeDtypeStruct((2 * count, Q), F32),
            jax.ShapeDtypeStruct((2 * count * norms, Q), F32),
            jax.ShapeDtypeStruct((2 * heads, 8), F32),
        ],
        scratch_shapes=[pltpu.VMEM((2 * count, 16, Q), F32)],
        compiler_params=pltpu.CompilerParams(vmem_limit_bytes=VMEM),
    )(jnp.stack([me, my]).astype(jnp.int32), got)
    return wide, gain, norm[:, :norms].reshape(1, -1), tall, head


def norm_kernel(place_ref, x_ref, gain_ref, window_ref, own_ref):
    mine = pl.program_id(0) - place_ref[0]
    x = x_ref[...].astype(F32)
    scaled = x * lax.rsqrt(jnp.mean(x * x, axis=1, keepdims=True) + EPS)
    normed = (scaled.T * gain_ref[...]).astype(BF16)
    window_ref[...] = normed

    @pl.when((mine >= 0) & (mine < pl.num_programs(0) - 1))
    def _():
        own_ref[...] = normed


def normalise(place_id, tokens, gain):
    total, width = tokens.shape
    own = total // 2
    blocks = own // Q
    return pl.pallas_call(
        norm_kernel,
        cost_estimate=takes(10),
        grid_spec=pltpu.PrefetchScalarGridSpec(
            num_scalar_prefetch=1,
            grid=(blocks + 1,),
            in_specs=[
                pl.BlockSpec((Q, width), lambda i, place: (i + place[0] * (blocks - 1), 0)),
                pl.BlockSpec((width, Q), lambda i, place: (0, 0)),
            ],
            out_specs=[
                pl.BlockSpec((width, Q), lambda i, place: (0, i)),
                pl.BlockSpec((width, Q), lambda i, place: (0, jnp.clip(i - place[0], 0, blocks - 1))),
            ],
        ),
        out_shape=[
            jax.ShapeDtypeStruct((width, own + HALO), BF16),
            jax.ShapeDtypeStruct((width, own), BF16),
        ],
        compiler_params=pltpu.CompilerParams(vmem_limit_bytes=VMEM),
    )(place_id, tokens, gain)


def cotangent_kernel(place_ref, mine_ref, other_ref, seg_ref, all_ref, turned_ref):
    first = place_ref[0] == 0
    mine, other = mine_ref[...].astype(F32), other_ref[...].astype(F32)
    whole = jnp.concatenate([jnp.where(first, mine, other), jnp.where(first, other, mine)], 1)
    all_ref[...] = whole.astype(BF16)
    turned_ref[...] = (whole.T * jnp.where(seg_ref[...] >= 0.0, 1.0, 0.0)).astype(BF16)


def cotangents(place_id, d_out, other, seg):
    own, half = other.shape
    blocks = own // Q
    return pl.pallas_call(
        cotangent_kernel,
        cost_estimate=takes(8),
        grid_spec=pltpu.PrefetchScalarGridSpec(
            num_scalar_prefetch=1,
            grid=(blocks,),
            in_specs=[
                pl.BlockSpec((Q, half), lambda i, place: (i + place[0] * blocks, 0)),
                pl.BlockSpec((Q, half), lambda i, place: (i, 0)),
                pl.BlockSpec((1, Q), lambda i, place: (0, i)),
            ],
            out_specs=[
                pl.BlockSpec((Q, 2 * half), lambda i, place: (i, 0)),
                pl.BlockSpec((2 * half, Q), lambda i, place: (0, i)),
            ],
        ),
        out_shape=[
            jax.ShapeDtypeStruct((own, 2 * half), BF16),
            jax.ShapeDtypeStruct((2 * half, own), BF16),
        ],
        compiler_params=pltpu.CompilerParams(vmem_limit_bytes=VMEM),
    )(place_id, d_out, other, seg)


def norm_back_kernel(place_ref, d_proj_ref, w_ref, d_z_ref, x_ref, cot_ref, gain_ref, *refs):
    out_ref, low_refs = refs[-3], refs[-2:]
    half = w_ref.shape[2]
    turned = dot(w_ref[0], d_proj_ref[:half, :], 1, 0) + dot(w_ref[1], d_proj_ref[half:, :], 1, 0)
    x = x_ref[...].astype(F32)
    inverse = lax.rsqrt(jnp.mean(x * x, axis=1, keepdims=True) + EPS)
    scaled = x * inverse
    d_scaled = (d_z_ref[...] + turned.T) * gain_ref[...]
    inner = jnp.mean(d_scaled * scaled, axis=1, keepdims=True)
    rows = cot_ref[...].astype(F32) + inverse * (d_scaled - scaled * inner)
    out_ref[...] = rows
    for k, low_ref in enumerate(low_refs):

        @pl.when(pl.program_id(0) == k)
        def _(low_ref=low_ref):
            low_ref[...] = rows.astype(BF16)


def norm_backward(place_id, d_proj, w, d_z, tokens, cotangent, gain, begin, whole=None):
    total, width = tokens.shape
    own = total // 2
    tile = own // 4
    here = pl.BlockSpec((tile, width), lambda i, place: (i + begin, 0))
    among = pl.BlockSpec((tile, width), lambda i, place: (i + begin + place[0] * 4, 0))
    more = [] if whole is None else [whole]
    return pl.pallas_call(
        norm_back_kernel,
        cost_estimate=takes(14),
        grid_spec=pltpu.PrefetchScalarGridSpec(
            num_scalar_prefetch=1,
            grid=(2,),
            in_specs=[
                pl.BlockSpec((d_proj.shape[0], tile), lambda i, place: (0, i + begin)),
                pl.BlockSpec(w.shape, lambda i, place: (0, 0, 0)),
                here,
                among,
                here,
                pl.BlockSpec((1, width), lambda i, place: (0, 0)),
            ]
            + [pl.BlockSpec(memory_space=pl.ANY)] * len(more),
            out_specs=[among] + [pl.BlockSpec((tile, width), lambda i, place: (0, 0))] * 2,
        ),
        out_shape=[jax.ShapeDtypeStruct((total, width), F32)] + [jax.ShapeDtypeStruct((tile, width), BF16)] * 2,
        input_output_aliases={7: 0} if more else {},
        compiler_params=pltpu.CompilerParams(vmem_limit_bytes=VMEM),
    )(place_id, d_proj, w, d_z, tokens, cotangent, gain, *more)


def fill_kernel(place_ref, *refs):
    out_ref = refs[-1]
    at = pl.program_id(0)
    for k, part in enumerate(refs[:-2]):

        @pl.when(at == k)
        def _(part=part):
            out_ref[...] = part[...].astype(F32)


def fill_rows(place_id, whole, parts):
    blocks = len(parts)
    rows, width = parts[0].shape
    return pl.pallas_call(
        fill_kernel,
        cost_estimate=takes(5),
        grid_spec=pltpu.PrefetchScalarGridSpec(
            num_scalar_prefetch=1,
            grid=(blocks,),
            in_specs=[pl.BlockSpec((rows, width), lambda i, place: (0, 0))] * blocks
            + [pl.BlockSpec(memory_space=pl.ANY)],
            out_specs=pl.BlockSpec((rows, width), lambda i, place: (i + (1 - place[0]) * blocks, 0)),
        ),
        out_shape=jax.ShapeDtypeStruct(whole.shape, F32),
        input_output_aliases={1 + blocks: 0},
        compiler_params=pltpu.CompilerParams(vmem_limit_bytes=VMEM),
    )(place_id, *parts, whole)


def finish_kernel(sizes, xbc_ref, z_ref, w_xbc_ref, w_dt_ref, w_z_ref, own_xbc_ref, own_dt_ref, own_z_ref, taps_ref, bias_ref, gain_ref, product_ref):
    conv = w_xbc_ref.shape[1]
    heads = w_dt_ref.shape[1]
    xbc, z = xbc_ref[:, :conv].astype(F32), z_ref[...].astype(F32)
    last = xbc_ref[:, conv:].astype(F32)
    dt = last[:, :heads]
    own_xbc_ref[...] = xbc
    own_dt_ref[...] = dt
    own_z_ref[...] = z
    taps, per = taps_ref.shape
    taps_ref[...] = last[:taps, heads : heads + per]
    bias_ref[...] = last[taps : taps + 1, heads : heads + per]
    gain_ref[...] = last[taps + 1 : taps + 2, heads : heads + gain_ref.shape[1]]
    product = jnp.sum(xbc * w_xbc_ref[...].astype(F32), axis=1, keepdims=True)
    product += jnp.sum(z * w_z_ref[...].astype(F32), axis=1, keepdims=True)
    product += jnp.sum(dt * w_dt_ref[...].astype(F32), axis=1, keepdims=True)
    product_ref[...] = jnp.broadcast_to(product, product_ref.shape)


def finish(sizes, own_xbc, own_z, w_xbc, w_dt, w_z):
    rows = w_z.shape[0]
    return pl.pallas_call(
        functools.partial(finish_kernel, sizes),
        cost_estimate=takes(3),
        out_shape=[
            jax.ShapeDtypeStruct(w_xbc.shape, F32),
            jax.ShapeDtypeStruct(w_dt.shape, F32),
            jax.ShapeDtypeStruct(w_z.shape, F32),
            jax.ShapeDtypeStruct((4, sizes[0]), F32),
            jax.ShapeDtypeStruct((1, sizes[0]), F32),
            jax.ShapeDtypeStruct((1, sizes[1]), F32),
            jax.ShapeDtypeStruct((rows, Q), F32),
        ],
        compiler_params=pltpu.CompilerParams(vmem_limit_bytes=VMEM),
    )(own_xbc, own_z, w_xbc, w_dt, w_z)


def spare_kernel(sizes, conv_ref, gain_ref, out_ref):
    per, gains, norms, heads, stride, skip = sizes
    count = out_ref.shape[1]
    lane = lax.broadcasted_iota(jnp.int32, (1, Q), 1)

    def turned(v):
        return jnp.concatenate([v, jnp.zeros((Q - v.shape[0], Q), F32)], 0).T

    def moved(row, size):
        return jnp.where((lane >= skip) & (lane < skip + size), pltpu.roll(row, skip, 1), 0.0)

    for y in range(2):
        for d in range(count):
            at = y * stride + d * per
            rows = [moved(turned(conv_ref[at : at + per, :])[k : k + 1], per) for k in range(5)]
            at = (y * count + d) * gains
            total = jnp.sum(turned(gain_ref[at : at + gains, :]), axis=0, keepdims=True)
            rows += [moved(total, gains), jnp.zeros((10, Q), F32)]
            out_ref[y, d] = jnp.concatenate(rows, 0)


def spare_block(sizes, count, conv_sums, gain_grad):
    return pl.pallas_call(
        functools.partial(spare_kernel, sizes),
        cost_estimate=takes(4),
        out_shape=jax.ShapeDtypeStruct((2, count, 16, Q), F32),
        compiler_params=pltpu.CompilerParams(vmem_limit_bytes=VMEM),
    )(conv_sums, gain_grad)


def grad_kernel(core_ref, left_ref, right_ref, *refs):
    spare_ref = refs[0] if len(refs) == 4 else None
    keep_ref, send_ref, scr = refs[-3:]
    parts, rows, tile = scr.shape
    scr[...] = dot(left_ref[...], right_ref[...], 1, 1).astype(BF16).reshape(scr.shape)
    if spare_ref is not None:

        @pl.when(pl.program_id(1) == pl.num_programs(1) - 1)
        def _():
            for p in range(parts):
                old = scr[p, :16, tile - Q :].astype(F32)
                scr[p, :16, tile - Q :] = (old + spare_ref[0, p]).astype(BF16)

    core = core_ref[0]
    for p in range(parts // 2):
        keep_ref[0, p] = scr[2 * p + core]
        send_ref[0, p] = scr[2 * p + 1 - core]


def grad_plain_kernel(left_ref, right_ref, out_ref):
    out_ref[...] = dot(left_ref[...], right_ref[...], 1, 1).astype(BF16).reshape(out_ref.shape)


def weight_grad_sum(left, right, count):
    width, rows = left.shape
    channels = right.shape[0] // 2
    tile = 256
    grad = pl.pallas_call(
        grad_plain_kernel,
        cost_estimate=takes(17),
        grid=(2, channels // tile),
        in_specs=[
            pl.BlockSpec((width, rows), lambda y, k: (0, 0)),
            pl.BlockSpec((tile, rows), lambda y, k: (y * (channels // tile) + k, 0)),
        ],
        out_specs=pl.BlockSpec((count, 1, width // count, tile), lambda y, k: (0, y, 0, k)),
        out_shape=jax.ShapeDtypeStruct((count, 2, width // count, channels), BF16),
        compiler_params=pltpu.CompilerParams(vmem_limit_bytes=VMEM),
    )(left, right)
    return grad, lax.psum_scatter(
        grad.reshape(-1, channels), ("dp", "mp"), scatter_dimension=0, tiled=True
    )


def weight_grad(left, right, count, tiles, spare=None):
    width, rows = left.shape
    tile = 256
    per_half = right.shape[0] // 2 // tile
    begin, end = tiles
    shape = (2, count // 2, width // count, (end - begin) * tile)
    block = pl.BlockSpec((1, count // 2, width // count, tile), lambda y, k: (y, 0, 0, k))
    core = (lax.axis_index("dp") % 2).reshape(1).astype(jnp.int32)
    more = [] if spare is None else [pl.BlockSpec((1,) + spare.shape[1:], lambda y, k: (y, 0, 0, 0))]
    return pl.pallas_call(
        grad_kernel,
        cost_estimate=takes(12),
        grid=(2, end - begin),
        in_specs=[
            pl.BlockSpec(memory_space=pltpu.SMEM),
            pl.BlockSpec((width, rows), lambda y, k: (0, 0)),
            pl.BlockSpec((tile, rows), lambda y, k: (y * per_half + begin + k, 0)),
        ]
        + more,
        out_specs=[block, block],
        out_shape=[jax.ShapeDtypeStruct(shape, BF16)] * 2,
        scratch_shapes=[pltpu.VMEM((count, width // count, tile), BF16)],
        compiler_params=pltpu.CompilerParams(vmem_limit_bytes=VMEM),
    )(core, left, right, *([] if spare is None else [spare]))


def rows_kernel(raw_ref, head_ref, mask_ref, *outs):
    cum_ref, shift_ref, into_ref, onto_ref, keep_ref, step_ref, slope_ref, ratio_ref, start_ref, end_ref = outs
    chunks = raw_ref.shape[1] // Q
    rate = -jnp.exp(head_ref[:, 0:1])
    bias = head_ref[:, 1:2]
    source = lax.broadcasted_iota(jnp.int32, (Q, Q), 0)
    target = lax.broadcasted_iota(jnp.int32, (Q, Q), 1)
    upto = (source <= target).astype(F32)
    totals, sums, log_steps, steps = [], [], [], []
    for c in range(chunks):
        span = slice(c * Q, (c + 1) * Q)
        v = raw_ref[:, span] + bias
        tail = jnp.log1p(jnp.exp(-jnp.abs(v)))
        step = jnp.maximum(v, 0.0) + tail
        low = v < -20.0
        log_step = jnp.where(low, v, jnp.log(jnp.where(low, 1.0, step)))
        slope = 1.0 / (1.0 + jnp.exp(-v))
        decay = step * rate * LOG2E
        cum = dot(decay, upto, 1, 0, lax.Precision.HIGHEST)
        total = cum[:, Q - 1 : Q]
        shift = cum - log_step * LOG2E
        cum_ref[:, span] = cum
        shift_ref[:, span] = shift
        step_ref[:, span] = step
        slope_ref[:, span] = slope
        ratio_ref[:, span] = jnp.where(low, 1.0, slope / jnp.where(low, 1.0, step))
        into_ref[:, span] = jnp.exp2(cum) * mask_ref[0:1, span]
        onto_ref[:, span] = jnp.exp2(total - cum) * step * mask_ref[1:2, span]
        keep_ref[:, span] = jnp.exp2(total) * mask_ref[2:3, span]
        totals.append(total)
        sums.append(cum)
        steps.append(step)
    before = jnp.zeros_like(totals[0])
    for c in range(chunks):
        span = slice(c * Q, (c + 1) * Q)
        start_ref[:, span] = jnp.exp2(before + sums[c]) * mask_ref[4:5, span]
        before = before + totals[c]
    after = jnp.zeros_like(totals[0])
    for c in reversed(range(chunks)):
        span = slice(c * Q, (c + 1) * Q)
        end_ref[:, span] = jnp.exp2(after + totals[c] - sums[c]) * steps[c] * mask_ref[3:4, span]
        after = after + totals[c]


def head_rows(raw, heads, masks):
    shape = jax.ShapeDtypeStruct(raw.shape, F32)
    return pl.pallas_call(
        rows_kernel,
        cost_estimate=takes(3),
        out_shape=[shape] * 10,
        compiler_params=pltpu.CompilerParams(vmem_limit_bytes=VMEM),
    )(raw, heads, masks)


def wide_columns(w_ref, rows):
    return [w_ref[rows, k * Q : (k + 1) * Q] for k in range(5)]


def conv_kernel(place_ref, proj_ref, w_ref, mask_ref, end_ref, out_ref, pre_ref, state_ref, b_scr, x_scr):
    s = pl.program_id(0)
    channels, own = out_ref.shape
    at = pl.multiple_of(place_ref[0] * HALO, HALO)
    size = 64

    def strip(i, carry):
        rows = pl.ds(pl.multiple_of(i * size, size), size)
        wide = wide_columns(w_ref, rows)
        before = proj_ref[rows, pl.ds(pl.multiple_of(jnp.maximum(at - Q, 0), Q), Q)].astype(F32)
        lane = lax.broadcasted_iota(jnp.int32, (size, Q), 1)
        last = [pltpu.roll(before, k, 1) for k in (1, 2, 3)]
        weight = end_ref[pl.ds(jnp.clip((s - 1) * 4 + i, 0, end_ref.shape[0] - 1), 1), :]
        for j in range(own // Q):
            now = proj_ref[rows, pl.ds(pl.multiple_of(at + j * Q, Q), Q)].astype(F32)
            span = slice(j * Q, (j + 1) * Q)
            pre = wide[4] + wide[3] * now
            for k in (1, 2, 3):
                rolled = pltpu.roll(now, k, 1)
                pre = pre + wide[3 - k] * (jnp.where(lane < k, last[k - 1], rolled) * mask_ref[k - 1 : k, span])
                last[k - 1] = rolled
            act = pre * sigmoid(pre)
            pre_ref[rows, span] = pre.astype(BF16)
            out_ref[rows, span] = act.astype(BF16)
            x_scr[rows, span] = (act * weight[:, span]).astype(BF16)
        return carry

    lax.fori_loop(0, channels // size, strip, 0)

    @pl.when(s == 0)
    def _():
        b_scr[...] = out_ref[:Q, :].astype(F32).T.astype(BF16)

    @pl.when((s > 0) & (s < pl.num_programs(0) - 1))
    def _():
        state_ref[...] = dot(x_scr[...], b_scr[...], 1, 0).astype(state_ref.dtype)


def conv_forward(place_id, proj, w_wide, masks, end_rows):
    channels, window = proj.shape
    own = window - HALO
    blocks = channels // 256
    half = blocks // 2

    def order(s):
        return jnp.where(s == 0, half - 1, jnp.where(s < half, s - 1, s))

    return pl.pallas_call(
        conv_kernel,
        cost_estimate=takes(25),
        grid=(blocks,),
        in_specs=[
            pl.BlockSpec(memory_space=pltpu.SMEM),
            pl.BlockSpec((256, window), lambda s: (order(s), 0)),
            pl.BlockSpec((256, 5 * Q), lambda s: (order(s), 0)),
            pl.BlockSpec(masks.shape, lambda s: (0, 0)),
            pl.BlockSpec(end_rows.shape, lambda s: (0, 0)),
        ],
        out_specs=[
            pl.BlockSpec((256, own), lambda s: (order(s), 0)),
            pl.BlockSpec((256, own), lambda s: (order(s), 0)),
            pl.BlockSpec((256, Q), lambda s: (jnp.clip(s - 1, 0, blocks - 3), 0)),
        ],
        out_shape=[
            jax.ShapeDtypeStruct((channels, own), BF16),
            jax.ShapeDtypeStruct((channels, own), BF16),
            jax.ShapeDtypeStruct(((blocks - 2) * 256, Q), BF16),
        ],
        scratch_shapes=[pltpu.VMEM((own, Q), BF16), pltpu.VMEM((256, own), BF16)],
        compiler_params=pltpu.CompilerParams(vmem_limit_bytes=VMEM),
    )(place_id, proj, w_wide, masks, end_rows)


def chunk_scores(conv_ref, bc, seg_ref):
    inner_half, stride = bc
    b_t = conv_ref[inner_half : inner_half + Q, :]
    c_t = conv_ref[stride + inner_half : stride + inner_half + Q, :]
    b_m = b_t.astype(F32).T.astype(BF16)
    scores = dot(b_m, c_t, 1, 0)
    source = lax.broadcasted_iota(jnp.int32, (Q, Q), 0)
    target = lax.broadcasted_iota(jnp.int32, (Q, Q), 1)
    seg = jnp.broadcast_to(seg_ref[...], (Q, Q))
    allowed = (source <= target) & (seg.T == seg)
    return b_t, c_t, b_m, jnp.where(allowed, scores, 0.0), allowed


def columns_of(shift_ref, col_scr):
    heads = shift_ref.shape[0]
    padded = jnp.concatenate([shift_ref[...], jnp.zeros((Q - heads, Q), F32)], 0).T
    for g in range(heads // 8):
        col_scr[g] = padded[:, g * 8 : (g + 1) * 8]


def scan_kernel(
    bc, skip_ref, conv_ref, z_ref, cum_ref, shift_ref, into_ref, onto_ref, keep_ref, seg_ref,
    gain_ref, first_ref, out_ref, ssd_ref, scale_ref, states_ref, state, gated, col_scr,
):
    inner_half, stride = bc
    groups = 2 * inner_half // 512

    @pl.when(pl.program_id(0) == 0)
    def _():
        state[...] = first_ref[...].astype(F32)

    _, c_t, b_m, scores, _ = chunk_scores(conv_ref, bc, seg_ref)
    columns_of(shift_ref, col_scr)

    def group(g, squares):
        at = pl.multiple_of(g * 512, 512)
        x_at = pl.multiple_of(g * 512 + jnp.where(g >= groups // 2, stride - inner_half, 0), 256)
        held = state[pl.ds(at, 512), :].astype(BF16)
        states_ref[0, pl.ds(at, 512), :] = held
        from_state = dot(held, c_t, 1, 0)
        cols = col_scr[g]
        parts = []
        for k in range(8):
            h = g * 8 + k
            x = conv_ref[pl.ds(x_at + k * 64, 64), :]
            spread = jnp.minimum(cum_ref[pl.ds(h, 1), :] - cols[:, k : k + 1], CAP)
            mixing = (jnp.exp2(spread) * scores).astype(BF16)
            xf = x.astype(F32)
            y = dot(x, mixing, 1, 0) + from_state[k * 64 : (k + 1) * 64] * into_ref[pl.ds(h, 1), :] + skip_ref[h] * xf
            z = z_ref[pl.ds(at + k * 64, 64), :].astype(F32)
            g_out = y * (z * sigmoid(z))
            squares = squares + g_out * g_out
            ssd_ref[pl.ds(at + k * 64, 64), :] = y.astype(BF16)
            gated[pl.ds(at + k * 64, 64), :] = g_out
            parts.append((xf * onto_ref[pl.ds(h, 1), :]).astype(BF16))
        fresh = dot(jnp.concatenate(parts, 0), b_m, 1, 0)
        for k in range(8):
            rows = pl.ds(at + k * 64, 64)
            state[rows, :] = state[rows, :] * keep_ref[pl.ds(g * 8 + k, 1), :] + fresh[k * 64 : (k + 1) * 64]
        return squares

    squares = lax.fori_loop(0, groups, group, jnp.zeros((64, Q), F32))
    scale = lax.rsqrt(jnp.sum(squares, axis=0, keepdims=True) / (2 * inner_half) + EPS)
    scale_ref[...] = scale

    def finish(g, carry):
        rows = pl.ds(pl.multiple_of(g * 512, 512), 512)
        out_ref[rows, :] = (gated[rows, :] * scale * gain_ref[rows, :]).astype(BF16)
        return carry

    lax.fori_loop(0, groups, finish, 0)


def scan_forward(bc, skip, conv, z, rows, seg, gain, first):
    inner = 2 * bc[0]
    channels, own = conv.shape
    chunks = own // Q
    heads = inner // 64
    row_spec = pl.BlockSpec((heads, Q), lambda c: (0, c))
    whole = pl.BlockSpec((inner, Q), lambda c: (0, 0))
    tile = pl.BlockSpec((inner, Q), lambda c: (0, c))
    cum, shift, into, onto, keep = rows[:5]
    return pl.pallas_call(
        functools.partial(scan_kernel, bc),
        cost_estimate=takes(29),
        grid=(chunks,),
        in_specs=[
            pl.BlockSpec(memory_space=pltpu.SMEM),
            pl.BlockSpec((channels, Q), lambda c: (0, c)),
            tile,
            row_spec, row_spec, row_spec, row_spec, row_spec,
            pl.BlockSpec((1, Q), lambda c: (0, c)),
            whole, whole,
        ],
        out_specs=[tile, tile, pl.BlockSpec((1, Q), lambda c: (0, c)), pl.BlockSpec((1, inner, Q), lambda c: (c, 0, 0))],
        out_shape=[
            jax.ShapeDtypeStruct((inner, own), BF16),
            jax.ShapeDtypeStruct((inner, own), BF16),
            jax.ShapeDtypeStruct((1, own), F32),
            jax.ShapeDtypeStruct((chunks, inner, Q), BF16),
        ],
        scratch_shapes=[pltpu.VMEM((inner, Q), F32), pltpu.VMEM((inner, Q), F32), pltpu.VMEM((heads // 8, Q, 8), F32)],
        compiler_params=pltpu.CompilerParams(vmem_limit_bytes=VMEM),
    )(skip, conv, z, cum, shift, into, onto, keep, seg, gain, first)


def gate_back_kernel(
    d_unit_ref, ssd_ref, z_ref, scale_ref, gain_ref, start_ref, c_ref, d_ssd_ref, d_gate_ref, gain_grad_ref, first_grad_ref, into, first_scr
):
    inner, width = ssd_ref.shape
    size = 64

    @pl.when(pl.program_id(0) == 0)
    def _():
        gain_grad_ref[...] = jnp.zeros_like(gain_grad_ref)
        first_scr[...] = jnp.zeros_like(first_scr)

    scale = scale_ref[...]

    def gain_of(rows):
        return jnp.concatenate([gain_ref[rows, :]] * (width // Q), 1)

    def look(g, cross):
        rows = pl.ds(pl.multiple_of(g * size, size), size)
        z = z_ref[rows, :].astype(F32)
        unit = ssd_ref[rows, :].astype(F32) * (z * sigmoid(z)) * scale
        product = d_unit_ref[rows, :].astype(F32) * unit
        gain_grad_ref[rows, :] += sum(product[:, k * Q : (k + 1) * Q] for k in range(width // Q))
        product = product * gain_of(rows)
        return cross + jnp.sum(product.reshape(size // 8, 8, width), axis=0)

    cross = lax.fori_loop(0, inner // size, look, jnp.zeros((8, width), F32))
    cross = jnp.sum(cross, axis=0, keepdims=True) / inner

    def head(h, carry):
        rows = pl.ds(pl.multiple_of(h * size, size), size)
        z = z_ref[rows, :].astype(F32)
        ssd = ssd_ref[rows, :].astype(F32)
        sig = sigmoid(z)
        act = z * sig
        unit = ssd * act * scale
        d_gated = scale * (d_unit_ref[rows, :].astype(F32) * gain_of(rows) - unit * cross)
        d_ssd = d_gated * act
        d_ssd_ref[rows, :] = d_ssd.astype(BF16)
        d_gate_ref[rows, :] = (d_gated * ssd * (sig + act * (1.0 - sig))).astype(BF16)
        into[rows, :] = (d_ssd * start_ref[pl.ds(h, 1), :]).astype(BF16)
        return carry

    lax.fori_loop(0, inner // size, head, 0)
    c_m = c_ref[...].astype(F32).T.astype(BF16)

    def sums(g, carry):
        rows = pl.ds(pl.multiple_of(g * 512, 512), 512)
        first_scr[rows, :] += dot(into[rows, :], c_m, 1, 0)
        return carry

    lax.fori_loop(0, inner // 512, sums, 0)

    @pl.when(pl.program_id(0) == pl.num_programs(0) - 1)
    def _():
        first_grad_ref[...] = first_scr[...].astype(BF16)


def gate_backward(bc, d_unit, ssd, z, scale, gain, start, conv):
    inner, own = ssd.shape
    heads = inner // 64
    width = 2 * Q
    tile = pl.BlockSpec((inner, width), lambda c: (0, c))
    whole = pl.BlockSpec((inner, Q), lambda c: (0, 0))
    c_block = (bc[0] + bc[1]) // Q
    return pl.pallas_call(
        gate_back_kernel,
        cost_estimate=takes(32),
        grid=(own // width,),
        in_specs=[
            tile, tile, tile,
            pl.BlockSpec((1, width), lambda c: (0, c)),
            whole,
            pl.BlockSpec((heads, width), lambda c: (0, c)),
            pl.BlockSpec((Q, width), lambda c: (c_block, c)),
        ],
        out_specs=[tile, tile, whole, whole],
        out_shape=[
            jax.ShapeDtypeStruct((inner, own), BF16),
            jax.ShapeDtypeStruct((inner, own), BF16),
            jax.ShapeDtypeStruct((inner, Q), F32),
            jax.ShapeDtypeStruct((inner, Q), BF16),
        ],
        scratch_shapes=[pltpu.VMEM((inner, width), BF16), pltpu.VMEM((inner, Q), F32)],
        compiler_params=pltpu.CompilerParams(vmem_limit_bytes=VMEM),
    )(d_unit, ssd, z, scale, gain, start, conv)


def scan_back_kernel(
    bc, skip_ref, conv_ref, d_ssd_ref, states_ref, last_ref, cum_ref, shift_ref, into_ref, onto_ref, keep_ref,
    step_ref, slope_ref, ratio_ref, seg_ref, head_ref,
    d_conv_ref, d_raw_ref, bias_grad_ref, rate_grad_ref, skip_grad_ref,
    grad, col_scr, row_scr, diag_scr, state_scr, hold_scr, y_scr, x_scr, dst_scr, dc_scr, db_scr,
):
    inner_half, stride = bc
    groups = 2 * inner_half // 512
    heads = 2 * inner_half // 64

    @pl.when(pl.program_id(0) == 0)
    def _():
        grad[...] = last_ref[...].astype(F32)
        bias_grad_ref[...] = jnp.zeros_like(bias_grad_ref)
        rate_grad_ref[...] = jnp.zeros_like(rate_grad_ref)
        skip_grad_ref[...] = jnp.zeros_like(skip_grad_ref)

    b_t, c_t, b_m, scores, allowed = chunk_scores(conv_ref, bc, seg_ref)
    c_m = c_t.astype(F32).T.astype(BF16)
    columns_of(shift_ref, col_scr)
    dst_scr[...] = jnp.zeros_like(dst_scr)
    dc_scr[...] = jnp.zeros_like(dc_scr)
    db_scr[...] = jnp.zeros_like(db_scr)

    def group(g, carry):
        at = pl.multiple_of(g * 512, 512)
        x_at = pl.multiple_of(g * 512 + jnp.where(g >= groups // 2, stride - inner_half, 0), 256)
        held = states_ref[0, pl.ds(at, 512), :]
        g_low = grad[pl.ds(at, 512), :].astype(BF16)
        from_state = dot(held, c_t, 1, 0)
        onto_state = dot(g_low, b_t, 1, 0)
        cols = col_scr[g]
        d_scores = jnp.zeros((Q, Q), F32)
        for k in range(8):
            h = g * 8 + k
            row = pl.ds(h, 1)
            span = slice(k * 64, (k + 1) * 64)
            x = conv_ref[pl.ds(x_at + k * 64, 64), :]
            dy = d_ssd_ref[pl.ds(at + k * 64, 64), :]
            xf, dyf = x.astype(F32), dy.astype(F32)
            decays = jnp.exp2(jnp.minimum(cum_ref[row, :] - cols[:, k : k + 1], CAP))
            mixing = (decays * scores).astype(BF16)
            d_scores = d_scores + decays * dot(x, dy, 0, 0)
            y = dot(x, mixing, 1, 0) + from_state[span] * into_ref[row, :]
            dx = dot(dy, mixing, 1, 1)
            dx_state = onto_state[span] * onto_ref[row, :]
            row_scr[row, :] = jnp.sum(dyf * y, axis=0, keepdims=True)
            diag_scr[row, :] = jnp.sum(xf * dx, axis=0, keepdims=True)
            state_scr[row, :] = jnp.sum(xf * dx_state, axis=0, keepdims=True)
            skip_grad_ref[row, :] += jnp.sum(xf * dyf, axis=0, keepdims=True)
            hold_scr[row, :] = jnp.sum(grad[pl.ds(at + k * 64, 64), :] * held[span].astype(F32), axis=0, keepdims=True)
            d_conv_ref[pl.ds(x_at + k * 64, 64), :] = (dx + dx_state + skip_ref[h] * dyf).astype(BF16)
            y_scr[span, :] = (dyf * into_ref[row, :]).astype(BF16)
            x_scr[span, :] = (xf * onto_ref[row, :]).astype(BF16)
        dst_scr[...] += d_scores
        fresh = dot(y_scr[...], c_m, 1, 0)
        dc_scr[...] += dot(held, y_scr[...], 0, 0)
        db_scr[...] += dot(g_low, x_scr[...], 0, 0)
        for k in range(8):
            rows = pl.ds(at + k * 64, 64)
            grad[rows, :] = grad[rows, :] * keep_ref[pl.ds(g * 8 + k, 1), :] + fresh[k * 64 : (k + 1) * 64]
        return carry

    lax.fori_loop(0, groups, group, 0)
    d_scores = jnp.where(allowed, dst_scr[...], 0.0).astype(BF16)
    zeros = jnp.zeros((stride - inner_half - Q, Q), BF16)
    d_conv_ref[inner_half : inner_half + Q, :] = (db_scr[...] + dot(c_t, d_scores, 1, 1)).astype(BF16)
    d_conv_ref[inner_half + Q : stride, :] = zeros
    d_conv_ref[stride + inner_half : stride + inner_half + Q, :] = (dc_scr[...] + dot(b_t, d_scores, 1, 0)).astype(BF16)
    d_conv_ref[stride + inner_half + Q :, :] = zeros

    source = lax.broadcasted_iota(jnp.int32, (Q, Q), 0)
    target = lax.broadcasted_iota(jnp.int32, (Q, Q), 1)
    since = (source >= target).astype(F32)
    columns = diag_scr[...] + state_scr[...]
    d_decay = dot(row_scr[...] - columns, since, 1, 0, lax.Precision.HIGHEST)
    d_decay = d_decay + jnp.sum(state_scr[...] + hold_scr[...] * keep_ref[...], axis=1, keepdims=True)
    rate = -jnp.exp(head_ref[:, 0:1])
    slope = slope_ref[...]
    d_raw = columns * ratio_ref[...] + rate * d_decay * slope
    bias_grad_ref[...] += d_raw
    rate_grad_ref[...] += step_ref[...] * d_decay * rate
    d_raw_ref[...] = jnp.zeros_like(d_raw_ref)
    d_raw_ref[0 : heads // 2, :] = d_raw[: heads // 2].astype(BF16)
    d_raw_ref[Q : Q + heads // 2, :] = d_raw[heads // 2 :].astype(BF16)


def scan_backward(bc, skip, conv, d_ssd, states, last, rows, seg, head_cols):
    inner = 2 * bc[0]
    channels, own = conv.shape
    chunks = own // Q
    heads = inner // 64
    end = chunks - 1
    row_spec = pl.BlockSpec((heads, Q), lambda c: (0, end - c))
    whole = pl.BlockSpec((inner, Q), lambda c: (0, 0))
    sums = pl.BlockSpec((heads, Q), lambda c: (0, 0))
    cum, shift, into, onto, keep, step, slope, ratio = rows[:8]
    small = jax.ShapeDtypeStruct((heads, Q), F32)
    row_buf = pltpu.VMEM((heads, Q), F32)
    square = pltpu.VMEM((Q, Q), F32)
    return pl.pallas_call(
        functools.partial(scan_back_kernel, bc),
        cost_estimate=takes(44),
        grid=(chunks,),
        in_specs=[
            pl.BlockSpec(memory_space=pltpu.SMEM),
            pl.BlockSpec((channels, Q), lambda c: (0, end - c)),
            pl.BlockSpec((inner, Q), lambda c: (0, end - c)),
            pl.BlockSpec((1, inner, Q), lambda c: (end - c, 0, 0)),
            whole,
        ]
        + [row_spec] * 8
        + [
            pl.BlockSpec((1, Q), lambda c: (0, end - c)),
            pl.BlockSpec(head_cols.shape, lambda c: (0, 0)),
        ],
        out_specs=[
            pl.BlockSpec((channels, Q), lambda c: (0, end - c)),
            pl.BlockSpec((2 * Q, Q), lambda c: (0, end - c)),
            sums, sums, sums,
        ],
        out_shape=[
            jax.ShapeDtypeStruct((channels, own), BF16),
            jax.ShapeDtypeStruct((2 * Q, own), BF16),
            small, small, small,
        ],
        scratch_shapes=[
            pltpu.VMEM((inner, Q), F32), pltpu.VMEM((heads // 8, Q, 8), F32),
            row_buf, row_buf, row_buf, row_buf,
            pltpu.VMEM((512, Q), BF16), pltpu.VMEM((512, Q), BF16),
            square, square, square,
        ],
        compiler_params=pltpu.CompilerParams(vmem_limit_bytes=VMEM),
    )(skip, conv, d_ssd, states, last, cum, shift, into, onto, keep, step, slope, ratio, seg, head_cols)


def conv_back_kernel(half, place_ref, proj_ref, pre_ref, d_ref, beyond_ref, raw_ref, w_ref, mask_ref, out_ref, sums_ref, acc):
    s = pl.program_id(0)
    channels, own = out_ref.shape
    tiles = own // Q
    at = pl.multiple_of(place_ref[0] * HALO, HALO)
    size = 32

    def strip(i, carry):
        rows = pl.ds(pl.multiple_of(i * size, size), size)
        wide = wide_columns(w_ref, rows)
        lane = lax.broadcasted_iota(jnp.int32, (size, Q), 1)
        sums = [jnp.zeros((size, Q), F32)] * 5
        kept, moved = None, None
        for j in range(tiles + 1):
            span = slice(j * Q, (j + 1) * Q)
            if j < tiles:
                pre = pre_ref[rows, span].astype(F32)
                sig = sigmoid(pre)
                d_pre = d_ref[rows, span].astype(F32) * (sig + pre * sig * (1.0 - sig))
            else:
                d_pre = beyond_ref[rows, :].astype(F32)
            back = [pltpu.roll(d_pre * mask_ref[k - 1 : k, span], Q - k, 1) for k in (1, 2, 3)]
            if j > 0:
                now = proj_ref[rows, pl.ds(pl.multiple_of(at + (j - 1) * Q, Q), Q)].astype(F32)
                shifted = [kept] + [jnp.where(lane < Q - k, moved[k - 1], back[k - 1]) for k in (1, 2, 3)]
                d_proj = wide[3] * kept
                for k in (1, 2, 3):
                    d_proj = d_proj + wide[3 - k] * shifted[k]
                for k in range(4):
                    sums[3 - k] = sums[3 - k] + now * shifted[k]
                out_ref[rows, (j - 1) * Q : j * Q] = d_proj.astype(BF16)
            if j < tiles:
                sums[4] = sums[4] + d_pre
            kept, moved = d_pre, back
        for k in range(5):
            acc[rows, k * Q : (k + 1) * Q] = sums[k]
        return carry

    lax.fori_loop(0, channels // size, strip, 0)
    rows_of = lax.broadcasted_iota(jnp.int32, (5 * Q, Q), 0) // Q
    column = lax.broadcasted_iota(jnp.int32, (5 * Q, Q), 1)
    ones = jnp.where(rows_of == column, 1.0, 0.0).astype(BF16)
    high = acc[...].astype(BF16)
    low = (acc[...] - high.astype(F32)).astype(BF16)
    sums_ref[...] = dot(high, ones, 1, 0) + dot(low, ones, 1, 0)

    @pl.when(lax.rem(s, half) == half - 1)
    def _():
        out_ref[Q:, :] = raw_ref[...]


def conv_backward(place_id, proj, pre, d_conv, beyond, d_raw, w_wide, masks):
    channels, window = proj.shape
    own = window - HALO
    blocks = channels // 256
    half = blocks // 2
    return pl.pallas_call(
        functools.partial(conv_back_kernel, half),
        cost_estimate=takes(31),
        grid=(blocks,),
        in_specs=[
            pl.BlockSpec(memory_space=pltpu.SMEM),
            pl.BlockSpec((256, window), lambda s: (s, 0)),
            pl.BlockSpec((256, own), lambda s: (s, 0)),
            pl.BlockSpec((256, own), lambda s: (s, 0)),
            pl.BlockSpec((256, HALO), lambda s: (s, 0)),
            pl.BlockSpec((Q, own), lambda s: (s // half, 0)),
            pl.BlockSpec((256, 5 * Q), lambda s: (s, 0)),
            pl.BlockSpec(masks.shape, lambda s: (0, 0)),
        ],
        out_specs=[pl.BlockSpec((256, own), lambda s: (s, 0)), pl.BlockSpec((256, Q), lambda s: (s, 0))],
        out_shape=[jax.ShapeDtypeStruct((channels, own), BF16), jax.ShapeDtypeStruct((channels, Q), F32)],
        scratch_shapes=[pltpu.VMEM((256, 5 * Q), F32)],
        compiler_params=pltpu.CompilerParams(vmem_limit_bytes=VMEM),
    )(place_id, proj, pre, d_conv, beyond, d_raw, w_wide, masks)


def shards(
    tokens, token_seq, w_z, w_xbc, w_dt, w_out, conv_w, conv_b, gate_gain, norm_gain, a_log, d_skip, dt_bias, d_out, *, count
):
    my = lax.axis_index("mp")
    all_rows, width = tokens.shape
    own = all_rows // 2
    window = own + HALO
    inner_half = w_z.shape[1]
    inner = 2 * inner_half
    conv_half = w_xbc.shape[1]
    state_dim = conv_half - inner_half
    heads_half = w_dt.shape[1]
    stride = -(-(conv_half + heads_half) // 256) * 256
    bc = (inner_half, stride)
    place_id = my.reshape(1).astype(jnp.int32)

    per, taps = conv_w.shape[1], conv_w.shape[0]
    shard_rows = w_dt.shape[0]
    spare = stride - conv_half - heads_half
    head_params = jnp.concatenate([a_log, dt_bias, d_skip])
    high = head_params.astype(BF16)
    middle = (head_params - high.astype(F32)).astype(BF16)
    low = (head_params - high.astype(F32) - middle.astype(F32)).astype(BF16)
    vectors = [*conv_w, conv_b, gate_gain, norm_gain, high, middle, low]
    small = jnp.stack([jnp.pad(v, (0, Q - v.shape[0])) for v in vectors])
    small = jnp.pad(small, ((0, 16 - len(vectors)), (0, 0)))
    shard_xbc = jnp.concatenate([w_xbc, w_dt, jnp.zeros((shard_rows, spare), BF16)], 1)
    sizes = (per, gate_gain.shape[0], norm_gain.shape[0], heads_half, stride)
    spare_sizes = (*sizes, Q - spare)
    conv_masks, scan_masks, seg_row = row_masks(place_id, token_seq)

    shard_out = w_out.T
    swapped = [swap(w_z), swap(shard_out)]
    if count == 16:
        full_xbc, prepared, normed_rows, swapped, marks = gather_now(
            shard_xbc,
            small,
            lambda got: parameters(got, sizes, True),
            lambda got: normalise(place_id, tokens, got[3]),
            swapped,
        )
    else:
        marks = ()
        full_xbc = gather_later(shard_xbc, swap(shard_xbc), marks)
        small = lax.all_gather(lax.all_gather(small, "dp", axis=0, tiled=False), "mp", axis=0, tiled=False)
        prepared = parameters(small.reshape(2 * count, 16, Q), sizes, False)
        normed_rows = normalise(place_id, tokens, prepared[3])
    full_z = gather_later(w_z, swapped[0], marks)
    full_out = gather_later(shard_out, swapped[1], marks)
    w_wide, gain_wide, gain_in, gain_tall, head_cols = prepared
    window_t, normed_t = normed_rows
    skip_all = head_cols[:, 2]
    full_xbc = full_xbc.reshape(2, width, stride)

    proj = jnp.einsum("ydc,dt->yct", full_xbc, window_t, preferred_element_type=F32).astype(BF16)
    proj = proj.reshape(2 * stride, window)
    full_dt = full_xbc[:, :, conv_half : conv_half + heads_half]
    dt_raw = jnp.einsum("ydh,dt->yht", full_dt, normed_t, preferred_element_type=F32).reshape(2 * heads_half, own)
    rows = head_rows(dt_raw, head_cols, scan_masks)
    start_rows, end_rows = rows[8], rows[9]
    conved, pre, end_state = conv_forward(place_id, proj, w_wide, conv_masks, end_rows)
    state_flow = once(end_state, lambda a: lax.ppermute(a, "mp", [(0, 1)]))
    z = jnp.einsum("ydk,dt->ykt", full_z, ahead(normed_t, state_flow), preferred_element_type=F32).astype(BF16).reshape(inner, own)
    z = after(z, state_flow)
    d_flow = once(lax.dynamic_slice_in_dim(tie(d_out, proj)[0], (1 - my) * own, own, 0), swap)
    z = ahead(z, d_flow)
    out_normed, ssd, scale, states = scan_forward(
        bc, skip_all, conved, z, rows, seg_row, gain_wide, state_flow.result
    )
    out_normed = after(out_normed, d_flow)
    cotangent, cot_t = cotangents(place_id, d_out, d_flow.result, seg_row)
    grad_out, own_out = weight_grad_sum(cot_t, out_normed, count)
    out_ready = tie(out_normed, grad_out)[0]
    branch = jnp.einsum(
        "ykt,ydk->td", out_ready.reshape(2, inner_half, own), full_out, preferred_element_type=F32
    )
    first_half = my == 0
    live_rows = (lax.dynamic_slice_in_dim(token_seq, my * own, own, 0) >= 0)[:, None]
    tokens_own = lax.dynamic_slice_in_dim(tokens, my * own, own, 0).astype(F32)
    layer_rows = (tokens_own + jnp.where(live_rows, branch, 0.0)).astype(BF16)
    half_width = width // 2
    layer_mine = lax.dynamic_slice_in_dim(layer_rows, my * half_width, half_width, 1)
    layer_flow = once(lax.dynamic_slice_in_dim(layer_rows, (1 - my) * half_width, half_width, 1), swap)

    d_unit = jnp.einsum("ydk,dt->ykt", full_out, ahead(cot_t, layer_flow), preferred_element_type=F32).astype(BF16).reshape(inner, own)
    d_ssd, d_gate, gain_grad, first_grad = gate_backward(bc, d_unit, ssd, z, scale, gain_wide, start_rows, conved)
    d_gate = after(d_gate, layer_flow)
    grad_flow = once(first_grad, lambda a: lax.ppermute(a, "mp", [(1, 0)]))
    ready = ahead(d_gate, grad_flow)
    d_normed_z = jnp.einsum("ykt,ydk->td", ready.reshape(2, inner_half, own), full_z, preferred_element_type=F32)
    first_pre = ahead(pre, grad_flow)[:, :HALO].astype(F32)
    first_sig = sigmoid(first_pre)
    first_slope = first_sig + first_pre * first_sig * (1.0 - first_sig)
    d_normed_z = after(d_normed_z, grad_flow, also=(first_slope,))
    grad_z, own_z = weight_grad_sum(normed_t, tie(d_gate, d_normed_z)[0], count)
    d_conv, d_raw, bias_grad, rate_grad, skip_grad = scan_backward(
        bc, skip_all, conved, tie(d_ssd, grad_z)[0], states, grad_flow.result, rows, seg_row, head_cols
    )
    head_grads = jnp.stack([jnp.sum(v, 1) for v in (rate_grad, skip_grad, bias_grad)])
    head_grads = jnp.pad(head_grads.reshape(1, -1), ((0, 7), (0, -head_grads.size % Q)))
    heads_flow = total(head_grads, count)
    d_first = d_conv[:, :HALO].astype(F32) * first_slope
    d_first = d_first[:, :16].astype(BF16).T
    beyond_flow = once(d_first, lambda a: lax.ppermute(a, "mp", [(1, 0)]))
    layer_recv = ahead(layer_flow.result, beyond_flow, heads_flow)
    layer_out = jnp.where(
        first_half, jnp.concatenate([layer_mine, layer_recv], 0), jnp.concatenate([layer_recv, layer_mine], 0)
    )
    layer_out = after(layer_out, beyond_flow, heads_flow)
    beyond = jnp.pad(beyond_flow.result.T, ((0, 0), (0, HALO - 16)))
    d_conv = ahead(tie(d_conv, own_out, layer_out)[0], heads_flow)
    d_proj, conv_sums = conv_backward(
        place_id, proj, pre, d_conv, beyond, d_raw, w_wide, conv_masks
    )
    d_proj = after(d_proj, heads_flow)
    small = spare_block(spare_sizes, count, conv_sums, gain_grad)
    tiles = stride // 256
    keep_b, sent_b = weight_grad(ahead(normed_t, heads_flow), d_proj, count, (tiles - 4, tiles), small)
    keep_b = after(keep_b, heads_flow)
    flow_b = sum_to_owners(keep_b, sent_b, count, "zxy")
    keep_a, sent_a = weight_grad(ahead(normed_t, flow_b, heads_flow), d_proj, count, (0, tiles - 4))
    keep_a = after(keep_a, flow_b, heads_flow)
    flow_a = sum_to_owners(keep_a, sent_a, count, "xzy")
    full_back = ahead(full_xbc, flow_a, flow_b, heads_flow)
    back = (d_normed_z, tokens, cotangent, gain_in)
    d_tokens, part_0, part_1 = norm_backward(place_id, d_proj, full_back, *back, 0)
    part_0 = after(part_0, flow_a, flow_b, heads_flow)
    low_flows = [once(part_0, swap), once(tie(part_1, part_0)[0], swap)]
    full_back = ahead(full_xbc, flow_a, flow_b, *low_flows)
    d_tokens, part_2, part_3 = norm_backward(place_id, d_proj, full_back, *back, 2, d_tokens)
    part_2 = after(part_2, flow_a, flow_b, heads_flow, *low_flows, also=(own_z,))
    low_flows += [once(part_2, swap), once(tie(part_3, part_2)[0], swap)]
    mark = after(tie(norm_gain, part_2)[0], flow_a, flow_b, heads_flow, low_flows[2])
    mark = after(mark, flow_a, flow_b, heads_flow, low_flows[3])
    mark = after(mark, flow_a, flow_b)
    mark = after(mark, flow_a, flow_b)
    own_xbc = jnp.concatenate([flow_a.finish(), flow_b.finish()], 1)
    head_grads = heads_flow.finish().reshape(-1)[: 6 * heads_half]
    d_tokens = fill_rows(place_id, d_tokens, [f.finish() for f in low_flows])

    own_xbc, own_dt, own_z, own_taps, own_bias, own_gain, product = finish(sizes, own_xbc, own_z, w_xbc, w_dt, w_z)
    own_out = own_out.astype(F32).T
    norms = norm_gain.shape[0]
    product = lax.dynamic_slice_in_dim(product[:, 0] + swap(product)[:, 0], my * norms, norms, 0)
    norm_mine = product / norm_gain.astype(F32)
    heads_mine = pick(head_grads.reshape(3, 2, heads_half), my, 1)
    return (
        layer_out,
        d_tokens,
        own_z,
        own_xbc,
        own_dt,
        own_out,
        own_taps,
        own_bias[0],
        own_gain[0],
        norm_mine,
        heads_mine[0],
        heads_mine[1],
        heads_mine[2],
    )


def solution(mesh):
    placed = (
        P("dp", None),
        P("dp"),
        P("dp", "mp"),
        P("dp", "mp"),
        P("dp", "mp"),
        P("mp", "dp"),
        P(None, ("mp", "dp")),
        P(("mp", "dp")),
        P(("mp", "dp")),
        P(("dp", "mp")),
        P("mp"),
        P("mp"),
        P("mp"),
        P("dp", "mp"),
    )
    return jax.shard_map(
        functools.partial(shards, count=mesh.shape["dp"]),
        mesh=mesh,
        in_specs=placed,
        out_specs=(
            P("dp", "mp"),
            P("dp", None),
            P("dp", "mp"),
            P("dp", "mp"),
            P("dp", "mp"),
            P("mp", "dp"),
            P(None, ("mp", "dp")),
            P(("mp", "dp")),
            P(("mp", "dp")),
            P(("dp", "mp")),
            P("mp"),
            P("mp"),
            P("mp"),
        ),
        check_vma=False,
    )
```

```python
import functools

import jax
import jax.numpy as jnp
from jax import lax
from jax.experimental import pallas as pl
from jax.experimental.pallas import tpu as pltpu
from jax.sharding import PartitionSpec as P

F32 = jnp.float32
BF16 = jnp.bfloat16
EPS = 1e-05
LOG2E = 1.4426950408889634
CAP = 60.0
Q = 128
HALO = 128
VMEM = 60 * 1024 * 1024


def dot(a, b, ca, cb, precision=None):
    return lax.dot_general(
        a, b, (((ca,), (cb,)), ((), ())), precision=precision, preferred_element_type=F32
    )


def takes(micros):
    return pl.CostEstimate(flops=0, transcendentals=0, bytes_accessed=int(micros * 3.0e6))


def xor_perm(count, bits):
    return [(i, i ^ bits) for i in range(count)]


def line_perm(pairs):
    return [(a * 4 + r, b * 4 + r) for a, b in pairs for r in range(4)]


ENDS_IN = ((1, 0), (2, 3))
ENDS_OUT = ((0, 1), (3, 2))
MIDDLE = ((1, 2), (2, 1))
PAIRS = ((0, 1), (1, 0), (2, 3), (3, 2))
SWAP = [(0, 1), (1, 0)]


def send_line(a, pairs):
    return lax.ppermute(a, "dp", line_perm(pairs))


def send_x(a):
    return lax.ppermute(a, "dp", xor_perm(16, 2))


def send_core(a):
    return lax.ppermute(a, "dp", xor_perm(16, 1))


def send_y(a):
    return lax.ppermute(a, "mp", SWAP)


def place_kernel(where, me_ref, *refs):
    pieces, out_ref, held, arrived, left = refs[:-4], refs[-4], refs[-3], refs[-2], refs[-1]
    me, my = me_ref[0], me_ref[1]
    inward, outward = [], []
    for piece, parts in zip(pieces, where):
        for k, (ry, rest) in enumerate(parts):
            n = len(inward)
            slot = out_ref.at[jnp.bitwise_xor(my, ry), jnp.bitwise_xor(me, rest)]
            inward.append(pltpu.make_async_copy(piece.at[k], held.at[n], arrived.at[n]))
            outward.append(pltpu.make_async_copy(held.at[n], slot, left.at[n]))
    for copy in inward:
        copy.start()
    for copy, further in zip(inward, outward):
        copy.wait()
        further.start()
    for copy in outward:
        copy.wait()


def place(pieces, where, me, my):
    rows, width = pieces[0].shape[1:]
    return pl.pallas_call(
        functools.partial(place_kernel, where),
        cost_estimate=takes(9),
        out_shape=jax.ShapeDtypeStruct((2, 16, rows, width), pieces[0].dtype),
        in_specs=[pl.BlockSpec(memory_space=pltpu.SMEM)]
        + [pl.BlockSpec(memory_space=pl.ANY)] * len(pieces),
        out_specs=pl.BlockSpec(memory_space=pl.ANY),
        scratch_shapes=[
            pltpu.VMEM((32, rows, width), pieces[0].dtype),
            pltpu.SemaphoreType.DMA((32,)),
            pltpu.SemaphoreType.DMA((32,)),
        ],
        compiler_params=pltpu.CompilerParams(vmem_limit_bytes=VMEM),
    )(jnp.stack([me, my]).astype(jnp.int32), *pieces)


def tie(*values):
    return lax.optimization_barrier(values)


def gather_now(shard, small, prepare, normalised, swapped):
    me, my = lax.axis_index("dp"), lax.axis_index("mp")
    near = send_line(shard, PAIRS)
    far_mid = send_line(shard, MIDDLE)
    small = small[None]
    for send in (send_x, send_core, send_y):
        small = jnp.concatenate([small, send(small)], 0)
    first = jnp.stack([shard, near])
    first_x, first_y = send_x(first), send_y(first)
    small, far_mid, near = tie(small, far_mid, near)
    across_end = send_line(far_mid, ENDS_IN)
    across_mid = send_line(near, MIDDLE)
    small_near, small_far = send_line(small, PAIRS), send_line(small, MIDDLE)
    across_end, across_mid, small_near, small_far = tie(across_end, across_mid, small_near, small_far)
    far_end = send_line(across_mid, ENDS_IN)
    small_across_end, small_across = send_line(small_far, ENDS_IN), send_line(small_near, MIDDLE)
    second = jnp.stack([across_end + across_mid, far_mid + far_end])
    second, first_x, first_y, small_across_end, small_across = tie(
        second, first_x, first_y, small_across_end, small_across
    )
    second_x, second_y = send_x(second), send_y(second)
    small_far_end = send_line(small_across, ENDS_IN)
    early = [first, first_x, first_y]
    early_core = [send_core(a) for a in early]
    small = jnp.concatenate([small, small_near, small_across_end + small_across, small_far + small_far_end], 0)
    prepared = prepare(small)
    second_x, second_y, first_x, second, *rest = tie(second_x, second_y, first_x, second, *early_core, *prepared)
    early_core, prepared = rest[:3], rest[3:]
    first_xy, second_xy = send_y(first_x), send_x(second_y)
    late = [second, second_x, second_y]
    late_core = [send_core(a) for a in late]
    rows = normalised(prepared)
    first_xy, second_xy, *rest = tie(first_xy, second_xy, *late_core, *rows)
    late_core, rows = rest[:3], rest[3:]
    last_core = [send_core(first_xy), send_core(second_xy)]
    pieces, where = [], []
    for own, other, pair, sides in (
        (early, early_core, 0, (0, 1, 2)),
        (late, late_core, 1, (0, 1, 2)),
        ([first_xy], last_core[:1], 0, (3,)),
        ([second_xy], last_core[1:], 1, (3,)),
    ):
        for rc, parts in enumerate((own, other)):
            pieces += parts
            where += [[(side // 2, (2 * pair + low) * 4 + (side % 2) * 2 + rc) for low in range(2)] for side in sides]
    return place(pieces, where, me, my), prepared, rows, swapped, (second_x, second_y)


def swap(a):
    return lax.ppermute(a, "mp", SWAP)


def gather_later(shard, other, marks):
    my = lax.axis_index("mp")
    pair = jnp.where(my == 0, jnp.stack([shard, other]), jnp.stack([other, shard]))
    if marks:
        pair = tie(pair, *marks)[0]
    return lax.all_gather(pair, "dp", axis=1, tiled=True)


class Flow:
    def __init__(self, steps=None, result=None):
        self.steps, self.result = steps, result
        self.sent, self.flying = [], []
        if steps is not None:
            self.sent, self.flying = next(steps)

    def move(self, got):
        try:
            self.sent, self.flying = self.steps.send(list(got))
        except StopIteration as stop:
            self.result = stop.value

    def finish(self):
        while self.result is None:
            self.move(self.flying)
        return self.result


def once(sent, send):
    def steps():
        (got,) = yield [sent], [send(sent)]
        return got

    return Flow(steps())


def ahead(value, *flows):
    sent = sum([f.sent for f in flows if f.result is None], [])
    return tie(value, *sent)[0] if sent else value


def after(value, *flows, also=()):
    live = [f for f in flows if f.result is None]
    if live:
        value, *got = tie(value, *sum([f.flying for f in live], []), *also)
        for f in live:
            count = len(f.flying)
            part, got = got[:count], got[count:]
            f.move(part)
    return value


def add(a, b):
    return (a.astype(F32) + b.astype(F32)).astype(a.dtype)


def pick(a, index, axis):
    return lax.dynamic_index_in_dim(a, index, axis, keepdims=False)


def line_steps(a, z):
    block = [pick(a, jnp.bitwise_xor(z, r), 0) for r in range(4)]
    (got,) = yield [block[3]], [send_line(block[3], ENDS_OUT)]
    into_near = add(block[2], got)
    out, got = yield [block[2], into_near], [send_line(block[2], ENDS_OUT), send_line(into_near, MIDDLE)]
    far, near = add(block[3], out), add(block[1], got)
    got, out = yield [far, near], [send_line(far, MIDDLE), send_line(near, PAIRS)]
    return (block[0].astype(F32) + got.astype(F32) + out.astype(F32)).astype(a.dtype)


def halve_step(a, axis, bit, send):
    sent = pick(a, 1 - bit, axis)
    return pick(a, bit, axis), sent, send(sent)


def stages(a, order, my, z, x):
    names = ["y", "z", "x"]
    for name in order:
        axis = names.index(name)
        names.remove(name)
        if name == "z":
            a = yield from line_steps(jnp.moveaxis(a, axis, 0), z)
        else:
            bit, send = (my, send_y) if name == "y" else (x, send_x)
            keep, sent, flying = halve_step(a, axis, bit, send)
            (got,) = yield [sent], [flying]
            a = add(keep, got)
    return a


def scatter_steps(keep, sent, order):
    rows, width = keep.shape[2:]
    me, my = lax.axis_index("dp"), lax.axis_index("mp")
    z, x = me // 4, (me // 2) % 2
    (got,) = yield [sent], [send_core(sent)]
    a = add(keep, got).reshape(2, 4, 2, rows, width)
    return (yield from stages(a, order, my, z, x))


def sum_to_owners(keep, sent, count, order):
    if count == 16:
        return Flow(scatter_steps(keep, sent, order))
    core = lax.axis_index("dp") % 2
    pair = jnp.stack([keep, sent], 2)
    grad = jnp.where(core == 0, pair, pair[:, :, ::-1])
    mine = lax.psum_scatter(grad, "mp", scatter_dimension=0, tiled=False)
    mine = mine.reshape((-1,) + keep.shape[2:])
    return Flow(result=lax.psum_scatter(mine, "dp", scatter_dimension=0, tiled=False))


def total_steps(a):
    for send in (send_core, send_x, send_y, lambda v: send_line(v, PAIRS)):
        (got,) = yield [a], [send(a)]
        a = a + got
    (far,) = yield [a], [send_line(a, MIDDLE)]
    (further,) = yield [far], [send_line(far, ENDS_IN)]
    return a + far + further


def total(a, count):
    if count == 16:
        return Flow(total_steps(a))
    return Flow(result=lax.psum(a, ("dp", "mp")))


def sigmoid(v):
    return 0.5 * jnp.tanh(0.5 * v) + 0.5


def mask_kernel(place_ref, seg_ref, conv_ref, scan_ref, own_ref):
    seg = jnp.broadcast_to(seg_ref[...].astype(F32), (8, seg_ref.shape[1]))
    total = seg.shape[1]
    own = total // 2
    first = place_ref[0] == 0
    lane = lax.broadcasted_iota(jnp.int32, seg.shape, 1)
    conv_ref[...] = jnp.zeros_like(conv_ref)
    for k in (1, 2, 3):
        same = jnp.where((lane >= k) & (pltpu.roll(seg, k, 1) == seg), 1.0, 0.0)
        conv_ref[k - 1 : k, :own] = jnp.where(first, same[:1, :own], same[:1, own:])
        conv_ref[k - 1 : k, own:] = jnp.where(first, same[:1, own : own + HALO], 0.0)
    mine = jnp.where(first, seg[:1, :own], seg[:1, own:])
    own_ref[...] = mine
    outside = jnp.where(first, -2.0, seg[:1, own - 1 : own])
    scan_ref[...] = jnp.zeros_like(scan_ref)
    before, final = outside, mine[:, own - 1 :]
    for c in range(own // Q):
        span = slice(c * Q, (c + 1) * Q)
        here = mine[:, span]
        last = here[:, Q - 1 :]
        flags = (here == before, here == last, jnp.broadcast_to(last, here.shape) == before, here == final, here == outside)
        for k, flag in enumerate(flags):
            scan_ref[k : k + 1, span] = jnp.where(flag, 1.0, 0.0)
        before = last


def row_masks(place_id, token_seq):
    total = token_seq.shape[0]
    own = total // 2
    return pl.pallas_call(
        mask_kernel,
        cost_estimate=takes(2),
        in_specs=[pl.BlockSpec(memory_space=pltpu.SMEM), pl.BlockSpec(memory_space=pltpu.VMEM)],
        out_shape=[
            jax.ShapeDtypeStruct((8, own + HALO), F32),
            jax.ShapeDtypeStruct((8, own), F32),
            jax.ShapeDtypeStruct((1, own), F32),
        ],
    )(place_id, token_seq[None, :])


def param_kernel(sizes, by_distance, me_ref, got_ref, w_ref, gain_ref, norm_ref, tall_ref, head_ref, scr):
    per, gains, norms, heads, stride = sizes
    count = got_ref.shape[0] // 2
    me, my = me_ref[0], me_ref[1]
    for r in range(2 * count):
        if by_distance:
            rz, ry, rest = r // 8, (r // 4) % 2, (r // 2) % 2 + (r % 2) * 2
            at = jnp.bitwise_xor(my, ry) * count + jnp.bitwise_xor(me, rz * 4 + rest)
        else:
            at = r
        scr[at] = got_ref[r].astype(F32)
    w_ref[...] = jnp.zeros_like(w_ref)
    head_ref[...] = jnp.zeros_like(head_ref)
    for y in range(2):
        for group in range(count // 8):
            tiles = [scr[y * count + group * 8 + d] for d in range(8)]
            turned = jnp.concatenate(tiles, 0).T
            for d in range(8):
                device = group * 8 + d
                at = y * stride + device * per
                for k in range(5):
                    column = turned[:per, d * 16 + k : d * 16 + k + 1]
                    w_ref[at : at + per, k * Q : (k + 1) * Q] = jnp.broadcast_to(column, (per, Q))
                column = turned[:gains, d * 16 + 5 : d * 16 + 6]
                at = (y * count + device) * gains
                gain_ref[at : at + gains, :] = jnp.broadcast_to(column, (gains, Q))
                at = 2 * device + y
                norm_ref[at : at + 1, :] = tiles[d][6:7]
                column = turned[:norms, d * 16 + 6 : d * 16 + 7]
                tall_ref[at * norms : (at + 1) * norms, :] = jnp.broadcast_to(column, (norms, Q))
            if group == 0:
                column = turned[:, 7:8] + turned[:, 8:9] + turned[:, 9:10]
                for j in range(3):
                    head_ref[y * heads : (y + 1) * heads, j : j + 1] = column[j * heads : (j + 1) * heads]


def parameters(got, sizes, by_distance):
    per, gains, norms, heads, stride = sizes
    count = got.shape[0] // 2
    me, my = lax.axis_index("dp"), lax.axis_index("mp")
    wide, gain, norm, tall, head = pl.pallas_call(
        functools.partial(param_kernel, sizes, by_distance),
        cost_estimate=takes(10),
        in_specs=[pl.BlockSpec(memory_space=pltpu.SMEM), pl.BlockSpec(memory_space=pltpu.VMEM)],
        out_shape=[
            jax.ShapeDtypeStruct((2 * stride, 5 * Q), F32),
            jax.ShapeDtypeStruct((2 * count * gains, Q), F32),
            jax.ShapeDtypeStruct((2 * count, Q), F32),
            jax.ShapeDtypeStruct((2 * count * norms, Q), F32),
            jax.ShapeDtypeStruct((2 * heads, 8), F32),
        ],
        scratch_shapes=[pltpu.VMEM((2 * count, 16, Q), F32)],
        compiler_params=pltpu.CompilerParams(vmem_limit_bytes=VMEM),
    )(jnp.stack([me, my]).astype(jnp.int32), got)
    return wide, gain, norm[:, :norms].reshape(1, -1), tall, head


def norm_kernel(place_ref, x_ref, gain_ref, window_ref, own_ref):
    mine = pl.program_id(0) - place_ref[0]
    x = x_ref[...].astype(F32)
    scaled = x * lax.rsqrt(jnp.mean(x * x, axis=1, keepdims=True) + EPS)
    normed = (scaled.T * gain_ref[...]).astype(BF16)
    window_ref[...] = normed

    @pl.when((mine >= 0) & (mine < pl.num_programs(0) - 1))
    def _():
        own_ref[...] = normed


def normalise(place_id, tokens, gain):
    total, width = tokens.shape
    own = total // 2
    blocks = own // Q
    return pl.pallas_call(
        norm_kernel,
        cost_estimate=takes(10),
        grid_spec=pltpu.PrefetchScalarGridSpec(
            num_scalar_prefetch=1,
            grid=(blocks + 1,),
            in_specs=[
                pl.BlockSpec((Q, width), lambda i, place: (i + place[0] * (blocks - 1), 0)),
                pl.BlockSpec((width, Q), lambda i, place: (0, 0)),
            ],
            out_specs=[
                pl.BlockSpec((width, Q), lambda i, place: (0, i)),
                pl.BlockSpec((width, Q), lambda i, place: (0, jnp.clip(i - place[0], 0, blocks - 1))),
            ],
        ),
        out_shape=[
            jax.ShapeDtypeStruct((width, own + HALO), BF16),
            jax.ShapeDtypeStruct((width, own), BF16),
        ],
        compiler_params=pltpu.CompilerParams(vmem_limit_bytes=VMEM),
    )(place_id, tokens, gain)


def cotangent_kernel(place_ref, mine_ref, other_ref, seg_ref, all_ref, turned_ref):
    first = place_ref[0] == 0
    mine, other = mine_ref[...].astype(F32), other_ref[...].astype(F32)
    whole = jnp.concatenate([jnp.where(first, mine, other), jnp.where(first, other, mine)], 1)
    all_ref[...] = whole.astype(BF16)
    turned_ref[...] = (whole.T * jnp.where(seg_ref[...] >= 0.0, 1.0, 0.0)).astype(BF16)


def cotangents(place_id, d_out, other, seg):
    own, half = other.shape
    blocks = own // Q
    return pl.pallas_call(
        cotangent_kernel,
        cost_estimate=takes(8),
        grid_spec=pltpu.PrefetchScalarGridSpec(
            num_scalar_prefetch=1,
            grid=(blocks,),
            in_specs=[
                pl.BlockSpec((Q, half), lambda i, place: (i + place[0] * blocks, 0)),
                pl.BlockSpec((Q, half), lambda i, place: (i, 0)),
                pl.BlockSpec((1, Q), lambda i, place: (0, i)),
            ],
            out_specs=[
                pl.BlockSpec((Q, 2 * half), lambda i, place: (i, 0)),
                pl.BlockSpec((2 * half, Q), lambda i, place: (0, i)),
            ],
        ),
        out_shape=[
            jax.ShapeDtypeStruct((own, 2 * half), BF16),
            jax.ShapeDtypeStruct((2 * half, own), BF16),
        ],
        compiler_params=pltpu.CompilerParams(vmem_limit_bytes=VMEM),
    )(place_id, d_out, other, seg)


def norm_back_kernel(place_ref, d_proj_ref, w_ref, d_z_ref, x_ref, cot_ref, gain_ref, *refs):
    out_ref, low_refs = refs[-3], refs[-2:]
    half = w_ref.shape[2]
    turned = dot(w_ref[0], d_proj_ref[:half, :], 1, 0) + dot(w_ref[1], d_proj_ref[half:, :], 1, 0)
    x = x_ref[...].astype(F32)
    inverse = lax.rsqrt(jnp.mean(x * x, axis=1, keepdims=True) + EPS)
    scaled = x * inverse
    d_scaled = (d_z_ref[...] + turned.T) * gain_ref[...]
    inner = jnp.mean(d_scaled * scaled, axis=1, keepdims=True)
    rows = cot_ref[...].astype(F32) + inverse * (d_scaled - scaled * inner)
    out_ref[...] = rows
    for k, low_ref in enumerate(low_refs):

        @pl.when(pl.program_id(0) == k)
        def _(low_ref=low_ref):
            low_ref[...] = rows.astype(BF16)


def norm_backward(place_id, d_proj, w, d_z, tokens, cotangent, gain, begin, whole=None):
    total, width = tokens.shape
    own = total // 2
    tile = own // 4
    here = pl.BlockSpec((tile, width), lambda i, place: (i + begin, 0))
    among = pl.BlockSpec((tile, width), lambda i, place: (i + begin + place[0] * 4, 0))
    more = [] if whole is None else [whole]
    return pl.pallas_call(
        norm_back_kernel,
        cost_estimate=takes(14),
        grid_spec=pltpu.PrefetchScalarGridSpec(
            num_scalar_prefetch=1,
            grid=(2,),
            in_specs=[
                pl.BlockSpec((d_proj.shape[0], tile), lambda i, place: (0, i + begin)),
                pl.BlockSpec(w.shape, lambda i, place: (0, 0, 0)),
                here,
                among,
                here,
                pl.BlockSpec((1, width), lambda i, place: (0, 0)),
            ]
            + [pl.BlockSpec(memory_space=pl.ANY)] * len(more),
            out_specs=[among] + [pl.BlockSpec((tile, width), lambda i, place: (0, 0))] * 2,
        ),
        out_shape=[jax.ShapeDtypeStruct((total, width), F32)] + [jax.ShapeDtypeStruct((tile, width), BF16)] * 2,
        input_output_aliases={7: 0} if more else {},
        compiler_params=pltpu.CompilerParams(vmem_limit_bytes=VMEM),
    )(place_id, d_proj, w, d_z, tokens, cotangent, gain, *more)


def fill_kernel(place_ref, *refs):
    out_ref = refs[-1]
    at = pl.program_id(0)
    for k, part in enumerate(refs[:-2]):

        @pl.when(at == k)
        def _(part=part):
            out_ref[...] = part[...].astype(F32)


def fill_rows(place_id, whole, parts):
    blocks = len(parts)
    rows, width = parts[0].shape
    return pl.pallas_call(
        fill_kernel,
        cost_estimate=takes(5),
        grid_spec=pltpu.PrefetchScalarGridSpec(
            num_scalar_prefetch=1,
            grid=(blocks,),
            in_specs=[pl.BlockSpec((rows, width), lambda i, place: (0, 0))] * blocks
            + [pl.BlockSpec(memory_space=pl.ANY)],
            out_specs=pl.BlockSpec((rows, width), lambda i, place: (i + (1 - place[0]) * blocks, 0)),
        ),
        out_shape=jax.ShapeDtypeStruct(whole.shape, F32),
        input_output_aliases={1 + blocks: 0},
        compiler_params=pltpu.CompilerParams(vmem_limit_bytes=VMEM),
    )(place_id, *parts, whole)


def finish_kernel(sizes, xbc_ref, z_ref, w_xbc_ref, w_dt_ref, w_z_ref, own_xbc_ref, own_dt_ref, own_z_ref, taps_ref, bias_ref, gain_ref, product_ref):
    conv = w_xbc_ref.shape[1]
    heads = w_dt_ref.shape[1]
    xbc, z = xbc_ref[:, :conv].astype(F32), z_ref[...].astype(F32)
    last = xbc_ref[:, conv:].astype(F32)
    dt = last[:, :heads]
    own_xbc_ref[...] = xbc
    own_dt_ref[...] = dt
    own_z_ref[...] = z
    taps, per = taps_ref.shape
    taps_ref[...] = last[:taps, heads : heads + per]
    bias_ref[...] = last[taps : taps + 1, heads : heads + per]
    gain_ref[...] = last[taps + 1 : taps + 2, heads : heads + gain_ref.shape[1]]
    product = jnp.sum(xbc * w_xbc_ref[...].astype(F32), axis=1, keepdims=True)
    product += jnp.sum(z * w_z_ref[...].astype(F32), axis=1, keepdims=True)
    product += jnp.sum(dt * w_dt_ref[...].astype(F32), axis=1, keepdims=True)
    product_ref[...] = jnp.broadcast_to(product, product_ref.shape)


def finish(sizes, own_xbc, own_z, w_xbc, w_dt, w_z):
    rows = w_z.shape[0]
    return pl.pallas_call(
        functools.partial(finish_kernel, sizes),
        cost_estimate=takes(3),
        out_shape=[
            jax.ShapeDtypeStruct(w_xbc.shape, F32),
            jax.ShapeDtypeStruct(w_dt.shape, F32),
            jax.ShapeDtypeStruct(w_z.shape, F32),
            jax.ShapeDtypeStruct((4, sizes[0]), F32),
            jax.ShapeDtypeStruct((1, sizes[0]), F32),
            jax.ShapeDtypeStruct((1, sizes[1]), F32),
            jax.ShapeDtypeStruct((rows, Q), F32),
        ],
        compiler_params=pltpu.CompilerParams(vmem_limit_bytes=VMEM),
    )(own_xbc, own_z, w_xbc, w_dt, w_z)


def spare_kernel(sizes, conv_ref, gain_ref, out_ref):
    per, gains, norms, heads, stride, skip = sizes
    count = out_ref.shape[1]
    lane = lax.broadcasted_iota(jnp.int32, (1, Q), 1)

    def turned(v):
        return jnp.concatenate([v, jnp.zeros((Q - v.shape[0], Q), F32)], 0).T

    def moved(row, size):
        return jnp.where((lane >= skip) & (lane < skip + size), pltpu.roll(row, skip, 1), 0.0)

    for y in range(2):
        for d in range(count):
            at = y * stride + d * per
            rows = [moved(turned(conv_ref[at : at + per, :])[k : k + 1], per) for k in range(5)]
            at = (y * count + d) * gains
            total = jnp.sum(turned(gain_ref[at : at + gains, :]), axis=0, keepdims=True)
            rows += [moved(total, gains), jnp.zeros((10, Q), F32)]
            out_ref[y, d] = jnp.concatenate(rows, 0)


def spare_block(sizes, count, conv_sums, gain_grad):
    return pl.pallas_call(
        functools.partial(spare_kernel, sizes),
        cost_estimate=takes(4),
        out_shape=jax.ShapeDtypeStruct((2, count, 16, Q), F32),
        compiler_params=pltpu.CompilerParams(vmem_limit_bytes=VMEM),
    )(conv_sums, gain_grad)


def grad_kernel(core_ref, left_ref, right_ref, *refs):
    spare_ref = refs[0] if len(refs) == 4 else None
    keep_ref, send_ref, scr = refs[-3:]
    parts, rows, tile = scr.shape
    scr[...] = dot(left_ref[...], right_ref[...], 1, 1).astype(BF16).reshape(scr.shape)
    if spare_ref is not None:

        @pl.when(pl.program_id(1) == pl.num_programs(1) - 1)
        def _():
            for p in range(parts):
                old = scr[p, :16, tile - Q :].astype(F32)
                scr[p, :16, tile - Q :] = (old + spare_ref[0, p]).astype(BF16)

    core = core_ref[0]
    for p in range(parts // 2):
        keep_ref[0, p] = scr[2 * p + core]
        send_ref[0, p] = scr[2 * p + 1 - core]


def grad_plain_kernel(left_ref, right_ref, out_ref):
    out_ref[...] = dot(left_ref[...], right_ref[...], 1, 1).astype(BF16).reshape(out_ref.shape)


def weight_grad_sum(left, right, count):
    width, rows = left.shape
    channels = right.shape[0] // 2
    tile = 256
    grad = pl.pallas_call(
        grad_plain_kernel,
        cost_estimate=takes(17),
        grid=(2, channels // tile),
        in_specs=[
            pl.BlockSpec((width, rows), lambda y, k: (0, 0)),
            pl.BlockSpec((tile, rows), lambda y, k: (y * (channels // tile) + k, 0)),
        ],
        out_specs=pl.BlockSpec((count, 1, width // count, tile), lambda y, k: (0, y, 0, k)),
        out_shape=jax.ShapeDtypeStruct((count, 2, width // count, channels), BF16),
        compiler_params=pltpu.CompilerParams(vmem_limit_bytes=VMEM),
    )(left, right)
    return grad, lax.psum_scatter(
        grad.reshape(-1, channels), ("dp", "mp"), scatter_dimension=0, tiled=True
    )


def weight_grad(left, right, count, tiles, spare=None):
    width, rows = left.shape
    tile = 256
    per_half = right.shape[0] // 2 // tile
    begin, end = tiles
    shape = (2, count // 2, width // count, (end - begin) * tile)
    block = pl.BlockSpec((1, count // 2, width // count, tile), lambda y, k: (y, 0, 0, k))
    core = (lax.axis_index("dp") % 2).reshape(1).astype(jnp.int32)
    more = [] if spare is None else [pl.BlockSpec((1,) + spare.shape[1:], lambda y, k: (y, 0, 0, 0))]
    return pl.pallas_call(
        grad_kernel,
        cost_estimate=takes(12),
        grid=(2, end - begin),
        in_specs=[
            pl.BlockSpec(memory_space=pltpu.SMEM),
            pl.BlockSpec((width, rows), lambda y, k: (0, 0)),
            pl.BlockSpec((tile, rows), lambda y, k: (y * per_half + begin + k, 0)),
        ]
        + more,
        out_specs=[block, block],
        out_shape=[jax.ShapeDtypeStruct(shape, BF16)] * 2,
        scratch_shapes=[pltpu.VMEM((count, width // count, tile), BF16)],
        compiler_params=pltpu.CompilerParams(vmem_limit_bytes=VMEM),
    )(core, left, right, *([] if spare is None else [spare]))


def rows_kernel(raw_ref, head_ref, mask_ref, *outs):
    cum_ref, shift_ref, into_ref, onto_ref, keep_ref, step_ref, slope_ref, ratio_ref, start_ref, end_ref = outs
    chunks = raw_ref.shape[1] // Q
    rate = -jnp.exp(head_ref[:, 0:1])
    bias = head_ref[:, 1:2]
    source = lax.broadcasted_iota(jnp.int32, (Q, Q), 0)
    target = lax.broadcasted_iota(jnp.int32, (Q, Q), 1)
    upto = (source <= target).astype(F32)
    totals, sums, log_steps, steps = [], [], [], []
    for c in range(chunks):
        span = slice(c * Q, (c + 1) * Q)
        v = raw_ref[:, span] + bias
        tail = jnp.log1p(jnp.exp(-jnp.abs(v)))
        step = jnp.maximum(v, 0.0) + tail
        low = v < -20.0
        log_step = jnp.where(low, v, jnp.log(jnp.where(low, 1.0, step)))
        slope = 1.0 / (1.0 + jnp.exp(-v))
        decay = step * rate * LOG2E
        cum = dot(decay, upto, 1, 0, lax.Precision.HIGHEST)
        total = cum[:, Q - 1 : Q]
        shift = cum - log_step * LOG2E
        cum_ref[:, span] = cum
        shift_ref[:, span] = shift
        step_ref[:, span] = step
        slope_ref[:, span] = slope
        ratio_ref[:, span] = jnp.where(low, 1.0, slope / jnp.where(low, 1.0, step))
        into_ref[:, span] = jnp.exp2(cum) * mask_ref[0:1, span]
        onto_ref[:, span] = jnp.exp2(total - cum) * step * mask_ref[1:2, span]
        keep_ref[:, span] = jnp.exp2(total) * mask_ref[2:3, span]
        totals.append(total)
        sums.append(cum)
        steps.append(step)
    before = jnp.zeros_like(totals[0])
    for c in range(chunks):
        span = slice(c * Q, (c + 1) * Q)
        start_ref[:, span] = jnp.exp2(before + sums[c]) * mask_ref[4:5, span]
        before = before + totals[c]
    after = jnp.zeros_like(totals[0])
    for c in reversed(range(chunks)):
        span = slice(c * Q, (c + 1) * Q)
        end_ref[:, span] = jnp.exp2(after + totals[c] - sums[c]) * steps[c] * mask_ref[3:4, span]
        after = after + totals[c]


def head_rows(raw, heads, masks):
    shape = jax.ShapeDtypeStruct(raw.shape, F32)
    return pl.pallas_call(
        rows_kernel,
        cost_estimate=takes(3),
        out_shape=[shape] * 10,
        compiler_params=pltpu.CompilerParams(vmem_limit_bytes=VMEM),
    )(raw, heads, masks)


def wide_columns(w_ref, rows):
    return [w_ref[rows, k * Q : (k + 1) * Q] for k in range(5)]


def conv_kernel(place_ref, proj_ref, w_ref, mask_ref, end_ref, out_ref, pre_ref, state_ref, b_scr, x_scr):
    s = pl.program_id(0)
    channels, own = out_ref.shape
    at = pl.multiple_of(place_ref[0] * HALO, HALO)
    size = 64

    def strip(i, carry):
        rows = pl.ds(pl.multiple_of(i * size, size), size)
        wide = wide_columns(w_ref, rows)
        before = proj_ref[rows, pl.ds(pl.multiple_of(jnp.maximum(at - Q, 0), Q), Q)].astype(F32)
        lane = lax.broadcasted_iota(jnp.int32, (size, Q), 1)
        last = [pltpu.roll(before, k, 1) for k in (1, 2, 3)]
        weight = end_ref[pl.ds(jnp.clip((s - 1) * 4 + i, 0, end_ref.shape[0] - 1), 1), :]
        for j in range(own // Q):
            now = proj_ref[rows, pl.ds(pl.multiple_of(at + j * Q, Q), Q)].astype(F32)
            span = slice(j * Q, (j + 1) * Q)
            pre = wide[4] + wide[3] * now
            for k in (1, 2, 3):
                rolled = pltpu.roll(now, k, 1)
                pre = pre + wide[3 - k] * (jnp.where(lane < k, last[k - 1], rolled) * mask_ref[k - 1 : k, span])
                last[k - 1] = rolled
            act = pre * sigmoid(pre)
            pre_ref[rows, span] = pre.astype(BF16)
            out_ref[rows, span] = act.astype(BF16)
            x_scr[rows, span] = (act * weight[:, span]).astype(BF16)
        return carry

    lax.fori_loop(0, channels // size, strip, 0)

    @pl.when(s == 0)
    def _():
        b_scr[...] = out_ref[:Q, :].astype(F32).T.astype(BF16)

    @pl.when((s > 0) & (s < pl.num_programs(0) - 1))
    def _():
        state_ref[...] = dot(x_scr[...], b_scr[...], 1, 0).astype(state_ref.dtype)


def conv_forward(place_id, proj, w_wide, masks, end_rows):
    channels, window = proj.shape
    own = window - HALO
    blocks = channels // 256
    half = blocks // 2

    def order(s):
        return jnp.where(s == 0, half - 1, jnp.where(s < half, s - 1, s))

    return pl.pallas_call(
        conv_kernel,
        cost_estimate=takes(25),
        grid=(blocks,),
        in_specs=[
            pl.BlockSpec(memory_space=pltpu.SMEM),
            pl.BlockSpec((256, window), lambda s: (order(s), 0)),
            pl.BlockSpec((256, 5 * Q), lambda s: (order(s), 0)),
            pl.BlockSpec(masks.shape, lambda s: (0, 0)),
            pl.BlockSpec(end_rows.shape, lambda s: (0, 0)),
        ],
        out_specs=[
            pl.BlockSpec((256, own), lambda s: (order(s), 0)),
            pl.BlockSpec((256, own), lambda s: (order(s), 0)),
            pl.BlockSpec((256, Q), lambda s: (jnp.clip(s - 1, 0, blocks - 3), 0)),
        ],
        out_shape=[
            jax.ShapeDtypeStruct((channels, own), BF16),
            jax.ShapeDtypeStruct((channels, own), BF16),
            jax.ShapeDtypeStruct(((blocks - 2) * 256, Q), BF16),
        ],
        scratch_shapes=[pltpu.VMEM((own, Q), BF16), pltpu.VMEM((256, own), BF16)],
        compiler_params=pltpu.CompilerParams(vmem_limit_bytes=VMEM),
    )(place_id, proj, w_wide, masks, end_rows)


def chunk_scores(conv_ref, bc, seg_ref):
    inner_half, stride = bc
    b_t = conv_ref[inner_half : inner_half + Q, :]
    c_t = conv_ref[stride + inner_half : stride + inner_half + Q, :]
    b_m = b_t.astype(F32).T.astype(BF16)
    scores = dot(b_m, c_t, 1, 0)
    source = lax.broadcasted_iota(jnp.int32, (Q, Q), 0)
    target = lax.broadcasted_iota(jnp.int32, (Q, Q), 1)
    seg = jnp.broadcast_to(seg_ref[...], (Q, Q))
    allowed = (source <= target) & (seg.T == seg)
    return b_t, c_t, b_m, jnp.where(allowed, scores, 0.0), allowed


def columns_of(shift_ref, col_scr):
    heads = shift_ref.shape[0]
    padded = jnp.concatenate([shift_ref[...], jnp.zeros((Q - heads, Q), F32)], 0).T
    for g in range(heads // 8):
        col_scr[g] = padded[:, g * 8 : (g + 1) * 8]


def scan_kernel(
    bc, skip_ref, conv_ref, z_ref, cum_ref, shift_ref, into_ref, onto_ref, keep_ref, seg_ref,
    gain_ref, first_ref, out_ref, ssd_ref, scale_ref, states_ref, state, gated, col_scr,
):
    inner_half, stride = bc
    groups = 2 * inner_half // 512

    @pl.when(pl.program_id(0) == 0)
    def _():
        state[...] = first_ref[...].astype(F32)

    _, c_t, b_m, scores, _ = chunk_scores(conv_ref, bc, seg_ref)
    columns_of(shift_ref, col_scr)

    def group(g, squares):
        at = pl.multiple_of(g * 512, 512)
        x_at = pl.multiple_of(g * 512 + jnp.where(g >= groups // 2, stride - inner_half, 0), 256)
        held = state[pl.ds(at, 512), :].astype(BF16)
        states_ref[0, pl.ds(at, 512), :] = held
        from_state = dot(held, c_t, 1, 0)
        cols = col_scr[g]
        parts = []
        for k in range(8):
            h = g * 8 + k
            x = conv_ref[pl.ds(x_at + k * 64, 64), :]
            spread = jnp.minimum(cum_ref[pl.ds(h, 1), :] - cols[:, k : k + 1], CAP)
            mixing = (jnp.exp2(spread) * scores).astype(BF16)
            xf = x.astype(F32)
            y = dot(x, mixing, 1, 0) + from_state[k * 64 : (k + 1) * 64] * into_ref[pl.ds(h, 1), :] + skip_ref[h] * xf
            z = z_ref[pl.ds(at + k * 64, 64), :].astype(F32)
            g_out = y * (z * sigmoid(z))
            squares = squares + g_out * g_out
            ssd_ref[pl.ds(at + k * 64, 64), :] = y.astype(BF16)
            gated[pl.ds(at + k * 64, 64), :] = g_out
            parts.append((xf * onto_ref[pl.ds(h, 1), :]).astype(BF16))
        fresh = dot(jnp.concatenate(parts, 0), b_m, 1, 0)
        for k in range(8):
            rows = pl.ds(at + k * 64, 64)
            state[rows, :] = state[rows, :] * keep_ref[pl.ds(g * 8 + k, 1), :] + fresh[k * 64 : (k + 1) * 64]
        return squares

    squares = lax.fori_loop(0, groups, group, jnp.zeros((64, Q), F32))
    scale = lax.rsqrt(jnp.sum(squares, axis=0, keepdims=True) / (2 * inner_half) + EPS)
    scale_ref[...] = scale

    def finish(g, carry):
        rows = pl.ds(pl.multiple_of(g * 512, 512), 512)
        out_ref[rows, :] = (gated[rows, :] * scale * gain_ref[rows, :]).astype(BF16)
        return carry

    lax.fori_loop(0, groups, finish, 0)


def scan_forward(bc, skip, conv, z, rows, seg, gain, first):
    inner = 2 * bc[0]
    channels, own = conv.shape
    chunks = own // Q
    heads = inner // 64
    row_spec = pl.BlockSpec((heads, Q), lambda c: (0, c))
    whole = pl.BlockSpec((inner, Q), lambda c: (0, 0))
    tile = pl.BlockSpec((inner, Q), lambda c: (0, c))
    cum, shift, into, onto, keep = rows[:5]
    return pl.pallas_call(
        functools.partial(scan_kernel, bc),
        cost_estimate=takes(29),
        grid=(chunks,),
        in_specs=[
            pl.BlockSpec(memory_space=pltpu.SMEM),
            pl.BlockSpec((channels, Q), lambda c: (0, c)),
            tile,
            row_spec, row_spec, row_spec, row_spec, row_spec,
            pl.BlockSpec((1, Q), lambda c: (0, c)),
            whole, whole,
        ],
        out_specs=[tile, tile, pl.BlockSpec((1, Q), lambda c: (0, c)), pl.BlockSpec((1, inner, Q), lambda c: (c, 0, 0))],
        out_shape=[
            jax.ShapeDtypeStruct((inner, own), BF16),
            jax.ShapeDtypeStruct((inner, own), BF16),
            jax.ShapeDtypeStruct((1, own), F32),
            jax.ShapeDtypeStruct((chunks, inner, Q), BF16),
        ],
        scratch_shapes=[pltpu.VMEM((inner, Q), F32), pltpu.VMEM((inner, Q), F32), pltpu.VMEM((heads // 8, Q, 8), F32)],
        compiler_params=pltpu.CompilerParams(vmem_limit_bytes=VMEM),
    )(skip, conv, z, cum, shift, into, onto, keep, seg, gain, first)


def gate_back_kernel(
    d_unit_ref, ssd_ref, z_ref, scale_ref, gain_ref, start_ref, c_ref, d_ssd_ref, d_gate_ref, gain_grad_ref, first_grad_ref, into, first_scr
):
    inner, width = ssd_ref.shape
    size = 64

    @pl.when(pl.program_id(0) == 0)
    def _():
        gain_grad_ref[...] = jnp.zeros_like(gain_grad_ref)
        first_scr[...] = jnp.zeros_like(first_scr)

    scale = scale_ref[...]

    def gain_of(rows):
        return jnp.concatenate([gain_ref[rows, :]] * (width // Q), 1)

    def look(g, cross):
        rows = pl.ds(pl.multiple_of(g * size, size), size)
        z = z_ref[rows, :].astype(F32)
        unit = ssd_ref[rows, :].astype(F32) * (z * sigmoid(z)) * scale
        product = d_unit_ref[rows, :].astype(F32) * unit
        gain_grad_ref[rows, :] += sum(product[:, k * Q : (k + 1) * Q] for k in range(width // Q))
        product = product * gain_of(rows)
        return cross + jnp.sum(product.reshape(size // 8, 8, width), axis=0)

    cross = lax.fori_loop(0, inner // size, look, jnp.zeros((8, width), F32))
    cross = jnp.sum(cross, axis=0, keepdims=True) / inner

    def head(h, carry):
        rows = pl.ds(pl.multiple_of(h * size, size), size)
        z = z_ref[rows, :].astype(F32)
        ssd = ssd_ref[rows, :].astype(F32)
        sig = sigmoid(z)
        act = z * sig
        unit = ssd * act * scale
        d_gated = scale * (d_unit_ref[rows, :].astype(F32) * gain_of(rows) - unit * cross)
        d_ssd = d_gated * act
        d_ssd_ref[rows, :] = d_ssd.astype(BF16)
        d_gate_ref[rows, :] = (d_gated * ssd * (sig + act * (1.0 - sig))).astype(BF16)
        into[rows, :] = (d_ssd * start_ref[pl.ds(h, 1), :]).astype(BF16)
        return carry

    lax.fori_loop(0, inner // size, head, 0)
    c_m = c_ref[...].astype(F32).T.astype(BF16)

    def sums(g, carry):
        rows = pl.ds(pl.multiple_of(g * 512, 512), 512)
        first_scr[rows, :] += dot(into[rows, :], c_m, 1, 0)
        return carry

    lax.fori_loop(0, inner // 512, sums, 0)

    @pl.when(pl.program_id(0) == pl.num_programs(0) - 1)
    def _():
        first_grad_ref[...] = first_scr[...].astype(BF16)


def gate_backward(bc, d_unit, ssd, z, scale, gain, start, conv):
    inner, own = ssd.shape
    heads = inner // 64
    width = 2 * Q
    tile = pl.BlockSpec((inner, width), lambda c: (0, c))
    whole = pl.BlockSpec((inner, Q), lambda c: (0, 0))
    c_block = (bc[0] + bc[1]) // Q
    return pl.pallas_call(
        gate_back_kernel,
        cost_estimate=takes(32),
        grid=(own // width,),
        in_specs=[
            tile, tile, tile,
            pl.BlockSpec((1, width), lambda c: (0, c)),
            whole,
            pl.BlockSpec((heads, width), lambda c: (0, c)),
            pl.BlockSpec((Q, width), lambda c: (c_block, c)),
        ],
        out_specs=[tile, tile, whole, whole],
        out_shape=[
            jax.ShapeDtypeStruct((inner, own), BF16),
            jax.ShapeDtypeStruct((inner, own), BF16),
            jax.ShapeDtypeStruct((inner, Q), F32),
            jax.ShapeDtypeStruct((inner, Q), BF16),
        ],
        scratch_shapes=[pltpu.VMEM((inner, width), BF16), pltpu.VMEM((inner, Q), F32)],
        compiler_params=pltpu.CompilerParams(vmem_limit_bytes=VMEM),
    )(d_unit, ssd, z, scale, gain, start, conv)


def scan_back_kernel(
    bc, skip_ref, conv_ref, d_ssd_ref, states_ref, last_ref, cum_ref, shift_ref, into_ref, onto_ref, keep_ref,
    step_ref, slope_ref, ratio_ref, seg_ref, head_ref,
    d_conv_ref, d_raw_ref, bias_grad_ref, rate_grad_ref, skip_grad_ref,
    grad, col_scr, row_scr, diag_scr, state_scr, hold_scr, y_scr, x_scr, dst_scr, dc_scr, db_scr,
):
    inner_half, stride = bc
    groups = 2 * inner_half // 512
    heads = 2 * inner_half // 64

    @pl.when(pl.program_id(0) == 0)
    def _():
        grad[...] = last_ref[...].astype(F32)
        bias_grad_ref[...] = jnp.zeros_like(bias_grad_ref)
        rate_grad_ref[...] = jnp.zeros_like(rate_grad_ref)
        skip_grad_ref[...] = jnp.zeros_like(skip_grad_ref)

    b_t, c_t, b_m, scores, allowed = chunk_scores(conv_ref, bc, seg_ref)
    c_m = c_t.astype(F32).T.astype(BF16)
    columns_of(shift_ref, col_scr)
    dst_scr[...] = jnp.zeros_like(dst_scr)
    dc_scr[...] = jnp.zeros_like(dc_scr)
    db_scr[...] = jnp.zeros_like(db_scr)

    def group(g, carry):
        at = pl.multiple_of(g * 512, 512)
        x_at = pl.multiple_of(g * 512 + jnp.where(g >= groups // 2, stride - inner_half, 0), 256)
        held = states_ref[0, pl.ds(at, 512), :]
        g_low = grad[pl.ds(at, 512), :].astype(BF16)
        from_state = dot(held, c_t, 1, 0)
        onto_state = dot(g_low, b_t, 1, 0)
        cols = col_scr[g]
        d_scores = jnp.zeros((Q, Q), F32)
        for k in range(8):
            h = g * 8 + k
            row = pl.ds(h, 1)
            span = slice(k * 64, (k + 1) * 64)
            x = conv_ref[pl.ds(x_at + k * 64, 64), :]
            dy = d_ssd_ref[pl.ds(at + k * 64, 64), :]
            xf, dyf = x.astype(F32), dy.astype(F32)
            decays = jnp.exp2(jnp.minimum(cum_ref[row, :] - cols[:, k : k + 1], CAP))
            mixing = (decays * scores).astype(BF16)
            d_scores = d_scores + decays * dot(x, dy, 0, 0)
            y = dot(x, mixing, 1, 0) + from_state[span] * into_ref[row, :]
            dx = dot(dy, mixing, 1, 1)
            dx_state = onto_state[span] * onto_ref[row, :]
            row_scr[row, :] = jnp.sum(dyf * y, axis=0, keepdims=True)
            diag_scr[row, :] = jnp.sum(xf * dx, axis=0, keepdims=True)
            state_scr[row, :] = jnp.sum(xf * dx_state, axis=0, keepdims=True)
            skip_grad_ref[row, :] += jnp.sum(xf * dyf, axis=0, keepdims=True)
            hold_scr[row, :] = jnp.sum(grad[pl.ds(at + k * 64, 64), :] * held[span].astype(F32), axis=0, keepdims=True)
            d_conv_ref[pl.ds(x_at + k * 64, 64), :] = (dx + dx_state + skip_ref[h] * dyf).astype(BF16)
            y_scr[span, :] = (dyf * into_ref[row, :]).astype(BF16)
            x_scr[span, :] = (xf * onto_ref[row, :]).astype(BF16)
        dst_scr[...] += d_scores
        fresh = dot(y_scr[...], c_m, 1, 0)
        dc_scr[...] += dot(held, y_scr[...], 0, 0)
        db_scr[...] += dot(g_low, x_scr[...], 0, 0)
        for k in range(8):
            rows = pl.ds(at + k * 64, 64)
            grad[rows, :] = grad[rows, :] * keep_ref[pl.ds(g * 8 + k, 1), :] + fresh[k * 64 : (k + 1) * 64]
        return carry

    lax.fori_loop(0, groups, group, 0)
    d_scores = jnp.where(allowed, dst_scr[...], 0.0).astype(BF16)
    zeros = jnp.zeros((stride - inner_half - Q, Q), BF16)
    d_conv_ref[inner_half : inner_half + Q, :] = (db_scr[...] + dot(c_t, d_scores, 1, 1)).astype(BF16)
    d_conv_ref[inner_half + Q : stride, :] = zeros
    d_conv_ref[stride + inner_half : stride + inner_half + Q, :] = (dc_scr[...] + dot(b_t, d_scores, 1, 0)).astype(BF16)
    d_conv_ref[stride + inner_half + Q :, :] = zeros

    source = lax.broadcasted_iota(jnp.int32, (Q, Q), 0)
    target = lax.broadcasted_iota(jnp.int32, (Q, Q), 1)
    since = (source >= target).astype(F32)
    columns = diag_scr[...] + state_scr[...]
    d_decay = dot(row_scr[...] - columns, since, 1, 0, lax.Precision.HIGHEST)
    d_decay = d_decay + jnp.sum(state_scr[...] + hold_scr[...] * keep_ref[...], axis=1, keepdims=True)
    rate = -jnp.exp(head_ref[:, 0:1])
    slope = slope_ref[...]
    d_raw = columns * ratio_ref[...] + rate * d_decay * slope
    bias_grad_ref[...] += d_raw
    rate_grad_ref[...] += step_ref[...] * d_decay * rate
    d_raw_ref[...] = jnp.zeros_like(d_raw_ref)
    d_raw_ref[0 : heads // 2, :] = d_raw[: heads // 2].astype(BF16)
    d_raw_ref[Q : Q + heads // 2, :] = d_raw[heads // 2 :].astype(BF16)


def scan_backward(bc, skip, conv, d_ssd, states, last, rows, seg, head_cols):
    inner = 2 * bc[0]
    channels, own = conv.shape
    chunks = own // Q
    heads = inner // 64
    end = chunks - 1
    row_spec = pl.BlockSpec((heads, Q), lambda c: (0, end - c))
    whole = pl.BlockSpec((inner, Q), lambda c: (0, 0))
    sums = pl.BlockSpec((heads, Q), lambda c: (0, 0))
    cum, shift, into, onto, keep, step, slope, ratio = rows[:8]
    small = jax.ShapeDtypeStruct((heads, Q), F32)
    row_buf = pltpu.VMEM((heads, Q), F32)
    square = pltpu.VMEM((Q, Q), F32)
    return pl.pallas_call(
        functools.partial(scan_back_kernel, bc),
        cost_estimate=takes(44),
        grid=(chunks,),
        in_specs=[
            pl.BlockSpec(memory_space=pltpu.SMEM),
            pl.BlockSpec((channels, Q), lambda c: (0, end - c)),
            pl.BlockSpec((inner, Q), lambda c: (0, end - c)),
            pl.BlockSpec((1, inner, Q), lambda c: (end - c, 0, 0)),
            whole,
        ]
        + [row_spec] * 8
        + [
            pl.BlockSpec((1, Q), lambda c: (0, end - c)),
            pl.BlockSpec(head_cols.shape, lambda c: (0, 0)),
        ],
        out_specs=[
            pl.BlockSpec((channels, Q), lambda c: (0, end - c)),
            pl.BlockSpec((2 * Q, Q), lambda c: (0, end - c)),
            sums, sums, sums,
        ],
        out_shape=[
            jax.ShapeDtypeStruct((channels, own), BF16),
            jax.ShapeDtypeStruct((2 * Q, own), BF16),
            small, small, small,
        ],
        scratch_shapes=[
            pltpu.VMEM((inner, Q), F32), pltpu.VMEM((heads // 8, Q, 8), F32),
            row_buf, row_buf, row_buf, row_buf,
            pltpu.VMEM((512, Q), BF16), pltpu.VMEM((512, Q), BF16),
            square, square, square,
        ],
        compiler_params=pltpu.CompilerParams(vmem_limit_bytes=VMEM),
    )(skip, conv, d_ssd, states, last, cum, shift, into, onto, keep, step, slope, ratio, seg, head_cols)


def conv_back_kernel(half, place_ref, proj_ref, pre_ref, d_ref, beyond_ref, raw_ref, w_ref, mask_ref, out_ref, sums_ref, acc):
    s = pl.program_id(0)
    channels, own = out_ref.shape
    tiles = own // Q
    at = pl.multiple_of(place_ref[0] * HALO, HALO)
    size = 32

    def strip(i, carry):
        rows = pl.ds(pl.multiple_of(i * size, size), size)
        wide = wide_columns(w_ref, rows)
        lane = lax.broadcasted_iota(jnp.int32, (size, Q), 1)
        sums = [jnp.zeros((size, Q), F32)] * 5
        kept, moved = None, None
        for j in range(tiles + 1):
            span = slice(j * Q, (j + 1) * Q)
            if j < tiles:
                pre = pre_ref[rows, span].astype(F32)
                sig = sigmoid(pre)
                d_pre = d_ref[rows, span].astype(F32) * (sig + pre * sig * (1.0 - sig))
            else:
                d_pre = beyond_ref[rows, :].astype(F32)
            back = [pltpu.roll(d_pre * mask_ref[k - 1 : k, span], Q - k, 1) for k in (1, 2, 3)]
            if j > 0:
                now = proj_ref[rows, pl.ds(pl.multiple_of(at + (j - 1) * Q, Q), Q)].astype(F32)
                shifted = [kept] + [jnp.where(lane < Q - k, moved[k - 1], back[k - 1]) for k in (1, 2, 3)]
                d_proj = wide[3] * kept
                for k in (1, 2, 3):
                    d_proj = d_proj + wide[3 - k] * shifted[k]
                for k in range(4):
                    sums[3 - k] = sums[3 - k] + now * shifted[k]
                out_ref[rows, (j - 1) * Q : j * Q] = d_proj.astype(BF16)
            if j < tiles:
                sums[4] = sums[4] + d_pre
            kept, moved = d_pre, back
        for k in range(5):
            acc[rows, k * Q : (k + 1) * Q] = sums[k]
        return carry

    lax.fori_loop(0, channels // size, strip, 0)
    rows_of = lax.broadcasted_iota(jnp.int32, (5 * Q, Q), 0) // Q
    column = lax.broadcasted_iota(jnp.int32, (5 * Q, Q), 1)
    ones = jnp.where(rows_of == column, 1.0, 0.0).astype(BF16)
    high = acc[...].astype(BF16)
    low = (acc[...] - high.astype(F32)).astype(BF16)
    sums_ref[...] = dot(high, ones, 1, 0) + dot(low, ones, 1, 0)

    @pl.when(lax.rem(s, half) == half - 1)
    def _():
        out_ref[Q:, :] = raw_ref[...]


def conv_backward(place_id, proj, pre, d_conv, beyond, d_raw, w_wide, masks):
    channels, window = proj.shape
    own = window - HALO
    blocks = channels // 256
    half = blocks // 2
    return pl.pallas_call(
        functools.partial(conv_back_kernel, half),
        cost_estimate=takes(31),
        grid=(blocks,),
        in_specs=[
            pl.BlockSpec(memory_space=pltpu.SMEM),
            pl.BlockSpec((256, window), lambda s: (s, 0)),
            pl.BlockSpec((256, own), lambda s: (s, 0)),
            pl.BlockSpec((256, own), lambda s: (s, 0)),
            pl.BlockSpec((256, HALO), lambda s: (s, 0)),
            pl.BlockSpec((Q, own), lambda s: (s // half, 0)),
            pl.BlockSpec((256, 5 * Q), lambda s: (s, 0)),
            pl.BlockSpec(masks.shape, lambda s: (0, 0)),
        ],
        out_specs=[pl.BlockSpec((256, own), lambda s: (s, 0)), pl.BlockSpec((256, Q), lambda s: (s, 0))],
        out_shape=[jax.ShapeDtypeStruct((channels, own), BF16), jax.ShapeDtypeStruct((channels, Q), F32)],
        scratch_shapes=[pltpu.VMEM((256, 5 * Q), F32)],
        compiler_params=pltpu.CompilerParams(vmem_limit_bytes=VMEM),
    )(place_id, proj, pre, d_conv, beyond, d_raw, w_wide, masks)


def shards(
    tokens, token_seq, w_z, w_xbc, w_dt, w_out, conv_w, conv_b, gate_gain, norm_gain, a_log, d_skip, dt_bias, d_out, *, count
):
    my = lax.axis_index("mp")
    all_rows, width = tokens.shape
    own = all_rows // 2
    window = own + HALO
    inner_half = w_z.shape[1]
    inner = 2 * inner_half
    conv_half = w_xbc.shape[1]
    state_dim = conv_half - inner_half
    heads_half = w_dt.shape[1]
    stride = -(-(conv_half + heads_half) // 256) * 256
    bc = (inner_half, stride)
    place_id = my.reshape(1).astype(jnp.int32)

    per, taps = conv_w.shape[1], conv_w.shape[0]
    shard_rows = w_dt.shape[0]
    spare = stride - conv_half - heads_half
    head_params = jnp.concatenate([a_log, dt_bias, d_skip])
    high = head_params.astype(BF16)
    middle = (head_params - high.astype(F32)).astype(BF16)
    low = (head_params - high.astype(F32) - middle.astype(F32)).astype(BF16)
    vectors = [*conv_w, conv_b, gate_gain, norm_gain, high, middle, low]
    small = jnp.stack([jnp.pad(v, (0, Q - v.shape[0])) for v in vectors])
    small = jnp.pad(small, ((0, 16 - len(vectors)), (0, 0)))
    shard_xbc = jnp.concatenate([w_xbc, w_dt, jnp.zeros((shard_rows, spare), BF16)], 1)
    sizes = (per, gate_gain.shape[0], norm_gain.shape[0], heads_half, stride)
    spare_sizes = (*sizes, Q - spare)
    conv_masks, scan_masks, seg_row = row_masks(place_id, token_seq)

    shard_out = w_out.T
    swapped = [swap(w_z), swap(shard_out)]
    if count == 16:
        full_xbc, prepared, normed_rows, swapped, marks = gather_now(
            shard_xbc,
            small,
            lambda got: parameters(got, sizes, True),
            lambda got: normalise(place_id, tokens, got[3]),
            swapped,
        )
    else:
        marks = ()
        full_xbc = gather_later(shard_xbc, swap(shard_xbc), marks)
        small = lax.all_gather(lax.all_gather(small, "dp", axis=0, tiled=False), "mp", axis=0, tiled=False)
        prepared = parameters(small.reshape(2 * count, 16, Q), sizes, False)
        normed_rows = normalise(place_id, tokens, prepared[3])
    full_z = gather_later(w_z, swapped[0], marks)
    full_out = gather_later(shard_out, swapped[1], marks)
    w_wide, gain_wide, gain_in, gain_tall, head_cols = prepared
    window_t, normed_t = normed_rows
    skip_all = head_cols[:, 2]
    full_xbc = full_xbc.reshape(2, width, stride)

    proj = jnp.einsum("ydc,dt->yct", full_xbc, window_t, preferred_element_type=F32).astype(BF16)
    proj = proj.reshape(2 * stride, window)
    full_dt = full_xbc[:, :, conv_half : conv_half + heads_half]
    dt_raw = jnp.einsum("ydh,dt->yht", full_dt, normed_t, preferred_element_type=F32).reshape(2 * heads_half, own)
    rows = head_rows(dt_raw, head_cols, scan_masks)
    start_rows, end_rows = rows[8], rows[9]
    conved, pre, end_state = conv_forward(place_id, proj, w_wide, conv_masks, end_rows)
    state_flow = once(end_state, lambda a: lax.ppermute(a, "mp", [(0, 1)]))
    z = jnp.einsum("ydk,dt->ykt", full_z, ahead(normed_t, state_flow), preferred_element_type=F32).astype(BF16).reshape(inner, own)
    z = after(z, state_flow)
    d_flow = once(lax.dynamic_slice_in_dim(tie(d_out, proj)[0], (1 - my) * own, own, 0), swap)
    z = ahead(z, d_flow)
    out_normed, ssd, scale, states = scan_forward(
        bc, skip_all, conved, z, rows, seg_row, gain_wide, state_flow.result
    )
    out_normed = after(out_normed, d_flow)
    cotangent, cot_t = cotangents(place_id, d_out, d_flow.result, seg_row)
    grad_out, own_out = weight_grad_sum(cot_t, out_normed, count)
    out_ready = tie(out_normed, grad_out)[0]
    branch = jnp.einsum(
        "ykt,ydk->td", out_ready.reshape(2, inner_half, own), full_out, preferred_element_type=F32
    )
    first_half = my == 0
    live_rows = (lax.dynamic_slice_in_dim(token_seq, my * own, own, 0) >= 0)[:, None]
    tokens_own = lax.dynamic_slice_in_dim(tokens, my * own, own, 0).astype(F32)
    layer_rows = (tokens_own + jnp.where(live_rows, branch, 0.0)).astype(BF16)
    half_width = width // 2
    layer_mine = lax.dynamic_slice_in_dim(layer_rows, my * half_width, half_width, 1)
    layer_flow = once(lax.dynamic_slice_in_dim(layer_rows, (1 - my) * half_width, half_width, 1), swap)

    d_unit = jnp.einsum("ydk,dt->ykt", full_out, ahead(cot_t, layer_flow), preferred_element_type=F32).astype(BF16).reshape(inner, own)
    d_ssd, d_gate, gain_grad, first_grad = gate_backward(bc, d_unit, ssd, z, scale, gain_wide, start_rows, conved)
    d_gate = after(d_gate, layer_flow)
    grad_flow = once(first_grad, lambda a: lax.ppermute(a, "mp", [(1, 0)]))
    ready = ahead(d_gate, grad_flow)
    d_normed_z = jnp.einsum("ykt,ydk->td", ready.reshape(2, inner_half, own), full_z, preferred_element_type=F32)
    first_pre = ahead(pre, grad_flow)[:, :HALO].astype(F32)
    first_sig = sigmoid(first_pre)
    first_slope = first_sig + first_pre * first_sig * (1.0 - first_sig)
    d_normed_z = after(d_normed_z, grad_flow, also=(first_slope,))
    grad_z, own_z = weight_grad_sum(normed_t, tie(d_gate, d_normed_z)[0], count)
    d_conv, d_raw, bias_grad, rate_grad, skip_grad = scan_backward(
        bc, skip_all, conved, tie(d_ssd, grad_z)[0], states, grad_flow.result, rows, seg_row, head_cols
    )
    head_grads = jnp.stack([jnp.sum(v, 1) for v in (rate_grad, skip_grad, bias_grad)])
    head_grads = jnp.pad(head_grads.reshape(1, -1), ((0, 7), (0, -head_grads.size % Q)))
    heads_flow = total(head_grads, count)
    d_first = d_conv[:, :HALO].astype(F32) * first_slope
    d_first = d_first[:, :16].astype(BF16).T
    beyond_flow = once(d_first, lambda a: lax.ppermute(a, "mp", [(1, 0)]))
    layer_recv = ahead(layer_flow.result, beyond_flow)
    layer_out = jnp.where(
        first_half, jnp.concatenate([layer_mine, layer_recv], 0), jnp.concatenate([layer_recv, layer_mine], 0)
    )
    layer_out = after(layer_out, beyond_flow)
    beyond = jnp.pad(beyond_flow.result.T, ((0, 0), (0, HALO - 16)))
    d_conv = tie(d_conv, own_out, layer_out)[0]
    d_proj, conv_sums = conv_backward(
        place_id, proj, pre, d_conv, beyond, d_raw, w_wide, conv_masks
    )
    tiles = stride // 256
    keep_b, sent_b = weight_grad(normed_t, d_proj, count, (0, tiles - 4))
    flow_b = sum_to_owners(keep_b, sent_b, count, "zxy")
    small = spare_block(spare_sizes, count, tie(conv_sums, keep_b)[0], gain_grad)
    keep_a, sent_a = weight_grad(ahead(normed_t, flow_b), d_proj, count, (tiles - 4, tiles), small)
    keep_a = after(keep_a, flow_b, heads_flow)
    flow_a = sum_to_owners(keep_a, sent_a, count, "xzy")
    full_back = ahead(full_xbc, flow_a, flow_b)
    back = (d_normed_z, tokens, cotangent, gain_in)
    d_tokens, part_0, part_1 = norm_backward(place_id, d_proj, full_back, *back, 0)
    part_0 = after(part_0, flow_a, flow_b, heads_flow)
    low_flows = [once(part_0, swap), once(tie(part_1, part_0)[0], swap)]
    full_back = ahead(full_xbc, flow_a, flow_b, *low_flows)
    d_tokens, part_2, part_3 = norm_backward(place_id, d_proj, full_back, *back, 2, d_tokens)
    part_2 = after(part_2, flow_a, flow_b, *low_flows, also=(own_z,))
    low_flows += [once(part_2, swap), once(tie(part_3, part_2)[0], swap)]
    mark = after(tie(norm_gain, part_2)[0], flow_a, flow_b, heads_flow, low_flows[2])
    mark = after(mark, flow_a, flow_b, heads_flow, low_flows[3])
    d_tokens = fill_rows(place_id, d_tokens, [f.finish() for f in low_flows])
    mark = after(mark, flow_a, flow_b, heads_flow)
    mark = after(mark, flow_a, flow_b, heads_flow, also=(d_tokens,))
    own_xbc = jnp.concatenate([flow_b.finish(), flow_a.finish()], 1)
    head_grads = heads_flow.finish().reshape(-1)[: 6 * heads_half]

    own_xbc, own_dt, own_z, own_taps, own_bias, own_gain, product = finish(sizes, own_xbc, own_z, w_xbc, w_dt, w_z)
    own_out = own_out.astype(F32).T
    norms = norm_gain.shape[0]
    product = lax.dynamic_slice_in_dim(product[:, 0] + swap(product)[:, 0], my * norms, norms, 0)
    norm_mine = product / norm_gain.astype(F32)
    heads_mine = pick(head_grads.reshape(3, 2, heads_half), my, 1)
    return (
        layer_out,
        d_tokens,
        own_z,
        own_xbc,
        own_dt,
        own_out,
        own_taps,
        own_bias[0],
        own_gain[0],
        norm_mine,
        heads_mine[0],
        heads_mine[1],
        heads_mine[2],
    )


def solution(mesh):
    placed = (
        P("dp", None),
        P("dp"),
        P("dp", "mp"),
        P("dp", "mp"),
        P("dp", "mp"),
        P("mp", "dp"),
        P(None, ("mp", "dp")),
        P(("mp", "dp")),
        P(("mp", "dp")),
        P(("dp", "mp")),
        P("mp"),
        P("mp"),
        P("mp"),
        P("dp", "mp"),
    )
    return jax.shard_map(
        functools.partial(shards, count=mesh.shape["dp"]),
        mesh=mesh,
        in_specs=placed,
        out_specs=(
            P("dp", "mp"),
            P("dp", None),
            P("dp", "mp"),
            P("dp", "mp"),
            P("dp", "mp"),
            P("mp", "dp"),
            P(None, ("mp", "dp")),
            P(("mp", "dp")),
            P(("mp", "dp")),
            P(("dp", "mp")),
            P("mp"),
            P("mp"),
            P("mp"),
        ),
        check_vma=False,
    )
```
